32 devices in a mesh: grp: 2 (over y), gx: 8 (over z, x), gy: 2 (over core).
Axes of the slice: x: 2, y: 2, z: 4, core: 2. Of those that a mesh axis runs over, the one named last changes fastest.
Arguments:
- source_matrix: float32 [64, 128, 1024], P('grp', 'gx', 'gy'), parts along dimension 0, may hold values from -6 to 6
- source_fracture: float32 [64, 4096], P(('grp', 'gy'), 'gx'), parts along dimension 0, may hold values from -6 to 6
- aperture: float32 [64, 4096], P(('grp', 'gy'), 'gx'), parts along dimension 0, may hold values from 0.5 to 2
- storage: float32 [128, 1024], P('gx', 'gy'), may hold values from 0.1 to 1
- perm_class: int32 [128, 1024], P('gx', 'gy'), may hold values from 0 to 7
- class_perm: float32 [8], replicated, may hold values from 0.1 to 10
- send_slots: int32 [8, 128], P('gx'), may hold values from 0 to 511
- isect_local: int32 [32, 128], P('gx'), may hold values from 0 to 511
- isect_other: int32 [32, 128], P('gx'), may hold values from 0 to 639, as said below
- isect_count: int32 [32], P('gx'), may hold values from 0 to 128, as said below
- ov_cell: int32 [8, 2, 2, 128], P('gx', 'gy'), may hold values from 0 to 8191
- ov_frac: int32 [8, 2, 2, 128], P('gx', 'gy'), may hold values from 0 to 511
- ov_weight: float32 [8, 2, 2, 128], P('gx', 'gy'), may hold values from 0.2 to 2
- ov_count: int32 [8, 2, 2], P('gx', 'gy'), may hold values from 0 to 128, as said below
Outputs:
- pressure_matrix: float32 [64, 128, 1024], P('grp', 'gx', 'gy'), parts along dimension 0
- pressure_fracture: float32 [64, 4096], P(('grp', 'gy'), 'gx'), parts along dimension 0
The draws below stay inside these ranges and needn't reach their ends.
There are 2 independent parts, one for each index of `grp`. The reference program is written for one: setup_inputs(seed, part) draws one part's arguments, and reference() takes and returns one part's arrays. A program takes and returns all parts, laid end to end along the dimension named above; an argument that names none is the same for every part. Nothing has to cross between parts.
Inputs may be any that keep to these rules, and one draw needn't show every extreme that they name: `isect_count`: live rows come first in a partition's intersection blocks and fill the blocks in order; some partition fills all its blocks and some partition has no live rows. `isect_other`: most intersection rows are local; the others name ghost slots of all four neighbour groups. `ov_count`: live rows come first in a device's margin blocks and fill the blocks in order; some device fills all its blocks and some device has no live rows.
All inputs are finite; a program needn't handle non-finite values.
Results may differ from the reference program's by a relative error of at most 0.0003.
Values sent between devices are 32-bit elements; how exact they have to be, the bound alone decides.
No kernel may reach another device: no remote copies, remote signals or barrier semaphores. Data moves between devices by JAX's collectives and lax.ppermute only.
A program may use at most 64 MiB of HBM per device.

```python
import math
import jax
import jax.numpy as jnp

MEMB = 32
CX = 16
CY = 512
FR_DEV = 512
GHOST = 32
IBLK = 4
OBLK = 2
NCLASS = 8
ITERS = 3
NX = 128
NY = 1024
NF = 4096
N_GX = 8
N_GY = 2


def spread_counts(key, devices, blocks):
    first_key, second_key = jax.random.split(key)
    totals = jax.random.randint(first_key, (devices,), 0, blocks * 128 + 1)
    chosen = jax.random.randint(second_key, (), 0, devices)
    device_ids = jnp.arange(devices)
    totals = jnp.where(device_ids == chosen, blocks * 128, totals)
    totals = jnp.where(device_ids == (chosen + 1) % devices, 0, totals)
    counts = totals[:, None] - jnp.arange(blocks)[None, :] * 128
    return jnp.clip(counts, 0, 128).astype(jnp.int32)


def draw_isect_count(key, part):
    key = jax.random.fold_in(key, 11)
    return spread_counts(key, N_GX, IBLK).reshape(N_GX * IBLK)


def draw_ov_count(key, part):
    key = jax.random.fold_in(key, 23)
    return spread_counts(key, N_GX * N_GY, OBLK).reshape(N_GX, N_GY, OBLK)


def draw_isect_other(key, part):
    key = jax.random.fold_in(key, 31)
    local_key, ghost_key, pick_key = jax.random.split(key, 3)
    shape = (N_GX * IBLK, 128)
    local_cells = jax.random.randint(local_key, shape, 0, FR_DEV)
    ghost_cells = jax.random.randint(ghost_key, shape, FR_DEV, FR_DEV + 4 * GHOST)
    picked = jax.random.randint(pick_key, shape, 0, 4) == 0
    values = jnp.where(picked, ghost_cells, local_cells)
    values = values.at[0, 0].set(FR_DEV + 4 * GHOST - 1)
    return values.astype(jnp.int32)


def touch_ends(values, key, least, largest):
    index_at = [jax.random.randint(jax.random.fold_in(key, axis), (), 0, length) for axis, length in enumerate(values.shape)]
    main_axis = values.shape.index(max(values.shape))
    beside = index_at[:main_axis] + [(index_at[main_axis] + 1) % values.shape[main_axis]] + index_at[main_axis + 1:]
    return values.at[tuple(index_at)].set(least).at[tuple(beside)].set(largest)


def block_scale(own_key, dims, cuts, least, top_value):
    def one(axis_at, blocks):
        steps = jax.random.uniform(jax.random.fold_in(jax.random.fold_in(own_key, 6), axis_at), (blocks,), jnp.float32, least / len(cuts), top_value / len(cuts))
        return jnp.repeat(jnp.exp(steps), dims[axis_at] // blocks).reshape((-1,) + (1,) * (len(dims) - axis_at - 1))

    loudness = one(*cuts[0])
    for cut in cuts[1:]:
        loudness = loudness * one(*cut)
    return loudness


def normal_values(own_key, shape, scale, bound, pieces=(), held_as=jnp.bfloat16):
    result = jax.random.normal(own_key, shape, jnp.float32) * scale
    if len(pieces) > 0:
        result = block_scale(own_key, shape, pieces, -0.22, 0.18) * result
    return jnp.clip(result, min=-bound, max=bound).astype(held_as)


def setup_inputs(seed: int = 0, part: int = 0) -> dict:
    streams_of = jax.random.split(jax.random.key(seed), 15)
    part_keys = jax.random.split(jax.random.fold_in(streams_of[14], part), 15)
    return {
        "source_matrix": normal_values(part_keys[0], (MEMB, NX, NY), 1.0, 6.0, ((1, 8), (2, 2)), jnp.float32),
        "source_fracture": normal_values(part_keys[1], (MEMB, NF), 1.0, 6.0, ((0, 2), (1, 8)), jnp.float32),
        "aperture": jnp.clip(jnp.exp(math.log(2.0) - 1.3862944 * jax.random.uniform(part_keys[2], (MEMB, NF), jnp.float32) ** block_scale(part_keys[2], (MEMB, NF), ((0, 2), (1, 8)), -0.2, 0.2)), 0.5, 2.0),
        "storage": jnp.clip(0.1 + 0.9 * jax.random.uniform(streams_of[3], (NX, NY), jnp.float32) ** block_scale(streams_of[3], (NX, NY), ((0, 8), (1, 2)), -0.2, 0.2), 0.1, 1.0),
        "perm_class": touch_ends(jax.random.randint(streams_of[4], (NX, NY), 0, NCLASS), jax.random.fold_in(streams_of[4], 1), 0, NCLASS - 1).astype(jnp.int32),
        "class_perm": jnp.clip(jnp.exp(jax.random.uniform(streams_of[5], (NCLASS,), jnp.float32, math.log(0.1), math.log(10.0))), 0.1, 10.0),
        "send_slots": touch_ends(jax.random.randint(streams_of[6], (N_GX, 4 * GHOST), 0, FR_DEV), jax.random.fold_in(streams_of[6], 1), 0, FR_DEV - 1).astype(jnp.int32),
        "isect_local": touch_ends(jax.random.randint(streams_of[7], (N_GX * IBLK, 128), 0, FR_DEV), jax.random.fold_in(streams_of[7], 1), 0, FR_DEV - 1).astype(jnp.int32),
        "isect_other": draw_isect_other(jax.random.fold_in(streams_of[14], 71), part),
        "isect_count": draw_isect_count(jax.random.fold_in(streams_of[14], 71), part),
        "ov_cell": touch_ends(jax.random.randint(streams_of[10], (N_GX, N_GY, OBLK, 128), 0, CX * CY), jax.random.fold_in(streams_of[10], 1), 0, (CX * CY) - 1).astype(jnp.int32),
        "ov_frac": touch_ends(jax.random.randint(streams_of[11], (N_GX, N_GY, OBLK, 128), 0, FR_DEV), jax.random.fold_in(streams_of[11], 1), 0, FR_DEV - 1).astype(jnp.int32),
        "ov_weight": jnp.clip(jnp.exp(math.log(2.0) - 2.3025851 * jax.random.uniform(streams_of[12], (N_GX, N_GY, OBLK, 128), jnp.float32) ** block_scale(streams_of[12], (N_GX, N_GY, OBLK, 128), ((0, 8), (1, 2)), -0.2, 0.2)), 0.2, 2.0),
        "ov_count": draw_ov_count(jax.random.fold_in(streams_of[14], 71), part),
    }


fracture_storage = 0.1


def harmonic(first_perm, second_perm):
    return 2.0 * first_perm * second_perm / (first_perm + second_perm)


def reference(source_matrix, source_fracture, aperture, storage, perm_class, class_perm, send_slots, isect_local, isect_other, isect_count, ov_cell, ov_frac, ov_weight, ov_count):
    classes = jnp.arange(NCLASS, dtype=jnp.int32)
    perm = jnp.sum(jnp.where(perm_class[:, :, None] == classes, class_perm, 0.0), -1)
    kpad = jnp.pad(perm, 1)
    east_trans = harmonic(perm, kpad[2:, 1:-1])
    west_trans = harmonic(perm, kpad[:-2, 1:-1])
    north_trans = harmonic(perm, kpad[1:-1, 2:])
    south_trans = harmonic(perm, kpad[1:-1, :-2])
    parts = jnp.arange(N_GX, dtype=jnp.int32)[:, None]
    local_first = isect_local.reshape(N_GX, IBLK * 128)
    local_other = isect_other.reshape(N_GX, IBLK * 128)
    first_idx = parts * FR_DEV + local_first
    ghost_slot = jnp.maximum(local_other - FR_DEV, 0)
    group_k = ghost_slot // GHOST
    slot_index = ghost_slot % GHOST
    offsets = jnp.array([1, -1, 2, -2], dtype=jnp.int32)
    peer_part = (parts - offsets[group_k] + N_GX) % N_GX
    remote_idx = peer_part * FR_DEV + send_slots[peer_part, group_k * GHOST + slot_index]
    second_idx = jnp.where(local_other < FR_DEV, parts * FR_DEV + local_other, remote_idx)
    positions = jnp.arange(128, dtype=jnp.int32)
    live_rows = (positions[None, None, :] < isect_count.reshape(N_GX, IBLK)[:, :, None]).reshape(N_GX, IBLK * 128)
    first_idx = first_idx.reshape(-1)
    second_idx = second_idx.reshape(-1)
    live_rows = live_rows.reshape(-1)
    cond = aperture * aperture * aperture
    cond_first = cond[:, first_idx]
    cond_second = cond[:, second_idx]
    edge_cond = jnp.where(live_rows[None, :], 2.0 * cond_first * cond_second / (cond_first + cond_second), 0.0)
    row_x = jnp.arange(N_GX, dtype=jnp.int32)[:, None, None, None]
    row_y = jnp.arange(N_GY, dtype=jnp.int32)[None, :, None, None]
    matrix_idx = ((row_x * CX + ov_cell // CY) * NY + row_y * CY + ov_cell % CY).reshape(-1)
    frac_idx = (row_x * FR_DEV + ov_frac).reshape(-1)
    ov_live = positions < ov_count[:, :, :, None]
    weights = jnp.where(ov_live, ov_weight, 0.0).reshape(-1)

    def operate(field_m, field_f):
        padded = jnp.pad(field_m, ((0, 0), (1, 1), (1, 1)))
        out_m = storage * field_m + east_trans * (field_m - padded[:, 2:, 1:-1]) + west_trans * (field_m - padded[:, :-2, 1:-1])
        out_m = out_m + north_trans * (field_m - padded[:, 1:-1, 2:]) + south_trans * (field_m - padded[:, 1:-1, :-2])
        flat_m = field_m.reshape(MEMB, NX * NY)
        flow = weights * (flat_m[:, matrix_idx] - field_f[:, frac_idx])
        out_m = out_m.reshape(MEMB, NX * NY).at[:, matrix_idx].add(flow).reshape(MEMB, NX, NY)
        fluxes = edge_cond * (field_f[:, first_idx] - field_f[:, second_idx])
        out_f = fracture_storage * field_f
        out_f = out_f.at[:, first_idx].add(fluxes).at[:, second_idx].add(-fluxes).at[:, frac_idx].add(-flow)
        return out_m, out_f

    diag_m = storage + east_trans + west_trans + north_trans + south_trans
    diag_m = diag_m + jnp.zeros((NX * NY,), jnp.float32).at[matrix_idx].add(weights).reshape(NX, NY)
    diag_f = fracture_storage + jnp.zeros((MEMB, NF), jnp.float32).at[:, first_idx].add(edge_cond)

    def inner(left_m, right_m, left_f, right_f):
        return jnp.sum((left_m * right_m).reshape(MEMB, -1), 1) + jnp.sum(left_f * right_f, 1)

    sol_m = jnp.zeros_like(source_matrix)
    sol_f = jnp.zeros_like(source_fracture)
    resid_m, resid_f = source_matrix, source_fracture
    prec_m = resid_m / diag_m
    prec_f = resid_f / diag_f
    dir_m, dir_f = prec_m, prec_f
    rz_now = inner(resid_m, prec_m, resid_f, prec_f)
    for iteration in range(ITERS):
        image_m, image_f = operate(dir_m, dir_f)
        alpha = rz_now / inner(dir_m, image_m, dir_f, image_f)
        sol_m = sol_m + alpha[:, None, None] * dir_m
        sol_f = sol_f + alpha[:, None] * dir_f
        resid_m = resid_m - alpha[:, None, None] * image_m
        resid_f = resid_f - alpha[:, None] * image_f
        prec_m = resid_m / diag_m
        prec_f = resid_f / diag_f
        rz_next = inner(resid_m, prec_m, resid_f, prec_f)
        ratio = rz_next / rz_now
        dir_m = prec_m + ratio[:, None, None] * dir_m
        dir_f = prec_f + ratio[:, None] * dir_f
        rz_now = rz_next
    return sol_m, sol_f
```

```python
import functools

import jax
import jax.numpy as jnp
from jax import lax
from jax.experimental import pallas as pl
from jax.experimental.pallas import tpu as pltpu
from jax.sharding import PartitionSpec as P

FRACTURE_STORAGE = 0.1
F32 = jnp.float32
BF16 = jnp.bfloat16
LANES = 128
GROUP = 4


def split3(x):
    high = x.astype(BF16)
    rest = x - high.astype(F32)
    mid = rest.astype(BF16)
    low = (rest - mid.astype(F32)).astype(BF16)
    return jnp.concatenate([high, mid, low], axis=0)


def pick(x, table, transposed=False):
    rows = x.shape[0]
    dims = (((1,), (1 if transposed else 0,)), ((), ()))
    out = lax.dot_general(split3(x), table, dims, preferred_element_type=F32)
    return out[:rows] + out[rows : 2 * rows] + out[2 * rows :]


def harmonic(first_perm, second_perm):
    return 2.0 * first_perm * second_perm / (first_perm + second_perm)


def one_hot(index_row, size):
    shape = (size, index_row.shape[1])
    ids = lax.broadcasted_iota(jnp.int32, shape, 0)
    return jnp.where(ids == index_row, 1.0, 0.0).astype(BF16)


def to_blocks(x):
    return jnp.concatenate(
        [x[:, q : q + LANES] for q in range(0, x.shape[1], LANES)], axis=0
    )


def from_blocks(x, rows):
    return jnp.concatenate(
        [x[q : q + rows] for q in range(0, x.shape[0], rows)], axis=1
    )


def by_group(first, second, third, fourth):
    group = first.shape[1] // 4
    lane = lax.broadcasted_iota(jnp.int32, first.shape, 1)
    return jnp.where(
        lane < group,
        first,
        jnp.where(lane < 2 * group, second, jnp.where(lane < 3 * group, third, fourth)),
    )


def total_rows(x):
    return jnp.sum(jnp.transpose(x), axis=0, keepdims=True)


def fold_lanes(x):
    rows, width = x.shape
    out = x[:, :LANES]
    for q in range(LANES, width, LANES):
        out = out + x[:, q : q + LANES]
    return out


def tables_kernel(local_ref, other_ref, frac_ref, first_ref, second_ref, ofrac_ref):
    first_ref[...] = one_hot(local_ref[...], first_ref.shape[0])
    second_ref[...] = one_hot(other_ref[...], second_ref.shape[0])
    ofrac_ref[...] = one_hot(frac_ref[...], ofrac_ref.shape[0])


def opening_kernel(
    place_ref,
    perm_table_ref,
    class_ref,
    col_ref,
    storage_ref,
    source_ref,
    aperture_ref,
    slots_ref,
    cell_ref,
    weight_ref,
    coef_ref,
    oy_ref,
    ox_ref,
    oslot_ref,
    cond_ref,
    up_ref,
    down_ref,
    far_ref,
):
    x_cells, y_cells = class_ref.shape
    members = source_ref.shape[0]
    half = aperture_ref.shape[0]
    high_side = place_ref[2] == 0

    def perm_of(classes):
        perm = jnp.zeros(classes.shape, F32)
        for index in range(perm_table_ref.shape[0]):
            perm = jnp.where(classes == index, perm_table_ref[index], perm)
        return perm

    perm = perm_of(class_ref[...])
    col = perm_of(col_ref[...])
    lane = lax.broadcasted_iota(jnp.int32, perm.shape, 1)
    row = lax.broadcasted_iota(jnp.int32, perm.shape, 0)
    north = jnp.concatenate([perm[:, 1:], col], axis=1)
    south = jnp.concatenate([col, perm[:, :-1]], axis=1)
    tn = jnp.where((lane == y_cells - 1) & jnp.logical_not(high_side), 0.0, harmonic(perm, north))
    ts = jnp.where((lane == 0) & high_side, 0.0, harmonic(perm, south))
    east = jnp.concatenate([perm[1:], perm[:1]], axis=0)
    west = jnp.concatenate([perm[-1:], perm[:-1]], axis=0)
    te = jnp.where(row == x_cells - 1, 0.0, harmonic(perm, east))
    tw = jnp.where(row == 0, 0.0, harmonic(perm, west))

    cell = cell_ref[...]
    oy = one_hot(cell % y_cells, y_cells)
    oy_ref[...] = oy
    shape_x = (x_cells, cell.shape[1])
    at_x = lax.broadcasted_iota(jnp.int32, shape_x, 0) == cell // y_cells
    ox_ref[...] = jnp.where(at_x, 1.0, 0.0)
    wsum = pick(jnp.where(at_x, weight_ref[...], 0.0), oy, True)

    part = storage_ref[...] + te + tw + tn + ts + wsum
    coef_ref[0] = te
    coef_ref[1] = tw
    coef_ref[2] = tn
    coef_ref[3] = ts
    coef_ref[4] = part
    coef_ref[5] = perm

    aperture = aperture_ref[...]
    cond = aperture * aperture * aperture
    cond_ref[...] = cond
    oslot = one_hot(slots_ref[...], cond.shape[1])
    oslot_ref[...] = oslot
    supplied = pick(cond, oslot)
    far_ref[...] = supplied
    blocks = y_cells // LANES
    for ref, at in ((up_ref, x_cells - 1), (down_ref, 0)):
        edge = source_ref[:, at, :]
        ref[0 : blocks * members, :] = to_blocks(edge)
        ref[blocks * members : blocks * members + blocks, :] = to_blocks(perm[at : at + 1])
        ref[blocks * members + blocks : blocks * members + 2 * blocks, :] = to_blocks(part[at : at + 1])
        ref[blocks * members + 2 * blocks : blocks * members + 2 * blocks + half, :] = supplied


def network_out(vf, sr, first, second, oslot):
    cells = first.shape[0]
    supplied = pick(vf, oslot)
    at_first = pick(vf, first)
    sums = pick(sr * at_first, second[cells:], True)
    return supplied, at_first, sums


def margin_values(read, members, oy, ox, scratch_ref):
    x_cells = ox.shape[0]

    @pl.loop(0, members // GROUP)
    def _(index):
        start = index * GROUP
        block = read(start)
        y_cells = block.shape[2]
        found = pick(block.reshape(GROUP * x_cells, y_cells), oy)
        found = found.reshape(GROUP, x_cells, -1) * ox[None]
        for m in range(GROUP):
            scratch_ref[pl.ds(start + m, 1), :] = jnp.sum(found[m], axis=0, keepdims=True)


def edge_column(tile_low, tile_high, high_side, m):
    tile = jnp.where(high_side, tile_high, tile_low)
    return pltpu.roll(tile, jnp.where(high_side, lax.rem(m + 1, LANES), m), 1)


def send_core(y_ref, vf, margin, weight, ofrac, column, j, half, work_ref, wown_ref):
    frac_blocks = vf.shape[1] // LANES
    work_ref[...] = pick(margin * weight, ofrac, True)
    wown_ref[...] = work_ref[pl.ds(pl.multiple_of(j * half, half), half), :]
    other = work_ref[pl.ds(pl.multiple_of((1 - j) * half, half), half), :]
    size = frac_blocks * half
    y_ref[0:size, :] = to_blocks(vf)
    y_ref[size : 2 * size, :] = to_blocks(other)
    y_ref[2 * size : 2 * size + column.shape[0], :] = column


def first_kernel(
    place_ref,
    count_ref,
    coef_ref,
    cond_ref,
    source_ref,
    source_f_ref,
    weight_ref,
    near_a_ref,
    near_b_ref,
    far_c_ref,
    far_d_ref,
    first_ref,
    second_ref,
    ofrac_ref,
    oslot_ref,
    oy_ref,
    ox_ref,
    unit_ref,
    v_ref,
    vf_ref,
    halo_ref,
    sr_ref,
    scale_f_ref,
    at_first_ref,
    wown_ref,
    sent_ref,
    core_ref,
    dots_ref,
    margin_ref,
    work_ref,
    acc_ref,
    column_ref,
):
    members, x_cells, y_cells = source_ref.shape
    half, frac_cells = source_f_ref.shape
    blocks = y_cells // LANES
    even = place_ref[0] == 0
    low_pair = place_ref[1] == 0
    j = place_ref[2]
    high_side = j == 0
    base = blocks * members

    def plus1(at, size):
        return jnp.where(even, near_a_ref[at : at + size, :], near_b_ref[at : at + size, :])

    def minus1(at, size):
        return jnp.where(even, near_b_ref[at : at + size, :], near_a_ref[at : at + size, :])

    te, tw = coef_ref[0], coef_ref[1]
    part, perm = coef_ref[4], coef_ref[5]
    row = lax.broadcasted_iota(jnp.int32, perm.shape, 0)
    perm_plus = from_blocks(plus1(base, blocks), 1)
    perm_minus = from_blocks(minus1(base, blocks), 1)
    part_plus = from_blocks(plus1(base + blocks, blocks), 1)
    part_minus = from_blocks(minus1(base + blocks, blocks), 1)
    te_edge = jnp.where(place_ref[4] == 1, 0.0, harmonic(perm[x_cells - 1 :], perm_plus))
    tw_edge = jnp.where(place_ref[3] == 1, 0.0, harmonic(perm[:1], perm_minus))
    te = jnp.where(row == x_cells - 1, te_edge, te)
    tw = jnp.where(row == 0, tw_edge, tw)
    diag = (
        part
        + jnp.where(row == x_cells - 1, te_edge, 0.0)
        + jnp.where(row == 0, tw_edge, 0.0)
    )
    inverse = 1.0 / diag
    unit_ref[0] = te * inverse
    unit_ref[1] = tw * inverse
    unit_ref[2] = coef_ref[2] * inverse
    unit_ref[3] = coef_ref[3] * inverse
    unit_ref[4] = inverse
    unit_ref[5] = diag
    halo_ref[0] = from_blocks(plus1(0, base), members) / (part_plus + te_edge)
    halo_ref[1] = from_blocks(minus1(0, base), members) / (part_minus + tw_edge)

    slot_at = base + 2 * blocks
    far_plus = jnp.where(low_pair, far_c_ref[...], far_d_ref[...])
    far_minus = jnp.where(low_pair, far_d_ref[...], far_c_ref[...])
    ghosts = by_group(minus1(slot_at, half), plus1(slot_at, half), far_minus, far_plus)
    first, second, oslot = first_ref[...], second_ref[...], oslot_ref[...]
    cond = cond_ref[...]
    cond_first = pick(cond, first)
    cond_second = pick(cond, second[:frac_cells]) + pick(ghosts, second[frac_cells:])
    lane = lax.broadcasted_iota(jnp.int32, cond_first.shape, 1)
    live = jnp.zeros(cond_first.shape, jnp.bool_)
    for block in range(cond_first.shape[1] // LANES):
        start = block * LANES
        live = live | ((lane >= start) & (lane < start + count_ref[block]))
    sr = jnp.where(live, harmonic(cond_first, cond_second), 0.0)
    sr_ref[...] = sr
    diag_f = FRACTURE_STORAGE + pick(sr, first, True)
    inverse_f = 1.0 / diag_f
    scale_f_ref[0] = inverse_f
    scale_f_ref[1] = diag_f
    source_f = source_f_ref[...]
    vf = source_f * inverse_f
    vf_ref[...] = vf
    supplied, at_first, sums = network_out(vf, sr, first, second, oslot)
    at_first_ref[...] = at_first
    sent_ref[0:half, :] = supplied
    sent_ref[half : 2 * half, :] = sums
    sent_ref[2 * half : 3 * half, :] = pick(sr, second[frac_cells:], True)

    acc_ref[...] = jnp.zeros_like(acc_ref)
    acc_ref[pl.ds(pl.multiple_of(j * half, half), half), :] = fold_lanes(source_f * vf)
    lane_c = lax.broadcasted_iota(jnp.int32, (x_cells, LANES), 1)
    column_ref[...] = jnp.zeros_like(column_ref)

    @pl.loop(0, members)
    def _(m):
        value = source_ref[m]
        scaled = value * unit_ref[4]
        v_ref[m] = scaled
        acc_ref[pl.ds(m, 1), :] += jnp.sum(fold_lanes(value * scaled), axis=0, keepdims=True)
        moved = edge_column(scaled[:, :LANES], scaled[:, y_cells - LANES :], high_side, m)
        column_ref[...] = jnp.where(lane_c == m, moved, column_ref[...])

    margin_values(lambda s: v_ref[pl.ds(s, GROUP)], members, oy_ref[...], ox_ref[...], margin_ref)
    weight = weight_ref[...]
    send_core(core_ref, vf, margin_ref[...], weight, ofrac_ref[...], column_ref[...], j, half, work_ref, wown_ref)
    wsum = pick(jnp.broadcast_to(weight, (8, weight.shape[1])), ofrac_ref[...], True)
    tail = core_ref.shape[0] - 8 * (frac_cells // LANES)
    core_ref[tail:, :] = to_blocks(wsum)
    dots_ref[...] = jnp.broadcast_to(total_rows(acc_ref[...]), dots_ref.shape)


def step_kernel(
    kind,
    place_ref,
    v_ref,
    vf_ref,
    halo_in_ref,
    near_a_ref,
    near_b_ref,
    far_c_ref,
    far_d_ref,
    core_in_ref,
    at_first_in_ref,
    wown_in_ref,
    sr_ref,
    scale_f_ref,
    own_f_in_ref,
    unit_ref,
    weight_ref,
    first_ref,
    second_ref,
    ofrac_ref,
    oslot_ref,
    oy_ref,
    ox_ref,
    *refs,
):
    if kind == "last":
        dots_ref, flow_ref, work_ref, acc_ref, acc2_ref = refs
    else:
        (
            out_ref,
            out_f_ref,
            own_f_ref,
            at_first_ref,
            wown_ref,
            up_ref,
            down_ref,
            sent_ref,
            core_ref,
            dots_ref,
            flow_ref,
            work_ref,
            acc_ref,
            acc2_ref,
            margin_ref,
            column_ref,
        ) = refs
    members, x_cells, y_cells = v_ref.shape
    half, frac_cells = vf_ref.shape
    blocks = y_cells // LANES
    frac_blocks = frac_cells // LANES
    even = place_ref[0] == 0
    low_pair = place_ref[1] == 0
    j = place_ref[2]
    high_side = j == 0
    base = 0 if kind == "first" else blocks * members

    def plus1(at, size):
        return jnp.where(even, near_a_ref[at : at + size, :], near_b_ref[at : at + size, :])

    def minus1(at, size):
        return jnp.where(even, near_b_ref[at : at + size, :], near_a_ref[at : at + size, :])

    def plus2(at, size):
        return jnp.where(low_pair, far_c_ref[at : at + size, :], far_d_ref[at : at + size, :])

    def minus2(at, size):
        return jnp.where(low_pair, far_d_ref[at : at + size, :], far_c_ref[at : at + size, :])

    first, second, oslot = first_ref[...], second_ref[...], oslot_ref[...]
    vf = vf_ref[...]
    ghosts = by_group(minus1(base, half), plus1(base, half), minus2(0, half), plus2(0, half))
    sums = by_group(
        plus1(base + half, half), minus1(base + half, half), plus2(half, half), minus2(half, half)
    )
    size = frac_blocks * half
    theirs = from_blocks(core_in_ref[0:size, :], half)
    their_sums = from_blocks(core_in_ref[size : 2 * size, :], half)
    column_in = core_in_ref[2 * size : 2 * size + x_cells, :]
    if kind == "first":
        at = 2 * half
        back = by_group(
            plus1(base + at, half), minus1(base + at, half), plus2(at, half), minus2(at, half)
        )
        wsum = pick(jnp.broadcast_to(weight_ref[...], (8, weight_ref.shape[1])), ofrac_ref[...], True)
        tail = core_in_ref.shape[0] - 8 * frac_blocks
        wsum = wsum + from_blocks(core_in_ref[tail:, :], 8)
        own_f = FRACTURE_STORAGE + wsum[:1] + pick(back, oslot, True)
        own_f_ref[...] = own_f
    else:
        own_f = own_f_in_ref[...]
        if kind == "middle":
            own_f_ref[...] = own_f
    sr = sr_ref[...]
    at_second = pick(vf, second[:frac_cells]) + pick(ghosts, second[frac_cells:])
    flux = sr * (at_first_in_ref[...] - at_second)
    image_f = own_f * vf + pick(flux, first, True) - pick(flux, second[:frac_cells], True)
    image_f = image_f - pick(sums, oslot, True) - wown_in_ref[...] - their_sums
    next_f = image_f * scale_f_ref[0]

    own_rows = pl.ds(pl.multiple_of(j * half, half), half)
    work_ref[own_rows, :] = vf
    work_ref[pl.ds(pl.multiple_of((1 - j) * half, half), half), :] = theirs
    weight = weight_ref[...]
    flow_ref[...] = pick(work_ref[...], ofrac_ref[...]) * weight

    acc_ref[...] = jnp.zeros_like(acc_ref)
    acc2_ref[...] = jnp.zeros_like(acc2_ref)
    acc_ref[own_rows, :] = fold_lanes(vf * image_f)
    if kind != "last":
        acc2_ref[own_rows, :] = fold_lanes(next_f * image_f)
        column_ref[...] = jnp.zeros_like(column_ref)
        out_f_ref[...] = next_f
    lane_c = lax.broadcasted_iota(jnp.int32, (x_cells, LANES), 1)
    lane = lax.broadcasted_iota(jnp.int32, (x_cells, y_cells), 1)
    row = lax.broadcasted_iota(jnp.int32, (x_cells, y_cells), 0)
    oy, ox = oy_ref[...], ox_ref[...]

    def halo(m, side):
        if kind == "first":
            return halo_in_ref[side, pl.ds(m, 1), :]
        pieces = []
        for q in range(blocks):
            a = near_a_ref[pl.ds(q * members + m, 1), :]
            b = near_b_ref[pl.ds(q * members + m, 1), :]
            pieces.append(jnp.where(even, a, b) if side == 0 else jnp.where(even, b, a))
        return jnp.concatenate(pieces, axis=1)

    @pl.loop(0, members // GROUP)
    def _(index):
        start = index * GROUP
        parts = []
        for k in range(GROUP):
            parts.append(ox * flow_ref[pl.ds(start + k, 1), :])
        coupled = pick(jnp.concatenate(parts, axis=0), oy, True)
        for k in range(GROUP):
            m = start + k
            value = v_ref[m]
            east = jnp.where(row == x_cells - 1, halo(m, 0), pltpu.roll(value, x_cells - 1, 0))
            west = jnp.where(row == 0, halo(m, 1), pltpu.roll(value, 1, 0))
            moved = pltpu.roll(column_in, jnp.where(high_side, LANES - 1 - m, lax.rem(LANES - m, LANES)), 1)
            moved = jnp.concatenate([moved] * blocks, axis=1)
            north = jnp.where(lane == y_cells - 1, moved, pltpu.roll(value, y_cells - 1, 1))
            south = jnp.where(lane == 0, moved, pltpu.roll(value, 1, 1))
            image = value - unit_ref[0] * east - unit_ref[1] * west
            image = image - unit_ref[2] * north - unit_ref[3] * south
            image = image - coupled[k * x_cells : (k + 1) * x_cells] * unit_ref[4]
            heavy = image * unit_ref[5]
            acc_ref[pl.ds(m, 1), :] += jnp.sum(fold_lanes(value * heavy), axis=0, keepdims=True)
            if kind != "last":
                acc2_ref[pl.ds(m, 1), :] += jnp.sum(fold_lanes(image * heavy), axis=0, keepdims=True)
                out_ref[m] = image
                shifted = edge_column(image[:, :LANES], image[:, y_cells - LANES :], high_side, m)
                column_ref[...] = jnp.where(lane_c == m, shifted, column_ref[...])
                for q in range(blocks):
                    cut = image[:, q * LANES : (q + 1) * LANES]
                    up_ref[pl.ds(q * members + m, 1), :] = cut[x_cells - 1 :]
                    down_ref[pl.ds(q * members + m, 1), :] = cut[:1]

    dots = [total_rows(acc_ref[...])]
    if kind != "last":
        dots.append(total_rows(acc2_ref[...]))
        supplied, at_first, sums = network_out(next_f, sr, first, second, oslot)
        at_first_ref[...] = at_first
        at = blocks * members
        for ref, where in ((up_ref, at), (down_ref, at), (sent_ref, 0)):
            ref[where : where + half, :] = supplied
            ref[where + half : where + 2 * half, :] = sums
        margin_values(lambda s: out_ref[pl.ds(s, GROUP)], members, oy, ox, margin_ref)
        send_core(
            core_ref, next_f, margin_ref[...], weight, ofrac_ref[...], column_ref[...], j, half, work_ref, wown_ref
        )
    dots.append(jnp.zeros((8 - len(dots), members), F32))
    dots_ref[...] = jnp.concatenate(dots, axis=0)


def close_kernel(place_ref, totals_ref, v0_ref, v1_ref, v2_ref, f0_ref, f1_ref, f2_ref, x_ref, xf_ref, c_ref):
    members, x_cells, y_cells = v0_ref.shape
    half, frac_cells = f0_ref.shape

    total = jnp.sum(totals_ref[...], axis=0)
    m0, m1, m2, m3, m4, m5 = (total[k : k + 1] for k in range(6))
    alpha0 = m0 / m1
    rz1 = m0 - 2.0 * alpha0 * m1 + alpha0 * alpha0 * m2
    beta1 = rz1 / m0
    a, b = 1.0 + beta1, -alpha0
    pap1 = a * a * m1 + 2.0 * a * b * m2 + b * b * m3
    alpha1 = rz1 / pap1
    e = -alpha0 - alpha1 * a
    g = -alpha1 * b
    rz2 = m0 + 2.0 * e * m1 + (e * e + 2.0 * g) * m2 + 2.0 * e * g * m3 + g * g * m4
    beta2 = rz2 / rz1
    c = 1.0 + beta2 * a
    d = e + beta2 * b
    pap2 = c * c * m1 + 2.0 * c * d * m2 + (d * d + 2.0 * c * g) * m3 + 2.0 * d * g * m4 + g * g * m5
    alpha2 = rz2 / pap2
    c0 = alpha0 + alpha1 * a + alpha2 * c
    c1 = alpha1 * b + alpha2 * d
    c2 = alpha2 * g
    for k, row in enumerate((c0, c1, c2)):
        c_ref[k] = jnp.transpose(jnp.broadcast_to(row, (LANES, LANES)))
    j = place_ref[2]
    own = pl.ds(pl.multiple_of(j * half, half), half)

    def wide(k, rows, width):
        return jnp.concatenate([c_ref[k, rows, :]] * (width // LANES), axis=1)

    xf_ref[...] = (
        wide(0, own, frac_cells) * f0_ref[...]
        + wide(1, own, frac_cells) * f1_ref[...]
        + wide(2, own, frac_cells) * f2_ref[...]
    )

    @pl.loop(0, members)
    def _(m):
        rows = pl.ds(m, 1)
        x_ref[m] = (
            wide(0, rows, y_cells) * v0_ref[m]
            + wide(1, rows, y_cells) * v1_ref[m]
            + wide(2, rows, y_cells) * v2_ref[m]
        )


def pairs_of(count, stride, phase):
    out = []
    for index in range(count):
        if (index // stride) % 2 == phase:
            mate = (index + stride) % count
            out += [(index, mate), (mate, index)]
    return out


VMEM = pl.BlockSpec(memory_space=pltpu.VMEM)
SMEM = pl.BlockSpec(memory_space=pltpu.SMEM)


def call(kernel, name, args, outs, scratch=(), scalars=0, cost=None):
    return pl.pallas_call(
        kernel,
        name=name,
        out_shape=[jax.ShapeDtypeStruct(shape, dtype) for shape, dtype in outs],
        in_specs=[SMEM] * scalars + [VMEM] * (len(args) - scalars),
        out_specs=[VMEM] * len(outs),
        scratch_shapes=list(scratch),
        compiler_params=pltpu.CompilerParams(vmem_limit_bytes=40 * 1024 * 1024),
        cost_estimate=cost,
    )(*args)


def per_device(
    source_matrix,
    source_fracture,
    aperture,
    storage,
    perm_class,
    class_perm,
    send_slots,
    isect_local,
    isect_other,
    isect_count,
    ov_cell,
    ov_frac,
    ov_weight,
    ov_count,
):
    members, x_cells, y_cells = source_matrix.shape
    half, frac_cells = source_fracture.shape
    slots = send_slots.shape[1]
    rows = isect_local.size
    margin = ov_cell.size
    count = lax.axis_size("gx")
    i, j = lax.axis_index("gx"), lax.axis_index("gy")
    place = jnp.stack(
        [i % 2, (i // 2) % 2, j, (i == 0).astype(jnp.int32), (i == count - 1).astype(jnp.int32)]
    ).astype(jnp.int32)

    def near(up, down):
        even = i % 2 == 0
        to_a = jnp.where(even, up, down)
        to_b = jnp.where(even, down, up)
        return (
            lax.ppermute(to_a, "gx", pairs_of(count, 1, 0)),
            lax.ppermute(to_b, "gx", pairs_of(count, 1, 1)),
        )

    def far(value):
        return (
            lax.ppermute(value, "gx", pairs_of(count, 2, 0)),
            lax.ppermute(value, "gx", pairs_of(count, 2, 1)),
        )

    def core(value):
        return lax.ppermute(value, "gy", [(0, 1), (1, 0)])

    blocks = y_cells // LANES
    frac_blocks = frac_cells // LANES
    positions = jnp.arange(LANES, dtype=jnp.int32)
    ov_live = positions[None, :] < ov_count.reshape(-1, 1)
    weight = jnp.where(ov_live, ov_weight.reshape(ov_live.shape), 0.0).reshape(1, margin)
    col = core(jnp.where(j == 0, perm_class[:, y_cells - 1 :], perm_class[:, :1]))
    near_rows = blocks * members + 2 * blocks + half
    coef, oy, ox, oslot, cond, up, down, supplied = call(
        opening_kernel,
        "opening",
        (
            place,
            class_perm,
            perm_class,
            col,
            storage,
            source_matrix,
            aperture,
            send_slots,
            ov_cell.reshape(1, margin),
            weight,
        ),
        [
            ((6, x_cells, y_cells), F32),
            ((y_cells, margin), BF16),
            ((x_cells, margin), F32),
            ((frac_cells, slots), BF16),
            ((half, frac_cells), F32),
            ((near_rows, LANES), F32),
            ((near_rows, LANES), F32),
            ((half, slots), F32),
        ],
        scalars=2,
    )
    near_a, near_b = near(up, down)
    far_c, far_d = far(supplied)
    first, second, ofrac = call(
        tables_kernel,
        "tables",
        (isect_local.reshape(1, rows), isect_other.reshape(1, rows), ov_frac.reshape(1, margin)),
        [((frac_cells, rows), BF16), ((frac_cells + slots, rows), BF16), ((frac_cells, margin), BF16)],
    )
    core_rows = 2 * frac_blocks * half + x_cells
    (unit, v0, f0, halo, sr, scale_f, at_first, wown, sent, core_msg, dots0) = call(
        first_kernel,
        "first_vector",
        (
            place,
            isect_count,
            coef,
            cond,
            source_matrix,
            source_fracture,
            weight,
            near_a,
            near_b,
            far_c,
            far_d,
            first,
            second,
            ofrac,
            oslot,
            oy,
            ox,
        ),
        [
            ((6, x_cells, y_cells), F32),
            ((members, x_cells, y_cells), F32),
            ((half, frac_cells), F32),
            ((2, members, y_cells), F32),
            ((half, rows), F32),
            ((2, half, frac_cells), F32),
            ((half, rows), F32),
            ((half, frac_cells), F32),
            ((3 * half, LANES), F32),
            ((core_rows + 8 * frac_blocks, LANES), F32),
            ((8, members), F32),
        ],
        scratch=[
            pltpu.VMEM((members, margin), F32),
            pltpu.VMEM((members, frac_cells), F32),
            pltpu.VMEM((members, LANES), F32),
            pltpu.VMEM((x_cells, LANES), F32),
        ],
        scalars=2,
    )
    step_scratch = [
        pltpu.VMEM((members, margin), F32),
        pltpu.VMEM((members, frac_cells), F32),
        pltpu.VMEM((members, LANES), F32),
        pltpu.VMEM((members, LANES), F32),
    ]
    more_scratch = [pltpu.VMEM((members, margin), F32), pltpu.VMEM((x_cells, LANES), F32)]
    near_rows = blocks * members + 2 * half
    step_outs = [
        ((members, x_cells, y_cells), F32),
        ((half, frac_cells), F32),
        ((half, frac_cells), F32),
        ((half, rows), F32),
        ((half, frac_cells), F32),
        ((near_rows, LANES), F32),
        ((near_rows, LANES), F32),
        ((2 * half, LANES), F32),
        ((core_rows, LANES), F32),
        ((8, members), F32),
    ]
    fixed = (unit, weight, first, second, ofrac, oslot, oy, ox)

    near_a, near_b = near(sent, sent)
    far_c, far_d = far(sent)
    core_in = core(core_msg)
    v1, f1, own_f, at_first, wown, up, down, sent, core_msg, dots1 = call(
        functools.partial(step_kernel, "first"),
        "power_1",
        (place, v0, f0, halo, near_a, near_b, far_c, far_d, core_in, at_first, wown, sr, scale_f, scale_f) + fixed,
        step_outs,
        scratch=step_scratch + more_scratch,
        scalars=1,
    )
    near_a, near_b = near(up, down)
    far_c, far_d = far(sent)
    core_in = core(core_msg)
    v2, f2, own_f, at_first, wown, up, down, sent, core_msg, dots2 = call(
        functools.partial(step_kernel, "middle"),
        "power_2",
        (place, v1, f1, halo, near_a, near_b, far_c, far_d, core_in, at_first, wown, sr, scale_f, own_f) + fixed,
        step_outs,
        scratch=step_scratch + more_scratch,
        scalars=1,
    )
    near_a, near_b = near(up, down)
    far_c, far_d = far(sent)
    core_in = core(core_msg)
    (dots3,) = call(
        functools.partial(step_kernel, "last"),
        "power_3",
        (place, v2, f2, halo, near_a, near_b, far_c, far_d, core_in, at_first, wown, sr, scale_f, own_f) + fixed,
        [((8, members), F32)],
        scratch=step_scratch,
        scalars=1,
    )
    moments = jnp.concatenate([dots0[:1], dots1[:2], dots2[:2], dots3[:1], dots3[2:4]], axis=0)
    moments = jnp.pad(moments, ((0, 0), (0, LANES - members)))
    peers = count * lax.axis_size("gy")
    totals = lax.all_to_all(jnp.broadcast_to(moments[None], (peers, 8, LANES)), ("gx", "gy"), 0, 0)
    return call(
        close_kernel,
        "iterate",
        (place, totals, v0, v1, v2, f0, f1, f2),
        [((members, x_cells, y_cells), F32), ((half, frac_cells), F32)],
        scratch=[pltpu.VMEM((3, LANES, LANES), F32)],
        scalars=1,
    )


def solution(mesh):
    placed = (
        P("grp", "gx", "gy"),
        P(("grp", "gy"), "gx"),
        P(("grp", "gy"), "gx"),
        P("gx", "gy"),
        P("gx", "gy"),
        P(),
        P("gx", None),
        P("gx", None),
        P("gx", None),
        P("gx"),
        P("gx", "gy", None, None),
        P("gx", "gy", None, None),
        P("gx", "gy", None, None),
        P("gx", "gy", None),
    )
    return jax.shard_map(
        per_device,
        mesh=mesh,
        in_specs=placed,
        out_specs=(P("grp", "gx", "gy"), P(("grp", "gy"), "gx")),
        check_vma=False,
    )
```

```python
import functools

import jax
import jax.numpy as jnp
from jax import lax
from jax.experimental import pallas as pl
from jax.experimental.pallas import tpu as pltpu
from jax.sharding import PartitionSpec as P

FRACTURE_STORAGE = 0.1
F32 = jnp.float32
BF16 = jnp.bfloat16
LANES = 128
GROUP = 16


def split3(x):
    high = x.astype(BF16)
    rest = x - high.astype(F32)
    mid = rest.astype(BF16)
    low = (rest - mid.astype(F32)).astype(BF16)
    return jnp.concatenate([high, mid, low], axis=0)


def pick(x, table, transposed=False):
    rows = x.shape[0]
    dims = (((1,), (1 if transposed else 0,)), ((), ()))
    out = lax.dot_general(split3(x), table, dims, preferred_element_type=F32)
    return out[:rows] + out[rows : 2 * rows] + out[2 * rows :]


def harmonic(first_perm, second_perm):
    return 2.0 * first_perm * second_perm / (first_perm + second_perm)


def one_hot(index_row, size):
    shape = (size, index_row.shape[1])
    ids = lax.broadcasted_iota(jnp.int32, shape, 0)
    return jnp.where(ids == index_row, 1.0, 0.0).astype(BF16)


def to_blocks(x):
    return jnp.concatenate(
        [x[:, q : q + LANES] for q in range(0, x.shape[1], LANES)], axis=0
    )


def from_blocks(x, rows):
    return jnp.concatenate(
        [x[q : q + rows] for q in range(0, x.shape[0], rows)], axis=1
    )


def by_group(first, second, third, fourth):
    group = first.shape[1] // 4
    lane = lax.broadcasted_iota(jnp.int32, first.shape, 1)
    return jnp.where(
        lane < group,
        first,
        jnp.where(lane < 2 * group, second, jnp.where(lane < 3 * group, third, fourth)),
    )


def total_rows(x):
    return jnp.sum(jnp.transpose(x), axis=0, keepdims=True)


def fold_lanes(x):
    rows, width = x.shape
    out = x[:, :LANES]
    for q in range(LANES, width, LANES):
        out = out + x[:, q : q + LANES]
    return out


def opening_kernel(
    place_ref,
    perm_table_ref,
    class_ref,
    col_ref,
    storage_ref,
    source_ref,
    aperture_ref,
    slots_ref,
    cell_ref,
    weight_ref,
    coef_ref,
    oy_ref,
    ox_ref,
    oslot_ref,
    cond_ref,
    up_ref,
    down_ref,
    far_ref,
):
    x_cells, y_cells = class_ref.shape
    members = source_ref.shape[0]
    half = aperture_ref.shape[0]
    high_side = place_ref[2] == 0

    def perm_of(classes):
        perm = jnp.zeros(classes.shape, F32)
        for index in range(perm_table_ref.shape[0]):
            perm = jnp.where(classes == index, perm_table_ref[index], perm)
        return perm

    perm = perm_of(class_ref[...])
    col = perm_of(col_ref[...])
    lane = lax.broadcasted_iota(jnp.int32, perm.shape, 1)
    row = lax.broadcasted_iota(jnp.int32, perm.shape, 0)
    north = jnp.concatenate([perm[:, 1:], col], axis=1)
    south = jnp.concatenate([col, perm[:, :-1]], axis=1)
    tn = jnp.where((lane == y_cells - 1) & jnp.logical_not(high_side), 0.0, harmonic(perm, north))
    ts = jnp.where((lane == 0) & high_side, 0.0, harmonic(perm, south))
    east = jnp.concatenate([perm[1:], perm[:1]], axis=0)
    west = jnp.concatenate([perm[-1:], perm[:-1]], axis=0)
    te = jnp.where(row == x_cells - 1, 0.0, harmonic(perm, east))
    tw = jnp.where(row == 0, 0.0, harmonic(perm, west))

    cell = cell_ref[...]
    oy = one_hot(cell % y_cells, y_cells)
    oy_ref[...] = oy
    shape_x = (x_cells, cell.shape[1])
    at_x = lax.broadcasted_iota(jnp.int32, shape_x, 0) == cell // y_cells
    ox_ref[...] = jnp.where(at_x, 1.0, 0.0)
    wsum = pick(jnp.where(at_x, weight_ref[...], 0.0), oy, True)

    part = storage_ref[...] + te + tw + tn + ts + wsum
    coef_ref[0] = te
    coef_ref[1] = tw
    coef_ref[2] = tn
    coef_ref[3] = ts
    coef_ref[4] = part
    coef_ref[5] = perm

    aperture = aperture_ref[...]
    cond = aperture * aperture * aperture
    cond_ref[...] = cond
    oslot = one_hot(slots_ref[...], cond.shape[1])
    oslot_ref[...] = oslot
    supplied = pick(cond, oslot)
    far_ref[...] = supplied
    blocks = y_cells // LANES
    for ref, at in ((up_ref, x_cells - 1), (down_ref, 0)):
        edge = source_ref[:, at, :]
        ref[0 : blocks * members, :] = to_blocks(edge)
        ref[blocks * members : blocks * members + blocks, :] = to_blocks(perm[at : at + 1])
        ref[blocks * members + blocks : blocks * members + 2 * blocks, :] = to_blocks(part[at : at + 1])
        ref[blocks * members + 2 * blocks : blocks * members + 2 * blocks + half, :] = supplied


def neighbours(place_ref, near_a_ref, near_b_ref, far_c_ref, far_d_ref):
    def reader(flag, at_zero, at_one):
        return lambda at, size: jnp.where(
            place_ref[flag] == 0, at_zero[at : at + size, :], at_one[at : at + size, :]
        )

    return (
        reader(0, near_a_ref, near_b_ref),
        reader(0, near_b_ref, near_a_ref),
        reader(1, far_c_ref, far_d_ref),
        reader(1, far_d_ref, far_c_ref),
    )


def spread(x, members):
    return jnp.concatenate(
        [jnp.broadcast_to(x[:, q : q + LANES], (members, LANES)) for q in range(0, x.shape[1], LANES)], axis=0
    )


def margin_values(found, ox):
    found = found.reshape(-1, *ox.shape) * ox[None]
    return jnp.sum(found, axis=1)


def border_column(tile_low, tile_high, high_side, m):
    tile = jnp.where(high_side, tile_high, tile_low)
    return pltpu.roll(tile, jnp.where(high_side, lax.rem(m + 1, LANES), m), 1)


def border_row(row_values, high_side):
    members, y_cells = row_values.shape
    tile = jnp.where(high_side, row_values[:, y_cells - LANES :], row_values[:, :LANES])
    turned = jnp.transpose(tile)
    line = jnp.where(high_side, turned[LANES - 1 :], turned[:1])
    return jnp.concatenate([line, jnp.zeros((1, LANES - members), F32)], axis=1)


def finish_edges(high_rows, low_rows, partial_ref, column, high_side, oy, ox):
    members = high_rows.shape[0]
    x_cells = ox.shape[0]
    found = pick(jnp.concatenate([high_rows, low_rows], axis=0), oy)
    margin = partial_ref[...] + found[:members] * ox[x_cells - 1 :] + found[members:] * ox[:1]
    row = lax.broadcasted_iota(jnp.int32, column.shape, 0)
    column = jnp.where(row == x_cells - 1, border_row(high_rows, high_side), column)
    return margin, jnp.where(row == 0, border_row(low_rows, high_side), column)


def send_network(vf, sr, table, ghost_table, diff_ref, refs):
    half = vf.shape[0]
    rows = sr.shape[1]
    found = pick(vf, table)
    diff_ref[...] = found[:, :rows]
    sums = pick(sr * found[:, :rows], ghost_table, True)
    for ref, at in refs:
        ref[at : at + half, :] = found[:, rows:]
        ref[at + half : at + 2 * half, :] = sums


def send_core(core_ref, vf, margin, weight, ofrac, column, j, work_ref, wown_ref):
    half, frac_cells = vf.shape
    work_ref[...] = pick(margin * weight, ofrac, True)
    wown_ref[...] = work_ref[pl.ds(pl.multiple_of(j * half, half), half), :]
    other = work_ref[pl.ds(pl.multiple_of((1 - j) * half, half), half), :]
    size = frac_cells // LANES * half
    core_ref[0:size, :] = to_blocks(vf)
    core_ref[size : 2 * size, :] = to_blocks(other)
    core_ref[2 * size : 2 * size + column.shape[0], :] = column


def inside_kernel(
    place_ref,
    coef_ref,
    source_ref,
    local_ref,
    other_ref,
    frac_ref,
    oslot_ref,
    oy_ref,
    ox_ref,
    first_ref,
    second_ref,
    table_ref,
    ghost_table_ref,
    ofrac_ref,
    v_ref,
    margin_ref,
    column_ref,
):
    members, x_cells, y_cells = source_ref.shape
    frac_cells = table_ref.shape[0]
    rows = local_ref.shape[1]
    other = other_ref[...]
    first, second = one_hot(local_ref[...], frac_cells), one_hot(other, frac_cells)
    first_ref[...] = first
    second_ref[...] = second
    table_ref[:, :rows] = first - second
    table_ref[:, rows:] = oslot_ref[...]
    ghost_table_ref[...] = one_hot(other - frac_cells, ghost_table_ref.shape[0])
    ofrac_ref[...] = one_hot(frac_ref[...], frac_cells)

    high_side = place_ref[2] == 0
    inverse = 1.0 / coef_ref[4]
    row_x = lax.broadcasted_iota(jnp.int32, ox_ref.shape, 0)
    inner_x = jnp.where((row_x == 0) | (row_x == x_cells - 1), 0.0, ox_ref[...])
    lane_c = lax.broadcasted_iota(jnp.int32, (x_cells, LANES), 1)
    column_ref[...] = jnp.zeros_like(column_ref)

    @pl.loop(0, members // GROUP)
    def _(index):
        start = index * GROUP
        block = source_ref[pl.ds(start, GROUP)] * inverse[None]
        v_ref[pl.ds(start, GROUP)] = block
        found = pick(block.reshape(GROUP * x_cells, y_cells), oy_ref[...])
        margin_ref[pl.ds(start, GROUP), :] = margin_values(found, inner_x)
        column = column_ref[...]
        for k in range(GROUP):
            m = start + k
            moved = border_column(block[k, :, :LANES], block[k, :, y_cells - LANES :], high_side, m)
            column = jnp.where(lane_c == m, moved, column)
        column_ref[...] = column


def first_kernel(
    place_ref,
    count_ref,
    coef_ref,
    cond_ref,
    source_ref,
    source_f_ref,
    weight_ref,
    near_a_ref,
    near_b_ref,
    far_c_ref,
    far_d_ref,
    first_ref,
    second_ref,
    table_ref,
    ghost_table_ref,
    ofrac_ref,
    oy_ref,
    ox_ref,
    inner_margin_ref,
    inner_column_ref,
    v_in_ref,
    unit_ref,
    vf_ref,
    halo_ref,
    sr_ref,
    scale_f_ref,
    diff_ref,
    wown_ref,
    sent_ref,
    core_ref,
    v_ref,
    work_ref,
):
    members, x_cells, y_cells = source_ref.shape
    half, frac_cells = source_f_ref.shape
    blocks = y_cells // LANES
    j = place_ref[2]
    high_side = j == 0
    base = blocks * members
    plus1, minus1, plus2, minus2 = neighbours(place_ref, near_a_ref, near_b_ref, far_c_ref, far_d_ref)

    slot_at = base + 2 * blocks
    ghosts = by_group(minus1(slot_at, half), plus1(slot_at, half), minus2(0, half), plus2(0, half))
    table, ghost_table = table_ref[...], ghost_table_ref[...]
    cond = cond_ref[...]
    cond_first = pick(cond, first_ref[...])
    cond_second = pick(cond, second_ref[...]) + pick(ghosts, ghost_table)
    lane = lax.broadcasted_iota(jnp.int32, cond_first.shape, 1)
    live = jnp.zeros(cond_first.shape, jnp.bool_)
    for block in range(cond_first.shape[1] // LANES):
        start = block * LANES
        live = live | ((lane >= start) & (lane < start + count_ref[block]))
    sr = jnp.where(live, harmonic(cond_first, cond_second), 0.0)
    sr_ref[...] = sr
    diag_f = FRACTURE_STORAGE + pick(sr, first_ref[...], True)
    inverse_f = 1.0 / diag_f
    scale_f_ref[0] = inverse_f
    scale_f_ref[1] = diag_f
    vf = source_f_ref[...] * inverse_f
    vf_ref[...] = vf
    send_network(vf, sr, table, ghost_table, diff_ref, [(sent_ref, 0)])
    sent_ref[2 * half : 3 * half, :] = pick(sr, ghost_table, True)

    perm, part = coef_ref[5], coef_ref[4]
    row = lax.broadcasted_iota(jnp.int32, perm.shape, 0)
    perm_plus = from_blocks(plus1(base, blocks), 1)
    perm_minus = from_blocks(minus1(base, blocks), 1)
    part_plus = from_blocks(plus1(base + blocks, blocks), 1)
    part_minus = from_blocks(minus1(base + blocks, blocks), 1)
    te_edge = jnp.where(place_ref[4] == 1, 0.0, harmonic(perm[x_cells - 1 :], perm_plus))
    tw_edge = jnp.where(place_ref[3] == 1, 0.0, harmonic(perm[:1], perm_minus))
    te = jnp.where(row == x_cells - 1, te_edge, coef_ref[0])
    tw = jnp.where(row == 0, tw_edge, coef_ref[1])
    diag = part + jnp.where(row == x_cells - 1, te_edge, 0.0) + jnp.where(row == 0, tw_edge, 0.0)
    inverse = 1.0 / diag
    unit_ref[0] = te * inverse
    unit_ref[1] = tw * inverse
    unit_ref[2] = coef_ref[2] * inverse
    unit_ref[3] = coef_ref[3] * inverse
    unit_ref[4] = inverse
    unit_ref[5] = diag
    halo_ref[0] = plus1(0, base) * spread(1.0 / (part_plus + te_edge), members)
    halo_ref[1] = minus1(0, base) * spread(1.0 / (part_minus + tw_edge), members)
    high_rows = source_ref[:, x_cells - 1, :] * inverse[x_cells - 1 :]
    low_rows = source_ref[:, 0, :] * inverse[:1]
    v_ref[:, x_cells - 1, :] = high_rows
    v_ref[:, 0, :] = low_rows
    margin, column = finish_edges(
        high_rows, low_rows, inner_margin_ref, inner_column_ref[...], high_side, oy_ref[...], ox_ref[...]
    )
    weight = weight_ref[...]
    send_core(core_ref, vf, margin, weight, ofrac_ref[...], column, j, work_ref, wown_ref)
    wsum = pick(jnp.broadcast_to(weight, (8, weight.shape[1])), ofrac_ref[...], True)
    tail = core_ref.shape[0] - 8 * (frac_cells // LANES)
    core_ref[tail:, :] = to_blocks(wsum)


def interior_kernel(
    power,
    place_ref,
    v_ref,
    before_ref,
    vf_ref,
    before_f_ref,
    core_ref,
    scale_f_ref,
    unit_ref,
    weight_ref,
    ofrac_ref,
    oy_ref,
    ox_ref,
    *refs,
):
    if power < 3:
        image_ref, margin_ref, column_ref, dots_ref, flow_ref, work_ref, *acc_refs = refs
    else:
        dots_ref, flow_ref, work_ref, *acc_refs = refs
    members, x_cells, y_cells = v_ref.shape
    half, frac_cells = vf_ref.shape
    blocks = y_cells // LANES
    j = place_ref[2]
    high_side = j == 0
    size = frac_cells // LANES * half
    theirs = from_blocks(core_ref[0:size, :], half)
    column_in = core_ref[2 * size : 2 * size + x_cells, :]
    vf = vf_ref[...]
    own_rows = pl.ds(pl.multiple_of(j * half, half), half)
    work_ref[own_rows, :] = vf
    work_ref[pl.ds(pl.multiple_of((1 - j) * half, half), half), :] = theirs
    flow_ref[...] = pick(work_ref[...], ofrac_ref[...]) * weight_ref[...]

    heavy_f = vf * scale_f_ref[1]
    for ref in acc_refs:
        ref[...] = jnp.zeros_like(ref)
    acc_refs[0][own_rows, :] = fold_lanes(vf * heavy_f)
    if power > 1:
        acc_refs[1][own_rows, :] = fold_lanes(before_f_ref[...] * heavy_f)

    lane_c = lax.broadcasted_iota(jnp.int32, (x_cells, LANES), 1)
    lane = lax.broadcasted_iota(jnp.int32, (x_cells, y_cells), 1)
    row = lax.broadcasted_iota(jnp.int32, (x_cells, y_cells), 0)
    row_x = lax.broadcasted_iota(jnp.int32, ox_ref.shape, 0)
    oy, ox = oy_ref[...], ox_ref[...]
    inner_x = jnp.where((row_x == 0) | (row_x == x_cells - 1), 0.0, ox)
    te = jnp.where(row == x_cells - 1, 0.0, unit_ref[0])
    tw = jnp.where(row == 0, 0.0, unit_ref[1])
    if power < 3:
        column_ref[...] = jnp.zeros_like(column_ref)

    @pl.loop(0, members // GROUP)
    def _(index):
        start = index * GROUP
        parts = []
        for k in range(GROUP):
            parts.append(ox * flow_ref[pl.ds(start + k, 1), :])
        coupled = pick(jnp.concatenate(parts, axis=0), oy, True)
        if power < 3:
            column = column_ref[...]
        for k in range(GROUP):
            m = start + k
            value = v_ref[m]
            east = pltpu.roll(value, x_cells - 1, 0)
            west = pltpu.roll(value, 1, 0)
            moved = pltpu.roll(column_in, jnp.where(high_side, LANES - 1 - m, lax.rem(LANES - m, LANES)), 1)
            moved = jnp.concatenate([moved] * blocks, axis=1)
            north = jnp.where(lane == y_cells - 1, moved, pltpu.roll(value, y_cells - 1, 1))
            south = jnp.where(lane == 0, moved, pltpu.roll(value, 1, 1))
            image = value - te * east - tw * west - unit_ref[2] * north - unit_ref[3] * south
            image = image - coupled[k * x_cells : (k + 1) * x_cells] * unit_ref[4]
            heavy = value * unit_ref[5]
            at = pl.ds(m, 1)
            acc_refs[0][at, :] += jnp.sum(fold_lanes(value * heavy), axis=0, keepdims=True)
            if power > 1:
                acc_refs[1][at, :] += jnp.sum(fold_lanes(before_ref[m] * heavy), axis=0, keepdims=True)
            if power < 3:
                image_ref[m] = image
                shifted = border_column(image[:, :LANES], image[:, y_cells - LANES :], high_side, m)
                column = jnp.where(lane_c == m, shifted, column)
            else:
                acc_refs[2][at, :] += jnp.sum(fold_lanes(image * heavy), axis=0, keepdims=True)
        if power < 3:
            column_ref[...] = column
            block = image_ref[pl.ds(start, GROUP)]
            found = pick(block.reshape(GROUP * x_cells, y_cells), oy)
            margin_ref[pl.ds(start, GROUP), :] = margin_values(found, inner_x)

    dots = [total_rows(ref[...]) for ref in acc_refs]
    dots.append(jnp.zeros((8 - len(dots), members), F32))
    dots_ref[...] = jnp.concatenate(dots, axis=0)


def finish_kernel(
    power,
    place_ref,
    vf_ref,
    near_a_ref,
    near_b_ref,
    far_c_ref,
    far_d_ref,
    core_in_ref,
    diff_in_ref,
    wown_in_ref,
    sr_ref,
    scale_f_ref,
    unit_ref,
    table_ref,
    ghost_table_ref,
    *refs,
):
    if power == 1:
        (
            halo_ref,
            weight_ref,
            ofrac_ref,
            oy_ref,
            ox_ref,
            inner_margin_ref,
            inner_column_ref,
            image_in_ref,
            own_f_ref,
            *refs,
        ) = refs
    elif power == 2:
        (
            own_f_in_ref,
            weight_ref,
            ofrac_ref,
            oy_ref,
            ox_ref,
            inner_margin_ref,
            inner_column_ref,
            image_in_ref,
            *refs,
        ) = refs
    if power < 3:
        out_f_ref, diff_ref, wown_ref, up_ref, down_ref, sent_ref, core_ref, image_ref, work_ref = refs
    else:
        own_f_in_ref, v_ref, dots1_ref, dots2_ref, dots3_ref, moments_ref, acc_ref = refs
    half, frac_cells = vf_ref.shape
    x_cells, y_cells = unit_ref.shape[1:]
    members = (near_a_ref.shape[0] - 2 * half) // (y_cells // LANES) if power > 1 else image_ref.shape[0]
    blocks = y_cells // LANES
    frac_blocks = frac_cells // LANES
    j = place_ref[2]
    high_side = j == 0
    base = 0 if power == 1 else blocks * members
    plus1, minus1, plus2, minus2 = neighbours(place_ref, near_a_ref, near_b_ref, far_c_ref, far_d_ref)
    rows = sr_ref.shape[1]

    table, ghost_table = table_ref[...], ghost_table_ref[...]
    vf = vf_ref[...]
    ghosts = by_group(minus1(base, half), plus1(base, half), minus2(0, half), plus2(0, half))
    sums = by_group(
        plus1(base + half, half), minus1(base + half, half), plus2(half, half), minus2(half, half)
    )
    size = frac_blocks * half
    their_sums = from_blocks(core_in_ref[size : 2 * size, :], half)
    if power == 1:
        at = 2 * half
        back = by_group(
            plus1(base + at, half), minus1(base + at, half), plus2(at, half), minus2(at, half)
        )
        weight = weight_ref[...]
        wsum = pick(jnp.broadcast_to(weight, (8, weight.shape[1])), ofrac_ref[...], True)
        tail = core_in_ref.shape[0] - 8 * frac_blocks
        wsum = wsum + from_blocks(core_in_ref[tail:, :], 8)
        own_f = FRACTURE_STORAGE + wsum[:1] + pick(back, table[:, rows:], True)
        own_f_ref[...] = own_f
    else:
        own_f = own_f_in_ref[...]
    sr = sr_ref[...]
    flux = sr * (diff_in_ref[...] - pick(ghosts, ghost_table))
    image_f = own_f * vf + pick(jnp.concatenate([flux, -sums], axis=1), table, True)
    image_f = image_f - wown_in_ref[...] - their_sums

    if power == 3:
        acc_ref[...] = jnp.zeros_like(acc_ref)
        acc_ref[pl.ds(pl.multiple_of(j * half, half), half), :] = fold_lanes(vf * image_f)
        for side, at, reader in ((0, x_cells - 1, plus1), (1, 0, minus1)):
            factor = unit_ref[side, at : at + 1, :] * unit_ref[5, at : at + 1, :]
            edge = v_ref[:, at, :] * factor
            for q in range(blocks):
                beyond = reader(q * members, members)
                acc_ref[...] -= edge[:, q * LANES : (q + 1) * LANES] * beyond
        last = total_rows(acc_ref[...]) + dots3_ref[2:3, :]
        gap = jnp.zeros((1, LANES - 3 * members), F32)
        lines = [
            jnp.concatenate([dots1_ref[0:1, :], dots2_ref[1:2, :], dots2_ref[0:1, :], gap], axis=1),
            jnp.concatenate([dots3_ref[1:2, :], dots3_ref[0:1, :], last, gap], axis=1),
        ]
        lines = jnp.concatenate(lines, axis=0)
        moments_ref[...] = jnp.broadcast_to(lines[None], moments_ref.shape)
        return

    next_f = image_f * scale_f_ref[0]
    out_f_ref[...] = next_f
    at = blocks * members
    send_network(next_f, sr, table, ghost_table, diff_ref, [(up_ref, at), (down_ref, at), (sent_ref, 0)])

    edges = []
    for side, at, reader, ref in ((0, x_cells - 1, plus1, up_ref), (1, 0, minus1, down_ref)):
        factor = unit_ref[side, at : at + 1, :]
        old = image_in_ref[:, at, :]
        pieces = []
        for q in range(blocks):
            beyond = halo_ref[side, q * members : (q + 1) * members, :] if power == 1 else reader(q * members, members)
            cut = slice(q * LANES, (q + 1) * LANES)
            piece = old[:, cut] - factor[:, cut] * beyond
            ref[q * members : (q + 1) * members, :] = piece
            pieces.append(piece)
        edge = jnp.concatenate(pieces, axis=1)
        image_ref[:, at, :] = edge
        edges.append(edge)
    margin, column = finish_edges(
        edges[0], edges[1], inner_margin_ref, inner_column_ref[...], high_side, oy_ref[...], ox_ref[...]
    )
    send_core(core_ref, next_f, margin, weight_ref[...], ofrac_ref[...], column, j, work_ref, wown_ref)


def close_kernel(place_ref, totals_ref, v0_ref, v1_ref, v2_ref, f0_ref, f1_ref, f2_ref, x_ref, xf_ref, c_ref):
    members, x_cells, y_cells = v0_ref.shape
    half, frac_cells = f0_ref.shape

    total = jnp.sum(totals_ref[...], axis=0)
    m0, m1, m2, m3, m4, m5 = (
        total[k // 3 : k // 3 + 1, k % 3 * members : k % 3 * members + members] for k in range(6)
    )
    alpha0 = m0 / m1
    rz1 = m0 - 2.0 * alpha0 * m1 + alpha0 * alpha0 * m2
    beta1 = rz1 / m0
    a, b = 1.0 + beta1, -alpha0
    pap1 = a * a * m1 + 2.0 * a * b * m2 + b * b * m3
    alpha1 = rz1 / pap1
    e = -alpha0 - alpha1 * a
    g = -alpha1 * b
    rz2 = m0 + 2.0 * e * m1 + (e * e + 2.0 * g) * m2 + 2.0 * e * g * m3 + g * g * m4
    beta2 = rz2 / rz1
    c = 1.0 + beta2 * a
    d = e + beta2 * b
    pap2 = c * c * m1 + 2.0 * c * d * m2 + (d * d + 2.0 * c * g) * m3 + 2.0 * d * g * m4 + g * g * m5
    alpha2 = rz2 / pap2
    c0 = alpha0 + alpha1 * a + alpha2 * c
    c1 = alpha1 * b + alpha2 * d
    c2 = alpha2 * g
    for k, row in enumerate((c0, c1, c2)):
        row = jnp.concatenate([row, jnp.zeros((1, LANES - members), F32)], axis=1)
        c_ref[k] = jnp.transpose(jnp.broadcast_to(row, (LANES, LANES)))
    j = place_ref[2]
    own = pl.ds(pl.multiple_of(j * half, half), half)

    def wide(k, rows, width):
        return jnp.concatenate([c_ref[k, rows, :]] * (width // LANES), axis=1)

    xf_ref[...] = (
        wide(0, own, frac_cells) * f0_ref[...]
        + wide(1, own, frac_cells) * f1_ref[...]
        + wide(2, own, frac_cells) * f2_ref[...]
    )

    @pl.loop(0, members)
    def _(m):
        rows = pl.ds(m, 1)
        x_ref[m] = (
            wide(0, rows, y_cells) * v0_ref[m]
            + wide(1, rows, y_cells) * v1_ref[m]
            + wide(2, rows, y_cells) * v2_ref[m]
        )


def pairs_of(count, stride, phase):
    out = []
    for index in range(count):
        if (index // stride) % 2 == phase:
            mate = (index + stride) % count
            out += [(index, mate), (mate, index)]
    return out


VMEM = pl.BlockSpec(memory_space=pltpu.VMEM)
SMEM = pl.BlockSpec(memory_space=pltpu.SMEM)


def call(kernel, name, args, outs, scratch=(), scalars=0, cost=None, aliases=None):
    return pl.pallas_call(
        kernel,
        name=name,
        out_shape=[jax.ShapeDtypeStruct(shape, dtype) for shape, dtype in outs],
        in_specs=[SMEM] * scalars + [VMEM] * (len(args) - scalars),
        out_specs=[VMEM] * len(outs),
        scratch_shapes=list(scratch),
        compiler_params=pltpu.CompilerParams(vmem_limit_bytes=40 * 1024 * 1024),
        cost_estimate=cost,
        input_output_aliases=aliases or {},
    )(*args)


def per_device(
    source_matrix,
    source_fracture,
    aperture,
    storage,
    perm_class,
    class_perm,
    send_slots,
    isect_local,
    isect_other,
    isect_count,
    ov_cell,
    ov_frac,
    ov_weight,
    ov_count,
):
    members, x_cells, y_cells = source_matrix.shape
    half, frac_cells = source_fracture.shape
    slots = send_slots.shape[1]
    rows = isect_local.size
    margin = ov_cell.size
    count = lax.axis_size("gx")
    i, j = lax.axis_index("gx"), lax.axis_index("gy")
    place = jnp.stack(
        [i % 2, (i // 2) % 2, j, (i == 0).astype(jnp.int32), (i == count - 1).astype(jnp.int32)]
    ).astype(jnp.int32)

    def near(up, down):
        even = i % 2 == 0
        to_a = jnp.where(even, up, down)
        to_b = jnp.where(even, down, up)
        return (
            lax.ppermute(to_a, "gx", pairs_of(count, 1, 0)),
            lax.ppermute(to_b, "gx", pairs_of(count, 1, 1)),
        )

    def far(value):
        return (
            lax.ppermute(value, "gx", pairs_of(count, 2, 0)),
            lax.ppermute(value, "gx", pairs_of(count, 2, 1)),
        )

    def core(value):
        return lax.ppermute(value, "gy", [(0, 1), (1, 0)])

    blocks = y_cells // LANES
    frac_blocks = frac_cells // LANES
    positions = jnp.arange(LANES, dtype=jnp.int32)
    ov_live = positions[None, :] < ov_count.reshape(-1, 1)
    weight = jnp.where(ov_live, ov_weight.reshape(ov_live.shape), 0.0).reshape(1, margin)
    col = core(jnp.where(j == 0, perm_class[:, y_cells - 1 :], perm_class[:, :1]))
    near_rows = blocks * members + 2 * blocks + half
    coef, oy, ox, oslot, cond, up, down, supplied = call(
        opening_kernel,
        "opening",
        (
            place,
            class_perm,
            perm_class,
            col,
            storage,
            source_matrix,
            aperture,
            send_slots,
            ov_cell.reshape(1, margin),
            weight,
        ),
        [
            ((6, x_cells, y_cells), F32),
            ((y_cells, margin), BF16),
            ((x_cells, margin), F32),
            ((frac_cells, slots), BF16),
            ((half, frac_cells), F32),
            ((near_rows, LANES), F32),
            ((near_rows, LANES), F32),
            ((half, slots), F32),
        ],
        scalars=2,
    )
    field = (members, x_cells, y_cells)
    own = (half, frac_cells)
    hidden = pl.CostEstimate(flops=4_000_000_000, bytes_accessed=12_000_000, transcendentals=0)
    near_a, near_b = near(up, down)
    far_c, far_d = far(supplied)
    first, second, table, ghost_table, ofrac, v0, margin_in, column = call(
        inside_kernel,
        "inside",
        (
            place,
            coef,
            source_matrix,
            isect_local.reshape(1, rows),
            isect_other.reshape(1, rows),
            ov_frac.reshape(1, margin),
            oslot,
            oy,
            ox,
        ),
        [
            ((frac_cells, rows), BF16),
            ((frac_cells, rows), BF16),
            ((frac_cells, rows + slots), BF16),
            ((slots, rows), BF16),
            ((frac_cells, margin), BF16),
            (field, F32),
            ((members, margin), F32),
            ((x_cells, LANES), F32),
        ],
        scalars=1,
        cost=hidden,
    )
    core_rows = 2 * frac_blocks * half + x_cells
    edge_rows = blocks * members
    unit, f0, halo, sr, scale_f, diff, wown, sent, core_msg, v0 = call(
        first_kernel,
        "first_vector",
        (
            place,
            isect_count,
            coef,
            cond,
            source_matrix,
            source_fracture,
            weight,
            near_a,
            near_b,
            far_c,
            far_d,
            first,
            second,
            table,
            ghost_table,
            ofrac,
            oy,
            ox,
            margin_in,
            column,
            v0,
        ),
        [
            ((6, x_cells, y_cells), F32),
            (own, F32),
            ((2, edge_rows, LANES), F32),
            ((half, rows), F32),
            ((2, half, frac_cells), F32),
            ((half, rows), F32),
            (own, F32),
            ((3 * half, LANES), F32),
            ((core_rows + 8 * frac_blocks, LANES), F32),
            (field, F32),
        ],
        scratch=[pltpu.VMEM((members, frac_cells), F32)],
        scalars=2,
        aliases={20: 9},
    )
    near_rows = edge_rows + 2 * half

    def interior(power, v, before, vf, before_f, core_in):
        outs = []
        if power < 3:
            outs = [(field, F32), ((members, margin), F32), ((x_cells, LANES), F32)]
        return call(
            functools.partial(interior_kernel, power),
            f"interior_{power}",
            (place, v, before, vf, before_f, core_in, scale_f, unit, weight, ofrac, oy, ox),
            outs + [((8, members), F32)],
            scratch=[pltpu.VMEM((members, margin), F32), pltpu.VMEM((members, frac_cells), F32)]
            + [pltpu.VMEM((members, LANES), F32)] * power,
            scalars=1,
            cost=hidden,
        )

    finish_outs = [
        (own, F32),
        ((half, rows), F32),
        (own, F32),
        ((near_rows, LANES), F32),
        ((near_rows, LANES), F32),
        ((2 * half, LANES), F32),
        ((core_rows, LANES), F32),
        (field, F32),
    ]
    finish_scratch = [pltpu.VMEM((members, frac_cells), F32)]

    near_a, near_b = near(sent, sent)
    far_c, far_d = far(sent)
    core_in = core(core_msg)
    image, margin_in, column, dots1 = interior(1, v0, halo, f0, f0, core_in)
    own_f, f1, diff, wown, up, down, sent, core_msg, v1 = call(
        functools.partial(finish_kernel, 1),
        "finish_1",
        (place, f0, near_a, near_b, far_c, far_d, core_in, diff, wown, sr, scale_f, unit, table, ghost_table)
        + (halo, weight, ofrac, oy, ox, margin_in, column, image),
        [(own, F32)] + finish_outs,
        scratch=finish_scratch,
        scalars=1,
        aliases={21: 8},
    )
    near_a, near_b = near(up, down)
    far_c, far_d = far(sent)
    core_in = core(core_msg)
    image, margin_in, column, dots2 = interior(2, v1, v0, f1, f0, core_in)
    f2, diff, wown, up, down, sent, core_msg, v2 = call(
        functools.partial(finish_kernel, 2),
        "finish_2",
        (place, f1, near_a, near_b, far_c, far_d, core_in, diff, wown, sr, scale_f, unit, table, ghost_table)
        + (own_f, weight, ofrac, oy, ox, margin_in, column, image),
        finish_outs,
        scratch=finish_scratch,
        scalars=1,
        aliases={21: 7},
    )
    near_a, near_b = near(up, down)
    far_c, far_d = far(sent)
    core_in = core(core_msg)
    (dots3,) = interior(3, v2, v1, f2, f1, core_in)
    peers = count * lax.axis_size("gy")
    (moments,) = call(
        functools.partial(finish_kernel, 3),
        "finish_3",
        (place, f2, near_a, near_b, far_c, far_d, core_in, diff, wown, sr, scale_f, unit, table, ghost_table)
        + (own_f, v2, dots1, dots2, dots3),
        [((peers, 2, LANES), F32)],
        scratch=[pltpu.VMEM((members, LANES), F32)],
        scalars=1,
    )
    totals = lax.all_to_all(moments, ("gx", "gy"), 0, 0)
    return call(
        close_kernel,
        "iterate",
        (place, totals, v0, v1, v2, f0, f1, f2),
        [(field, F32), (own, F32)],
        scratch=[pltpu.VMEM((3, LANES, LANES), F32)],
        scalars=1,
    )


def solution(mesh):
    placed = (
        P("grp", "gx", "gy"),
        P(("grp", "gy"), "gx"),
        P(("grp", "gy"), "gx"),
        P("gx", "gy"),
        P("gx", "gy"),
        P(),
        P("gx", None),
        P("gx", None),
        P("gx", None),
        P("gx"),
        P("gx", "gy", None, None),
        P("gx", "gy", None, None),
        P("gx", "gy", None, None),
        P("gx", "gy", None),
    )
    return jax.shard_map(
        per_device,
        mesh=mesh,
        in_specs=placed,
        out_specs=(P("grp", "gx", "gy"), P(("grp", "gy"), "gx")),
        check_vma=False,
    )
```

```python
import functools

import jax
import jax.numpy as jnp
from jax import lax
from jax.experimental import pallas as pl
from jax.experimental.pallas import tpu as pltpu
from jax.sharding import PartitionSpec as P

FRACTURE_STORAGE = 0.1
F32 = jnp.float32
BF16 = jnp.bfloat16
LANES = 128
GROUP = 16


def split3(x):
    high = x.astype(BF16)
    rest = x - high.astype(F32)
    mid = rest.astype(BF16)
    low = (rest - mid.astype(F32)).astype(BF16)
    return jnp.concatenate([high, mid, low], axis=0)


def pick(x, table, transposed=False):
    rows = x.shape[0]
    dims = (((1,), (1 if transposed else 0,)), ((), ()))
    out = lax.dot_general(split3(x), table, dims, preferred_element_type=F32)
    return out[:rows] + out[rows : 2 * rows] + out[2 * rows :]


class Place:
    def __init__(self):
        count = lax.axis_size("gx")
        i = lax.axis_index("gx")
        self.j = lax.axis_index("gy")
        self.high_side = self.j == 0
        self.even = lax.rem(i, 2) == 0
        self.low_pair = lax.rem(lax.div(i, 2), 2) == 0
        self.first = i == 0
        self.last = i == count - 1


def harmonic(first_perm, second_perm):
    return 2.0 * first_perm * second_perm / (first_perm + second_perm)


def one_hot(index_row, size):
    shape = (size, index_row.shape[1])
    ids = lax.broadcasted_iota(jnp.int32, shape, 0)
    return jnp.where(ids == index_row, 1.0, 0.0).astype(BF16)


def to_blocks(x):
    return jnp.concatenate(
        [x[:, q : q + LANES] for q in range(0, x.shape[1], LANES)], axis=0
    )


def from_blocks(x, rows):
    return jnp.concatenate(
        [x[q : q + rows] for q in range(0, x.shape[0], rows)], axis=1
    )


def by_group(first, second, third, fourth):
    group = first.shape[1] // 4
    lane = lax.broadcasted_iota(jnp.int32, first.shape, 1)
    return jnp.where(
        lane < group,
        first,
        jnp.where(lane < 2 * group, second, jnp.where(lane < 3 * group, third, fourth)),
    )


def total_rows(x):
    return jnp.sum(jnp.transpose(x), axis=0, keepdims=True)


def fold_lanes(x):
    rows, width = x.shape
    out = x[:, :LANES]
    for q in range(LANES, width, LANES):
        out = out + x[:, q : q + LANES]
    return out


def opening_kernel(
    perm_table_ref,
    class_ref,
    aperture_ref,
    slots_ref,
    perm_ref,
    cond_ref,
    oslot_ref,
    near_a_ref,
    near_b_ref,
    far_ref,
    border_ref,
):
    x_cells, y_cells = class_ref.shape
    half = aperture_ref.shape[0]
    here = Place()
    classes = class_ref[...]
    perm = jnp.zeros(classes.shape, F32)
    for index in range(perm_table_ref.shape[0]):
        perm = jnp.where(classes == index, perm_table_ref[index], perm)
    perm_ref[...] = perm
    border_ref[...] = jnp.where(here.high_side, perm[:, y_cells - LANES :], perm[:, :LANES])

    aperture = aperture_ref[...]
    cond = aperture * aperture * aperture
    cond_ref[...] = cond
    oslot = one_hot(slots_ref[...], cond.shape[1])
    oslot_ref[...] = oslot
    supplied = pick(cond, oslot)
    far_ref[...] = supplied
    up, down = to_blocks(perm[x_cells - 1 :]), to_blocks(perm[:1])
    blocks = up.shape[0]
    pad = jnp.zeros((near_a_ref.shape[0] - half - blocks, LANES), F32)
    for ref, edge in ((near_a_ref, jnp.where(here.even, up, down)), (near_b_ref, jnp.where(here.even, down, up))):
        ref[...] = jnp.concatenate([supplied, edge, pad], axis=0)


def neighbours(here, near_a_ref, near_b_ref, far_c_ref, far_d_ref):
    def reader(flag, at_zero, at_one):
        return lambda at, size: jnp.where(
            flag, at_zero[at : at + size, :], at_one[at : at + size, :]
        )

    return (
        reader(here.even, near_a_ref, near_b_ref),
        reader(here.even, near_b_ref, near_a_ref),
        reader(here.low_pair, far_c_ref, far_d_ref),
        reader(here.low_pair, far_d_ref, far_c_ref),
    )


def margin_values(found, ox):
    found = found.reshape(-1, *ox.shape) * ox[None]
    return jnp.sum(found, axis=1)


def border_column(tile_low, tile_high, high_side, m):
    tile = jnp.where(high_side, tile_high, tile_low)
    return pltpu.roll(tile, jnp.where(high_side, lax.rem(m + 1, LANES), m), 1)


def border_row(row_values, high_side):
    members, y_cells = row_values.shape
    tile = jnp.where(high_side, row_values[:, y_cells - LANES :], row_values[:, :LANES])
    turned = jnp.transpose(tile)
    line = jnp.where(high_side, turned[LANES - 1 :], turned[:1])
    return jnp.concatenate([line, jnp.zeros((1, LANES - members), F32)], axis=1)


def finish_edges(high_rows, low_rows, partial_ref, column, high_side, oy, ox):
    members = high_rows.shape[0]
    x_cells = ox.shape[0]
    found = pick(jnp.concatenate([high_rows, low_rows], axis=0), oy)
    margin = partial_ref[...] + found[:members] * ox[x_cells - 1 :] + found[members:] * ox[:1]
    row = lax.broadcasted_iota(jnp.int32, column.shape, 0)
    column = jnp.where(row == x_cells - 1, border_row(high_rows, high_side), column)
    return margin, jnp.where(row == 0, border_row(low_rows, high_side), column)


def send_network(vf, sr, table, ghost_table, diff_ref, refs):
    half = vf.shape[0]
    rows = sr.shape[1]
    found = pick(vf, table)
    diff_ref[...] = found[:, :rows]
    sums = pick(sr * found[:, :rows], ghost_table, True)
    for ref, at in refs:
        ref[at : at + half, :] = found[:, rows:]
        ref[at + half : at + 2 * half, :] = sums


def send_core(core_ref, vf, margin, weight, ofrac, column, j, work_ref, wown_ref):
    half, frac_cells = vf.shape
    work_ref[...] = pick(margin * weight, ofrac, True)
    wown_ref[...] = work_ref[pl.ds(pl.multiple_of(j * half, half), half), :]
    other = work_ref[pl.ds(pl.multiple_of((1 - j) * half, half), half), :]
    size = frac_cells // LANES * half
    core_ref[0:size, :] = to_blocks(vf)
    core_ref[size : 2 * size, :] = to_blocks(other)
    core_ref[2 * size : 2 * size + column.shape[0], :] = column


def inside_kernel(
    ov_count_ref,
    perm_ref,
    border_ref,
    storage_ref,
    source_ref,
    cell_ref,
    ov_weight_ref,
    local_ref,
    other_in_ref,
    frac_ref,
    oslot_ref,
    coef_ref,
    oy_ref,
    ox_ref,
    weight_ref,
    first_ref,
    second_ref,
    table_ref,
    ghost_table_ref,
    ofrac_ref,
    v_ref,
    margin_ref,
    column_ref,
):
    members, x_cells, y_cells = source_ref.shape
    frac_cells = table_ref.shape[0]
    here = Place()
    high_side = here.high_side

    def line(ref):
        return jnp.concatenate([ref[k : k + 1, :] for k in range(ref.shape[0])], axis=1)

    rows = local_ref.size
    perm, border = perm_ref[...], border_ref[...]
    col = jnp.where(high_side, border[:, :1], border[:, LANES - 1 :])
    lane = lax.broadcasted_iota(jnp.int32, perm.shape, 1)
    row = lax.broadcasted_iota(jnp.int32, perm.shape, 0)
    north = jnp.concatenate([perm[:, 1:], col], axis=1)
    south = jnp.concatenate([col, perm[:, :-1]], axis=1)
    tn = jnp.where((lane == y_cells - 1) & jnp.logical_not(high_side), 0.0, harmonic(perm, north))
    ts = jnp.where((lane == 0) & high_side, 0.0, harmonic(perm, south))
    east = jnp.concatenate([perm[1:], perm[:1]], axis=0)
    west = jnp.concatenate([perm[-1:], perm[:-1]], axis=0)
    te = jnp.where(row == x_cells - 1, 0.0, harmonic(perm, east))
    tw = jnp.where(row == 0, 0.0, harmonic(perm, west))
    cell = line(cell_ref)
    oy = one_hot(cell % y_cells, y_cells)
    oy_ref[...] = oy
    row_x = lax.broadcasted_iota(jnp.int32, ox_ref.shape, 0)
    at_x = row_x == cell // y_cells
    ox = jnp.where(at_x, 1.0, 0.0)
    ox_ref[...] = ox
    lane_w = lax.broadcasted_iota(jnp.int32, (1, LANES), 1)
    weight = jnp.concatenate(
        [jnp.where(lane_w < ov_count_ref[k], ov_weight_ref[k : k + 1, :], 0.0) for k in range(ov_weight_ref.shape[0])],
        axis=1,
    )
    weight_ref[...] = weight
    part = storage_ref[...] + te + tw + tn + ts + pick(jnp.where(at_x, weight, 0.0), oy, True)
    coef_ref[0] = te
    coef_ref[1] = tw
    coef_ref[2] = tn
    coef_ref[3] = ts
    coef_ref[4] = part

    other = line(other_in_ref)
    first, second = one_hot(line(local_ref), frac_cells), one_hot(other, frac_cells)
    first_ref[...] = first
    second_ref[...] = second
    table_ref[:, :rows] = first - second
    table_ref[:, rows:] = oslot_ref[...]
    ghost_table_ref[...] = one_hot(other - frac_cells, ghost_table_ref.shape[0])
    ofrac_ref[...] = one_hot(line(frac_ref), frac_cells)

    inverse = 1.0 / part
    inner_x = jnp.where((row_x == 0) | (row_x == x_cells - 1), 0.0, ox)
    lane_c = lax.broadcasted_iota(jnp.int32, (x_cells, LANES), 1)
    column_ref[...] = jnp.zeros_like(column_ref)

    @pl.loop(0, members // GROUP)
    def _(index):
        start = index * GROUP
        block = source_ref[pl.ds(start, GROUP)] * inverse[None]
        v_ref[pl.ds(start, GROUP)] = block
        found = pick(block.reshape(GROUP * x_cells, y_cells), oy_ref[...])
        margin_ref[pl.ds(start, GROUP), :] = margin_values(found, inner_x)
        column = column_ref[...]
        for k in range(GROUP):
            m = start + k
            moved = border_column(block[k, :, :LANES], block[k, :, y_cells - LANES :], high_side, m)
            column = jnp.where(lane_c == m, moved, column)
        column_ref[...] = column


def first_kernel(
    count_ref,
    coef_ref,
    perm_ref,
    cond_ref,
    source_ref,
    source_f_ref,
    weight_ref,
    near_a_ref,
    near_b_ref,
    far_c_ref,
    far_d_ref,
    first_ref,
    second_ref,
    table_ref,
    ghost_table_ref,
    ofrac_ref,
    oy_ref,
    ox_ref,
    inner_margin_ref,
    inner_column_ref,
    v_in_ref,
    unit_ref,
    vf_ref,
    sr_ref,
    scale_f_ref,
    diff_ref,
    wown_ref,
    to_a_ref,
    to_b_ref,
    sent_ref,
    core_ref,
    v_ref,
    work_ref,
):
    members, x_cells, y_cells = source_ref.shape
    half, frac_cells = source_f_ref.shape
    blocks = y_cells // LANES
    here = Place()
    j, high_side = here.j, here.high_side
    base = blocks * members
    plus1, minus1, plus2, minus2 = neighbours(here, near_a_ref, near_b_ref, far_c_ref, far_d_ref)

    ghosts = by_group(minus1(0, half), plus1(0, half), minus2(0, half), plus2(0, half))
    table, ghost_table = table_ref[...], ghost_table_ref[...]
    cond = cond_ref[...]
    cond_first = pick(cond, first_ref[...])
    cond_second = pick(cond, second_ref[...]) + pick(ghosts, ghost_table)
    lane = lax.broadcasted_iota(jnp.int32, cond_first.shape, 1)
    live = jnp.zeros(cond_first.shape, jnp.bool_)
    for block in range(cond_first.shape[1] // LANES):
        start = block * LANES
        live = live | ((lane >= start) & (lane < start + count_ref[block]))
    sr = jnp.where(live, harmonic(cond_first, cond_second), 0.0)
    sr_ref[...] = sr
    diag_f = FRACTURE_STORAGE + pick(sr, first_ref[...], True)
    inverse_f = 1.0 / diag_f
    scale_f_ref[0] = inverse_f
    scale_f_ref[1] = diag_f
    vf = source_f_ref[...] * inverse_f
    vf_ref[...] = vf
    refs = [(to_a_ref, base), (to_b_ref, base), (sent_ref, 0)]
    send_network(vf, sr, table, ghost_table, diff_ref, refs)
    slot_sums = pick(sr, ghost_table, True)
    for ref, at in refs:
        ref[at + 2 * half : at + 3 * half, :] = slot_sums

    perm, part = perm_ref[...], coef_ref[4]
    row = lax.broadcasted_iota(jnp.int32, perm.shape, 0)
    perm_plus = from_blocks(plus1(half, blocks), 1)
    perm_minus = from_blocks(minus1(half, blocks), 1)
    te_edge = jnp.where(here.last, 0.0, harmonic(perm[x_cells - 1 :], perm_plus))
    tw_edge = jnp.where(here.first, 0.0, harmonic(perm[:1], perm_minus))
    te = jnp.where(row == x_cells - 1, te_edge, coef_ref[0])
    tw = jnp.where(row == 0, tw_edge, coef_ref[1])
    diag = part + jnp.where(row == x_cells - 1, te_edge, 0.0) + jnp.where(row == 0, tw_edge, 0.0)
    inverse = 1.0 / diag
    unit_ref[0] = te * inverse
    unit_ref[1] = tw * inverse
    unit_ref[2] = coef_ref[2] * inverse
    unit_ref[3] = coef_ref[3] * inverse
    unit_ref[4] = inverse
    unit_ref[5] = diag
    high_rows = source_ref[:, x_cells - 1, :] * inverse[x_cells - 1 :]
    low_rows = source_ref[:, 0, :] * inverse[:1]
    v_ref[:, x_cells - 1, :] = high_rows
    v_ref[:, 0, :] = low_rows
    to_a_ref[0:base, :] = to_blocks(jnp.where(here.even, high_rows, low_rows))
    to_b_ref[0:base, :] = to_blocks(jnp.where(here.even, low_rows, high_rows))
    margin, column = finish_edges(
        high_rows, low_rows, inner_margin_ref, inner_column_ref[...], high_side, oy_ref[...], ox_ref[...]
    )
    weight = weight_ref[...]
    send_core(core_ref, vf, margin, weight, ofrac_ref[...], column, j, work_ref, wown_ref)
    wsum = pick(jnp.broadcast_to(weight, (8, weight.shape[1])), ofrac_ref[...], True)
    tail = core_ref.shape[0] - 8 * (frac_cells // LANES)
    core_ref[tail:, :] = to_blocks(wsum)


def interior_kernel(
    power,
    v_ref,
    before_ref,
    vf_ref,
    before_f_ref,
    core_ref,
    scale_f_ref,
    unit_ref,
    weight_ref,
    ofrac_ref,
    oy_ref,
    ox_ref,
    *refs,
):
    if power < 3:
        image_ref, margin_ref, column_ref, dots_ref, flow_ref, work_ref, *acc_refs = refs
    else:
        dots_ref, flow_ref, work_ref, *acc_refs = refs
    members, x_cells, y_cells = v_ref.shape
    half, frac_cells = vf_ref.shape
    blocks = y_cells // LANES
    here = Place()
    j, high_side = here.j, here.high_side
    size = frac_cells // LANES * half
    theirs = from_blocks(core_ref[0:size, :], half)
    column_in = core_ref[2 * size : 2 * size + x_cells, :]
    vf = vf_ref[...]
    own_rows = pl.ds(pl.multiple_of(j * half, half), half)
    work_ref[own_rows, :] = vf
    work_ref[pl.ds(pl.multiple_of((1 - j) * half, half), half), :] = theirs
    flow_ref[...] = pick(work_ref[...], ofrac_ref[...]) * weight_ref[...]

    heavy_f = vf * scale_f_ref[1]
    for ref in acc_refs:
        ref[...] = jnp.zeros_like(ref)
    acc_refs[0][own_rows, :] = fold_lanes(vf * heavy_f)
    if power > 1:
        acc_refs[1][own_rows, :] = fold_lanes(before_f_ref[...] * heavy_f)

    lane_c = lax.broadcasted_iota(jnp.int32, (x_cells, LANES), 1)
    lane = lax.broadcasted_iota(jnp.int32, (x_cells, y_cells), 1)
    row = lax.broadcasted_iota(jnp.int32, (x_cells, y_cells), 0)
    row_x = lax.broadcasted_iota(jnp.int32, ox_ref.shape, 0)
    oy, ox = oy_ref[...], ox_ref[...]
    inner_x = jnp.where((row_x == 0) | (row_x == x_cells - 1), 0.0, ox)
    te = jnp.where(row == x_cells - 1, 0.0, unit_ref[0])
    tw = jnp.where(row == 0, 0.0, unit_ref[1])
    if power < 3:
        column_ref[...] = jnp.zeros_like(column_ref)

    @pl.loop(0, members // GROUP)
    def _(index):
        start = index * GROUP
        parts = []
        for k in range(GROUP):
            parts.append(ox * flow_ref[pl.ds(start + k, 1), :])
        coupled = pick(jnp.concatenate(parts, axis=0), oy, True)
        if power < 3:
            column = column_ref[...]
        for k in range(GROUP):
            m = start + k
            value = v_ref[m]
            east = pltpu.roll(value, x_cells - 1, 0)
            west = pltpu.roll(value, 1, 0)
            moved = pltpu.roll(column_in, jnp.where(high_side, LANES - 1 - m, lax.rem(LANES - m, LANES)), 1)
            moved = jnp.concatenate([moved] * blocks, axis=1)
            north = jnp.where(lane == y_cells - 1, moved, pltpu.roll(value, y_cells - 1, 1))
            south = jnp.where(lane == 0, moved, pltpu.roll(value, 1, 1))
            image = value - te * east - tw * west - unit_ref[2] * north - unit_ref[3] * south
            image = image - coupled[k * x_cells : (k + 1) * x_cells] * unit_ref[4]
            heavy = value * unit_ref[5]
            at = pl.ds(m, 1)
            acc_refs[0][at, :] += jnp.sum(fold_lanes(value * heavy), axis=0, keepdims=True)
            if power > 1:
                acc_refs[1][at, :] += jnp.sum(fold_lanes(before_ref[m] * heavy), axis=0, keepdims=True)
            if power < 3:
                image_ref[m] = image
                shifted = border_column(image[:, :LANES], image[:, y_cells - LANES :], high_side, m)
                column = jnp.where(lane_c == m, shifted, column)
            else:
                acc_refs[2][at, :] += jnp.sum(fold_lanes(image * heavy), axis=0, keepdims=True)
        if power < 3:
            column_ref[...] = column
            block = image_ref[pl.ds(start, GROUP)]
            found = pick(block.reshape(GROUP * x_cells, y_cells), oy)
            margin_ref[pl.ds(start, GROUP), :] = margin_values(found, inner_x)

    dots = [total_rows(ref[...]) for ref in acc_refs]
    dots.append(jnp.zeros((8 - len(dots), members), F32))
    dots_ref[...] = jnp.concatenate(dots, axis=0)


def finish_kernel(
    power,
    vf_ref,
    near_a_ref,
    near_b_ref,
    far_c_ref,
    far_d_ref,
    core_in_ref,
    diff_in_ref,
    wown_in_ref,
    sr_ref,
    scale_f_ref,
    unit_ref,
    table_ref,
    ghost_table_ref,
    *refs,
):
    if power == 1:
        (
            weight_ref,
            ofrac_ref,
            oy_ref,
            ox_ref,
            inner_margin_ref,
            inner_column_ref,
            image_in_ref,
            own_f_ref,
            *refs,
        ) = refs
    elif power == 2:
        (
            own_f_in_ref,
            weight_ref,
            ofrac_ref,
            oy_ref,
            ox_ref,
            inner_margin_ref,
            inner_column_ref,
            image_in_ref,
            *refs,
        ) = refs
    if power < 3:
        out_f_ref, diff_ref, wown_ref, to_a_ref, to_b_ref, sent_ref, core_ref, image_ref, work_ref = refs
    else:
        own_f_in_ref, v_ref, dots1_ref, dots2_ref, dots3_ref, moments_ref, acc_ref = refs
    half, frac_cells = vf_ref.shape
    x_cells, y_cells = unit_ref.shape[1:]
    members = v_ref.shape[0] if power == 3 else image_ref.shape[0]
    blocks = y_cells // LANES
    frac_blocks = frac_cells // LANES
    here = Place()
    j, high_side = here.j, here.high_side
    base = blocks * members
    plus1, minus1, plus2, minus2 = neighbours(here, near_a_ref, near_b_ref, far_c_ref, far_d_ref)
    rows = sr_ref.shape[1]

    table, ghost_table = table_ref[...], ghost_table_ref[...]
    vf = vf_ref[...]
    ghosts = by_group(minus1(base, half), plus1(base, half), minus2(0, half), plus2(0, half))
    sums = by_group(
        plus1(base + half, half), minus1(base + half, half), plus2(half, half), minus2(half, half)
    )
    size = frac_blocks * half
    their_sums = from_blocks(core_in_ref[size : 2 * size, :], half)
    if power == 1:
        at = 2 * half
        back = by_group(
            plus1(base + at, half), minus1(base + at, half), plus2(at, half), minus2(at, half)
        )
        weight = weight_ref[...]
        wsum = pick(jnp.broadcast_to(weight, (8, weight.shape[1])), ofrac_ref[...], True)
        tail = core_in_ref.shape[0] - 8 * frac_blocks
        wsum = wsum + from_blocks(core_in_ref[tail:, :], 8)
        own_f = FRACTURE_STORAGE + wsum[:1] + pick(back, table[:, rows:], True)
        own_f_ref[...] = own_f
    else:
        own_f = own_f_in_ref[...]
    sr = sr_ref[...]
    flux = sr * (diff_in_ref[...] - pick(ghosts, ghost_table))
    image_f = own_f * vf + pick(jnp.concatenate([flux, -sums], axis=1), table, True)
    image_f = image_f - wown_in_ref[...] - their_sums

    if power == 3:
        acc_ref[...] = jnp.zeros_like(acc_ref)
        acc_ref[pl.ds(pl.multiple_of(j * half, half), half), :] = fold_lanes(vf * image_f)
        for side, at, reader in ((0, x_cells - 1, plus1), (1, 0, minus1)):
            factor = unit_ref[side, at : at + 1, :] * unit_ref[5, at : at + 1, :]
            edge = v_ref[:, at, :] * factor
            for q in range(blocks):
                beyond = reader(q * members, members)
                acc_ref[...] -= edge[:, q * LANES : (q + 1) * LANES] * beyond
        last = total_rows(acc_ref[...]) + dots3_ref[2:3, :]
        gap = jnp.zeros((1, LANES - 3 * members), F32)
        lines = [
            jnp.concatenate([dots1_ref[0:1, :], dots2_ref[1:2, :], dots2_ref[0:1, :], gap], axis=1),
            jnp.concatenate([dots3_ref[1:2, :], dots3_ref[0:1, :], last, gap], axis=1),
        ]
        lines = jnp.concatenate(lines, axis=0)
        moments_ref[...] = jnp.broadcast_to(lines[None], moments_ref.shape)
        return

    next_f = image_f * scale_f_ref[0]
    out_f_ref[...] = next_f
    at = blocks * members
    send_network(next_f, sr, table, ghost_table, diff_ref, [(to_a_ref, at), (to_b_ref, at), (sent_ref, 0)])

    edges = []
    for side, at, reader in ((0, x_cells - 1, plus1), (1, 0, minus1)):
        beyond = from_blocks(reader(0, base), members)
        edge = image_in_ref[:, at, :] - unit_ref[side, at : at + 1, :] * beyond
        image_ref[:, at, :] = edge
        edges.append(edge)
    to_a_ref[0:base, :] = to_blocks(jnp.where(here.even, edges[0], edges[1]))
    to_b_ref[0:base, :] = to_blocks(jnp.where(here.even, edges[1], edges[0]))
    margin, column = finish_edges(
        edges[0], edges[1], inner_margin_ref, inner_column_ref[...], high_side, oy_ref[...], ox_ref[...]
    )
    send_core(core_ref, next_f, margin, weight_ref[...], ofrac_ref[...], column, j, work_ref, wown_ref)


def close_kernel(totals_ref, v0_ref, v1_ref, v2_ref, f0_ref, f1_ref, f2_ref, x_ref, xf_ref, c_ref):
    members, x_cells, y_cells = v0_ref.shape
    half, frac_cells = f0_ref.shape

    total = jnp.sum(totals_ref[...], axis=0)
    m0, m1, m2, m3, m4, m5 = (
        total[k // 3 : k // 3 + 1, k % 3 * members : k % 3 * members + members] for k in range(6)
    )
    alpha0 = m0 / m1
    rz1 = m0 - 2.0 * alpha0 * m1 + alpha0 * alpha0 * m2
    beta1 = rz1 / m0
    a, b = 1.0 + beta1, -alpha0
    pap1 = a * a * m1 + 2.0 * a * b * m2 + b * b * m3
    alpha1 = rz1 / pap1
    e = -alpha0 - alpha1 * a
    g = -alpha1 * b
    rz2 = m0 + 2.0 * e * m1 + (e * e + 2.0 * g) * m2 + 2.0 * e * g * m3 + g * g * m4
    beta2 = rz2 / rz1
    c = 1.0 + beta2 * a
    d = e + beta2 * b
    pap2 = c * c * m1 + 2.0 * c * d * m2 + (d * d + 2.0 * c * g) * m3 + 2.0 * d * g * m4 + g * g * m5
    alpha2 = rz2 / pap2
    c0 = alpha0 + alpha1 * a + alpha2 * c
    c1 = alpha1 * b + alpha2 * d
    c2 = alpha2 * g
    for k, row in enumerate((c0, c1, c2)):
        row = jnp.concatenate([row, jnp.zeros((1, LANES - members), F32)], axis=1)
        c_ref[k] = jnp.transpose(jnp.broadcast_to(row, (LANES, LANES)))
    j = lax.axis_index("gy")
    own = pl.ds(pl.multiple_of(j * half, half), half)

    def wide(k, rows, width):
        return jnp.concatenate([c_ref[k, rows, :]] * (width // LANES), axis=1)

    xf_ref[...] = (
        wide(0, own, frac_cells) * f0_ref[...]
        + wide(1, own, frac_cells) * f1_ref[...]
        + wide(2, own, frac_cells) * f2_ref[...]
    )

    @pl.loop(0, members)
    def _(m):
        rows = pl.ds(m, 1)
        x_ref[m] = (
            wide(0, rows, y_cells) * v0_ref[m]
            + wide(1, rows, y_cells) * v1_ref[m]
            + wide(2, rows, y_cells) * v2_ref[m]
        )


def pairs_of(count, stride, phase):
    out = []
    for index in range(count):
        if (index // stride) % 2 == phase:
            mate = (index + stride) % count
            out += [(index, mate), (mate, index)]
    return out


VMEM = pl.BlockSpec(memory_space=pltpu.VMEM)
SMEM = pl.BlockSpec(memory_space=pltpu.SMEM)


def call(kernel, name, args, outs, scratch=(), scalars=0, cost=None, aliases=None):
    return pl.pallas_call(
        kernel,
        name=name,
        out_shape=[jax.ShapeDtypeStruct(shape, dtype) for shape, dtype in outs],
        in_specs=[SMEM] * scalars + [VMEM] * (len(args) - scalars),
        out_specs=[VMEM] * len(outs),
        scratch_shapes=list(scratch),
        compiler_params=pltpu.CompilerParams(vmem_limit_bytes=40 * 1024 * 1024),
        cost_estimate=cost,
        input_output_aliases=aliases or {},
    )(*args)


def per_device(
    source_matrix,
    source_fracture,
    aperture,
    storage,
    perm_class,
    class_perm,
    send_slots,
    isect_local,
    isect_other,
    isect_count,
    ov_cell,
    ov_frac,
    ov_weight,
    ov_count,
):
    members, x_cells, y_cells = source_matrix.shape
    half, frac_cells = source_fracture.shape
    slots = send_slots.shape[1]
    rows = isect_local.size
    margin = ov_cell.size
    count = lax.axis_size("gx")

    def near(to_a, to_b):
        return (
            lax.ppermute(to_a, "gx", pairs_of(count, 1, 0)),
            lax.ppermute(to_b, "gx", pairs_of(count, 1, 1)),
        )

    def far(value):
        return (
            lax.ppermute(value, "gx", pairs_of(count, 2, 0)),
            lax.ppermute(value, "gx", pairs_of(count, 2, 1)),
        )

    def core(value):
        return lax.ppermute(value, "gy", [(0, 1), (1, 0)])

    blocks = y_cells // LANES
    frac_blocks = frac_cells // LANES
    field = (members, x_cells, y_cells)
    own = (half, frac_cells)
    hidden = pl.CostEstimate(flops=4_000_000_000, bytes_accessed=12_000_000, transcendentals=0)
    perm, cond, oslot, to_a, to_b, sent, border = call(
        opening_kernel,
        "opening",
        (class_perm, perm_class, aperture, send_slots),
        [
            ((x_cells, y_cells), F32),
            (own, F32),
            ((frac_cells, slots), BF16),
            ((half + 8 * (-(-blocks // 8)), LANES), F32),
            ((half + 8 * (-(-blocks // 8)), LANES), F32),
            ((half, slots), F32),
            ((x_cells, LANES), F32),
        ],
        scalars=1,
    )

    def exchange(to_a, to_b, sent, to_core):
        near_a, near_b = near(to_a, to_b)
        core_in = core(to_core)
        sent, core_in = lax.optimization_barrier((sent, core_in))
        far_c, far_d = far(sent)
        return near_a, near_b, far_c, far_d, core_in

    near_a, near_b, far_c, far_d, border = exchange(to_a, to_b, sent, border)
    coef, oy, ox, weight, first, second, table, ghost_table, ofrac, v0, margin_in, column = call(
        inside_kernel,
        "inside",
        (
            ov_count.reshape(-1),
            perm,
            border,
            storage,
            source_matrix,
            ov_cell.reshape(-1, LANES),
            ov_weight.reshape(-1, LANES),
            isect_local,
            isect_other,
            ov_frac.reshape(-1, LANES),
            oslot,
        ),
        [
            ((5, x_cells, y_cells), F32),
            ((y_cells, margin), BF16),
            ((x_cells, margin), F32),
            ((1, margin), F32),
            ((frac_cells, rows), BF16),
            ((frac_cells, rows), BF16),
            ((frac_cells, rows + slots), BF16),
            ((slots, rows), BF16),
            ((frac_cells, margin), BF16),
            (field, F32),
            ((members, margin), F32),
            ((x_cells, LANES), F32),
        ],
        scalars=1,
        cost=hidden,
    )
    core_rows = 2 * frac_blocks * half + x_cells
    edge_rows = blocks * members
    unit, f0, sr, scale_f, diff, wown, to_a, to_b, sent, core_msg, v0 = call(
        first_kernel,
        "first_vector",
        (
            isect_count,
            coef,
            perm,
            cond,
            source_matrix,
            source_fracture,
            weight,
            near_a,
            near_b,
            far_c,
            far_d,
            first,
            second,
            table,
            ghost_table,
            ofrac,
            oy,
            ox,
            margin_in,
            column,
            v0,
        ),
        [
            ((6, x_cells, y_cells), F32),
            (own, F32),
            ((half, rows), F32),
            ((2, half, frac_cells), F32),
            ((half, rows), F32),
            (own, F32),
            ((edge_rows + 3 * half, LANES), F32),
            ((edge_rows + 3 * half, LANES), F32),
            ((3 * half, LANES), F32),
            ((core_rows + 8 * frac_blocks, LANES), F32),
            (field, F32),
        ],
        scratch=[pltpu.VMEM((members, frac_cells), F32)],
        scalars=1,
        aliases={20: 10},
    )
    near_rows = edge_rows + 2 * half

    def interior(power, v, before, vf, before_f, core_in):
        outs = []
        if power < 3:
            outs = [(field, F32), ((members, margin), F32), ((x_cells, LANES), F32)]
        return call(
            functools.partial(interior_kernel, power),
            f"interior_{power}",
            (v, before, vf, before_f, core_in, scale_f, unit, weight, ofrac, oy, ox),
            outs + [((8, members), F32)],
            scratch=[pltpu.VMEM((members, margin), F32), pltpu.VMEM((members, frac_cells), F32)]
            + [pltpu.VMEM((members, LANES), F32)] * power,
            cost=hidden,
        )

    finish_outs = [
        (own, F32),
        ((half, rows), F32),
        (own, F32),
        ((near_rows, LANES), F32),
        ((near_rows, LANES), F32),
        ((2 * half, LANES), F32),
        ((core_rows, LANES), F32),
        (field, F32),
    ]
    finish_scratch = [pltpu.VMEM((members, frac_cells), F32)]

    near_a, near_b, far_c, far_d, core_in = exchange(to_a, to_b, sent, core_msg)
    image, margin_in, column, dots1 = interior(1, v0, v0, f0, f0, core_in)
    own_f, f1, diff, wown, to_a, to_b, sent, core_msg, v1 = call(
        functools.partial(finish_kernel, 1),
        "finish_1",
        (f0, near_a, near_b, far_c, far_d, core_in, diff, wown, sr, scale_f, unit, table, ghost_table)
        + (weight, ofrac, oy, ox, margin_in, column, image),
        [(own, F32)] + finish_outs,
        scratch=finish_scratch,
        aliases={19: 8},
    )
    near_a, near_b, far_c, far_d, core_in = exchange(to_a, to_b, sent, core_msg)
    image, margin_in, column, dots2 = interior(2, v1, v0, f1, f0, core_in)
    f2, diff, wown, to_a, to_b, sent, core_msg, v2 = call(
        functools.partial(finish_kernel, 2),
        "finish_2",
        (f1, near_a, near_b, far_c, far_d, core_in, diff, wown, sr, scale_f, unit, table, ghost_table)
        + (own_f, weight, ofrac, oy, ox, margin_in, column, image),
        finish_outs,
        scratch=finish_scratch,
        aliases={20: 7},
    )
    near_a, near_b, far_c, far_d, core_in = exchange(to_a, to_b, sent, core_msg)
    (dots3,) = interior(3, v2, v1, f2, f1, core_in)
    peers = count * lax.axis_size("gy")
    (moments,) = call(
        functools.partial(finish_kernel, 3),
        "finish_3",
        (f2, near_a, near_b, far_c, far_d, core_in, diff, wown, sr, scale_f, unit, table, ghost_table)
        + (own_f, v2, dots1, dots2, dots3),
        [((peers, 2, LANES), F32)],
        scratch=[pltpu.VMEM((members, LANES), F32)],
    )
    totals = lax.all_to_all(moments, ("gx", "gy"), 0, 0)
    return call(
        close_kernel,
        "iterate",
        (totals, v0, v1, v2, f0, f1, f2),
        [(field, F32), (own, F32)],
        scratch=[pltpu.VMEM((3, LANES, LANES), F32)],
    )


def solution(mesh):
    placed = (
        P("grp", "gx", "gy"),
        P(("grp", "gy"), "gx"),
        P(("grp", "gy"), "gx"),
        P("gx", "gy"),
        P("gx", "gy"),
        P(),
        P("gx", None),
        P("gx", None),
        P("gx", None),
        P("gx"),
        P("gx", "gy", None, None),
        P("gx", "gy", None, None),
        P("gx", "gy", None, None),
        P("gx", "gy", None),
    )
    return jax.shard_map(
        per_device,
        mesh=mesh,
        in_specs=placed,
        out_specs=(P("grp", "gx", "gy"), P(("grp", "gy"), "gx")),
        check_vma=False,
    )
```

```python
import functools

import jax
import jax.numpy as jnp
from jax import lax
from jax.experimental import pallas as pl
from jax.experimental.pallas import tpu as pltpu
from jax.sharding import PartitionSpec as P

FRACTURE_STORAGE = 0.1
F32 = jnp.float32
BF16 = jnp.bfloat16
LANES = 128
GROUP = 16


def split3(x):
    high = x.astype(BF16)
    rest = x - high.astype(F32)
    mid = rest.astype(BF16)
    low = (rest - mid.astype(F32)).astype(BF16)
    return jnp.concatenate([high, mid, low], axis=0)


def pick(x, table, transposed=False):
    rows = x.shape[0]
    dims = (((1,), (1 if transposed else 0,)), ((), ()))
    out = lax.dot_general(split3(x), table, dims, preferred_element_type=F32)
    return out[:rows] + out[rows : 2 * rows] + out[2 * rows :]


def fetch(sources, targets, sems):
    copies = [pltpu.make_async_copy(a, b, sems.at[k]) for k, (a, b) in enumerate(zip(sources, targets))]
    for copy in copies:
        copy.start()
    return copies


class Place:
    def __init__(self):
        count = lax.axis_size("gx")
        i = lax.axis_index("gx")
        self.j = lax.axis_index("gy")
        self.high_side = self.j == 0
        self.even = lax.rem(i, 2) == 0
        self.low_pair = lax.rem(lax.div(i, 2), 2) == 0
        self.first = i == 0
        self.last = i == count - 1


def harmonic(first_perm, second_perm):
    return 2.0 * first_perm * second_perm / (first_perm + second_perm)


def one_hot(index_row, size):
    shape = (size, index_row.shape[1])
    ids = lax.broadcasted_iota(jnp.int32, shape, 0)
    return jnp.where(ids == index_row, 1.0, 0.0).astype(BF16)


def to_blocks(x):
    return jnp.concatenate(
        [x[:, q : q + LANES] for q in range(0, x.shape[1], LANES)], axis=0
    )


def from_blocks(x, rows):
    return jnp.concatenate(
        [x[q : q + rows] for q in range(0, x.shape[0], rows)], axis=1
    )


def by_group(first, second, third, fourth):
    group = first.shape[1] // 4
    lane = lax.broadcasted_iota(jnp.int32, first.shape, 1)
    return jnp.where(
        lane < group,
        first,
        jnp.where(lane < 2 * group, second, jnp.where(lane < 3 * group, third, fourth)),
    )


def total_rows(x):
    return jnp.sum(jnp.transpose(x), axis=0, keepdims=True)


def fold_lanes(x):
    rows, width = x.shape
    out = x[:, :LANES]
    for q in range(LANES, width, LANES):
        out = out + x[:, q : q + LANES]
    return out


def opening_kernel(
    perm_table_hbm,
    class_hbm,
    aperture_hbm,
    slots_hbm,
    perm_ref,
    cond_ref,
    oslot_ref,
    near_a_ref,
    near_b_ref,
    far_ref,
    border_ref,
    perm_table_ref,
    class_ref,
    aperture_ref,
    slots_ref,
    sems,
):
    copies = fetch(
        (class_hbm, perm_table_hbm, aperture_hbm, slots_hbm),
        (class_ref, perm_table_ref, aperture_ref, slots_ref),
        sems,
    )
    for copy in copies:
        copy.wait()
    x_cells, y_cells = class_ref.shape
    half = aperture_ref.shape[0]
    here = Place()
    classes = class_ref[...]
    perm = jnp.zeros(classes.shape, F32)
    for index in range(perm_table_ref.shape[0]):
        perm = jnp.where(classes == index, perm_table_ref[index], perm)
    perm_ref[...] = perm
    border_ref[...] = jnp.where(here.high_side, perm[:, y_cells - LANES :], perm[:, :LANES])

    aperture = aperture_ref[...]
    cond = aperture * aperture * aperture
    cond_ref[...] = cond
    oslot = one_hot(slots_ref[...], cond.shape[1])
    oslot_ref[...] = oslot
    supplied = pick(cond, oslot)
    far_ref[...] = supplied
    up, down = to_blocks(perm[x_cells - 1 :]), to_blocks(perm[:1])
    blocks = up.shape[0]
    pad = jnp.zeros((near_a_ref.shape[0] - half - blocks, LANES), F32)
    for ref, edge in ((near_a_ref, jnp.where(here.even, up, down)), (near_b_ref, jnp.where(here.even, down, up))):
        ref[...] = jnp.concatenate([supplied, edge, pad], axis=0)


def neighbours(here, near_a_ref, near_b_ref, far_c_ref, far_d_ref):
    def reader(flag, at_zero, at_one):
        return lambda at, size: jnp.where(
            flag, at_zero[at : at + size, :], at_one[at : at + size, :]
        )

    return (
        reader(here.even, near_a_ref, near_b_ref),
        reader(here.even, near_b_ref, near_a_ref),
        reader(here.low_pair, far_c_ref, far_d_ref),
        reader(here.low_pair, far_d_ref, far_c_ref),
    )


def margin_values(found, ox):
    found = found.reshape(-1, *ox.shape) * ox[None]
    return jnp.sum(found, axis=1)


def border_column(tile_low, tile_high, high_side, m):
    tile = jnp.where(high_side, tile_high, tile_low)
    return pltpu.roll(tile, jnp.where(high_side, lax.rem(m + 1, LANES), m), 1)


def border_row(row_values, high_side):
    members, y_cells = row_values.shape
    tile = jnp.where(high_side, row_values[:, y_cells - LANES :], row_values[:, :LANES])
    turned = jnp.transpose(tile)
    line = jnp.where(high_side, turned[LANES - 1 :], turned[:1])
    return jnp.concatenate([line, jnp.zeros((1, LANES - members), F32)], axis=1)


def finish_edges(high_rows, low_rows, partial_ref, column, high_side, oy, ox):
    members = high_rows.shape[0]
    x_cells = ox.shape[0]
    found = pick(jnp.concatenate([high_rows, low_rows], axis=0), oy)
    margin = partial_ref[...] + found[:members] * ox[x_cells - 1 :] + found[members:] * ox[:1]
    row = lax.broadcasted_iota(jnp.int32, column.shape, 0)
    column = jnp.where(row == x_cells - 1, border_row(high_rows, high_side), column)
    return margin, jnp.where(row == 0, border_row(low_rows, high_side), column)


def send_network(vf, sr, table, ghost_table, diff_ref, refs):
    half = vf.shape[0]
    rows = sr.shape[1]
    found = pick(vf, table)
    diff_ref[...] = found[:, :rows]
    sums = pick(sr * found[:, :rows], ghost_table, True)
    for ref, at in refs:
        ref[at : at + half, :] = found[:, rows:]
        ref[at + half : at + 2 * half, :] = sums


def send_core(core_ref, vf, margin, weight, ofrac, column, j, work_ref, wown_ref):
    half, frac_cells = vf.shape
    work_ref[...] = pick(margin * weight, ofrac, True)
    wown_ref[...] = work_ref[pl.ds(pl.multiple_of(j * half, half), half), :]
    other = work_ref[pl.ds(pl.multiple_of((1 - j) * half, half), half), :]
    size = frac_cells // LANES * half
    core_ref[0:size, :] = to_blocks(vf)
    core_ref[size : 2 * size, :] = to_blocks(other)
    core_ref[2 * size : 2 * size + column.shape[0], :] = column


def inside_kernel(
    ov_count_hbm,
    isect_count_hbm,
    storage_hbm,
    source_hbm,
    source_f_hbm,
    cell_hbm,
    ov_weight_hbm,
    local_hbm,
    other_hbm,
    frac_hbm,
    perm_ref,
    border_ref,
    oslot_ref,
    source_f_ref,
    live_ref,
    edge_ref,
    coef_ref,
    oy_ref,
    ox_ref,
    weight_ref,
    first_ref,
    second_ref,
    table_ref,
    ghost_table_ref,
    ofrac_ref,
    v_ref,
    margin_ref,
    column_ref,
    ov_count_ref,
    isect_count_ref,
    storage_ref,
    source_ref,
    cell_ref,
    ov_weight_ref,
    local_ref,
    other_in_ref,
    frac_ref,
    sems,
):
    members, x_cells, y_cells = source_ref.shape
    frac_cells = table_ref.shape[0]
    here = Place()
    high_side = here.high_side
    copies = fetch(
        (
            cell_hbm,
            local_hbm,
            other_hbm,
            frac_hbm,
            ov_weight_hbm,
            ov_count_hbm,
            isect_count_hbm,
            storage_hbm,
            source_f_hbm,
            source_hbm,
        ),
        (
            cell_ref,
            local_ref,
            other_in_ref,
            frac_ref,
            ov_weight_ref,
            ov_count_ref,
            isect_count_ref,
            storage_ref,
            source_f_ref,
            source_ref,
        ),
        sems,
    )

    def line(ref):
        return jnp.concatenate([ref[k : k + 1, :] for k in range(ref.shape[0])], axis=1)

    rows = local_ref.size
    perm, border = perm_ref[...], border_ref[...]
    col = jnp.where(high_side, border[:, :1], border[:, LANES - 1 :])
    lane = lax.broadcasted_iota(jnp.int32, perm.shape, 1)
    row = lax.broadcasted_iota(jnp.int32, perm.shape, 0)
    north = jnp.concatenate([perm[:, 1:], col], axis=1)
    south = jnp.concatenate([col, perm[:, :-1]], axis=1)
    tn = jnp.where((lane == y_cells - 1) & jnp.logical_not(high_side), 0.0, harmonic(perm, north))
    ts = jnp.where((lane == 0) & high_side, 0.0, harmonic(perm, south))
    east = jnp.concatenate([perm[1:], perm[:1]], axis=0)
    west = jnp.concatenate([perm[-1:], perm[:-1]], axis=0)
    te = jnp.where(row == x_cells - 1, 0.0, harmonic(perm, east))
    tw = jnp.where(row == 0, 0.0, harmonic(perm, west))
    for copy in copies[:-1]:
        copy.wait()
    cell = line(cell_ref)
    oy = one_hot(cell % y_cells, y_cells)
    oy_ref[...] = oy
    row_x = lax.broadcasted_iota(jnp.int32, ox_ref.shape, 0)
    at_x = row_x == cell // y_cells
    ox = jnp.where(at_x, 1.0, 0.0)
    ox_ref[...] = ox
    lane_w = lax.broadcasted_iota(jnp.int32, (1, LANES), 1)
    weight = jnp.concatenate(
        [jnp.where(lane_w < ov_count_ref[k], ov_weight_ref[k : k + 1, :], 0.0) for k in range(ov_weight_ref.shape[0])],
        axis=1,
    )
    weight_ref[...] = weight
    for block in range(local_ref.shape[0]):
        at = slice(block * LANES, (block + 1) * LANES)
        live_ref[:, at] = jnp.where(lane_w < isect_count_ref[block], 1.0, 0.0)
    part = storage_ref[...] + te + tw + tn + ts + pick(jnp.where(at_x, weight, 0.0), oy, True)
    coef_ref[0] = te
    coef_ref[1] = tw
    coef_ref[2] = tn
    coef_ref[3] = ts
    coef_ref[4] = part

    other = line(other_in_ref)
    first, second = one_hot(line(local_ref), frac_cells), one_hot(other, frac_cells)
    first_ref[...] = first
    second_ref[...] = second
    table_ref[:, :rows] = first - second
    table_ref[:, rows:] = oslot_ref[...]
    ghost_table_ref[...] = one_hot(other - frac_cells, ghost_table_ref.shape[0])
    ofrac_ref[...] = one_hot(line(frac_ref), frac_cells)

    inverse = 1.0 / part
    inner_x = jnp.where((row_x == 0) | (row_x == x_cells - 1), 0.0, ox)
    lane_c = lax.broadcasted_iota(jnp.int32, (x_cells, LANES), 1)
    column_ref[...] = jnp.zeros_like(column_ref)
    copies[-1].wait()
    edge_ref[0] = source_ref[:, x_cells - 1, :]
    edge_ref[1] = source_ref[:, 0, :]

    @pl.loop(0, members // GROUP)
    def _(index):
        start = index * GROUP
        block = source_ref[pl.ds(start, GROUP)] * inverse[None]
        v_ref[pl.ds(start, GROUP)] = block
        found = pick(block.reshape(GROUP * x_cells, y_cells), oy_ref[...])
        margin_ref[pl.ds(start, GROUP), :] = margin_values(found, inner_x)
        column = column_ref[...]
        for k in range(GROUP):
            m = start + k
            moved = border_column(block[k, :, :LANES], block[k, :, y_cells - LANES :], high_side, m)
            column = jnp.where(lane_c == m, moved, column)
        column_ref[...] = column


def first_kernel(
    live_ref,
    coef_ref,
    perm_ref,
    cond_ref,
    edge_ref,
    source_f_ref,
    weight_ref,
    near_a_ref,
    near_b_ref,
    far_c_ref,
    far_d_ref,
    first_ref,
    second_ref,
    table_ref,
    ghost_table_ref,
    ofrac_ref,
    oy_ref,
    ox_ref,
    inner_margin_ref,
    inner_column_ref,
    v_in_ref,
    unit_ref,
    vf_ref,
    sr_ref,
    scale_f_ref,
    diff_ref,
    wown_ref,
    to_a_ref,
    to_b_ref,
    sent_ref,
    core_ref,
    v_ref,
    work_ref,
):
    members, x_cells, y_cells = v_ref.shape
    half, frac_cells = source_f_ref.shape
    blocks = y_cells // LANES
    here = Place()
    j, high_side = here.j, here.high_side
    base = blocks * members
    plus1, minus1, plus2, minus2 = neighbours(here, near_a_ref, near_b_ref, far_c_ref, far_d_ref)

    ghosts = by_group(minus1(0, half), plus1(0, half), minus2(0, half), plus2(0, half))
    table, ghost_table = table_ref[...], ghost_table_ref[...]
    cond = cond_ref[...]
    cond_first = pick(cond, first_ref[...])
    cond_second = pick(cond, second_ref[...]) + pick(ghosts, ghost_table)
    sr = jnp.where(live_ref[...] > 0.0, harmonic(cond_first, cond_second), 0.0)
    sr_ref[...] = sr
    diag_f = FRACTURE_STORAGE + pick(sr, first_ref[...], True)
    inverse_f = 1.0 / diag_f
    scale_f_ref[0] = inverse_f
    scale_f_ref[1] = diag_f
    vf = source_f_ref[...] * inverse_f
    vf_ref[...] = vf
    refs = [(to_a_ref, base), (to_b_ref, base), (sent_ref, 0)]
    send_network(vf, sr, table, ghost_table, diff_ref, refs)
    slot_sums = pick(sr, ghost_table, True)
    for ref, at in refs:
        ref[at + 2 * half : at + 3 * half, :] = slot_sums

    perm, part = perm_ref[...], coef_ref[4]
    row = lax.broadcasted_iota(jnp.int32, perm.shape, 0)
    perm_plus = from_blocks(plus1(half, blocks), 1)
    perm_minus = from_blocks(minus1(half, blocks), 1)
    te_edge = jnp.where(here.last, 0.0, harmonic(perm[x_cells - 1 :], perm_plus))
    tw_edge = jnp.where(here.first, 0.0, harmonic(perm[:1], perm_minus))
    te = jnp.where(row == x_cells - 1, te_edge, coef_ref[0])
    tw = jnp.where(row == 0, tw_edge, coef_ref[1])
    diag = part + jnp.where(row == x_cells - 1, te_edge, 0.0) + jnp.where(row == 0, tw_edge, 0.0)
    inverse = 1.0 / diag
    unit_ref[0] = te * inverse
    unit_ref[1] = tw * inverse
    unit_ref[2] = coef_ref[2] * inverse
    unit_ref[3] = coef_ref[3] * inverse
    unit_ref[4] = inverse
    unit_ref[5] = diag
    high_rows = edge_ref[0] * inverse[x_cells - 1 :]
    low_rows = edge_ref[1] * inverse[:1]
    v_ref[:, x_cells - 1, :] = high_rows
    v_ref[:, 0, :] = low_rows
    to_a_ref[0:base, :] = to_blocks(jnp.where(here.even, high_rows, low_rows))
    to_b_ref[0:base, :] = to_blocks(jnp.where(here.even, low_rows, high_rows))
    margin, column = finish_edges(
        high_rows, low_rows, inner_margin_ref, inner_column_ref[...], high_side, oy_ref[...], ox_ref[...]
    )
    weight = weight_ref[...]
    send_core(core_ref, vf, margin, weight, ofrac_ref[...], column, j, work_ref, wown_ref)
    wsum = pick(jnp.broadcast_to(weight, (8, weight.shape[1])), ofrac_ref[...], True)
    tail = core_ref.shape[0] - 8 * (frac_cells // LANES)
    core_ref[tail:, :] = to_blocks(wsum)


def interior_kernel(
    power,
    v_ref,
    before_ref,
    vf_ref,
    before_f_ref,
    core_ref,
    scale_f_ref,
    unit_ref,
    weight_ref,
    ofrac_ref,
    oy_ref,
    ox_ref,
    *refs,
):
    if power < 3:
        image_ref, margin_ref, column_ref, dots_ref, flow_ref, work_ref, *acc_refs = refs
    else:
        dots_ref, flow_ref, work_ref, *acc_refs = refs
    members, x_cells, y_cells = v_ref.shape
    half, frac_cells = vf_ref.shape
    blocks = y_cells // LANES
    here = Place()
    j, high_side = here.j, here.high_side
    size = frac_cells // LANES * half
    theirs = from_blocks(core_ref[0:size, :], half)
    column_in = core_ref[2 * size : 2 * size + x_cells, :]
    vf = vf_ref[...]
    own_rows = pl.ds(pl.multiple_of(j * half, half), half)
    work_ref[own_rows, :] = vf
    work_ref[pl.ds(pl.multiple_of((1 - j) * half, half), half), :] = theirs
    flow_ref[...] = pick(work_ref[...], ofrac_ref[...]) * weight_ref[...]

    heavy_f = vf * scale_f_ref[1]
    for ref in acc_refs:
        ref[...] = jnp.zeros_like(ref)
    acc_refs[0][own_rows, :] = fold_lanes(vf * heavy_f)
    if power > 1:
        acc_refs[1][own_rows, :] = fold_lanes(before_f_ref[...] * heavy_f)

    lane_c = lax.broadcasted_iota(jnp.int32, (x_cells, LANES), 1)
    lane = lax.broadcasted_iota(jnp.int32, (x_cells, y_cells), 1)
    row = lax.broadcasted_iota(jnp.int32, (x_cells, y_cells), 0)
    row_x = lax.broadcasted_iota(jnp.int32, ox_ref.shape, 0)
    oy, ox = oy_ref[...], ox_ref[...]
    inner_x = jnp.where((row_x == 0) | (row_x == x_cells - 1), 0.0, ox)
    te = jnp.where(row == x_cells - 1, 0.0, unit_ref[0])
    tw = jnp.where(row == 0, 0.0, unit_ref[1])
    if power < 3:
        column_ref[...] = jnp.zeros_like(column_ref)

    @pl.loop(0, members // GROUP)
    def _(index):
        start = index * GROUP
        parts = []
        for k in range(GROUP):
            parts.append(ox * flow_ref[pl.ds(start + k, 1), :])
        coupled = pick(jnp.concatenate(parts, axis=0), oy, True)
        if power < 3:
            column = column_ref[...]
        for k in range(GROUP):
            m = start + k
            value = v_ref[m]
            east = pltpu.roll(value, x_cells - 1, 0)
            west = pltpu.roll(value, 1, 0)
            moved = pltpu.roll(column_in, jnp.where(high_side, LANES - 1 - m, lax.rem(LANES - m, LANES)), 1)
            moved = jnp.concatenate([moved] * blocks, axis=1)
            north = jnp.where(lane == y_cells - 1, moved, pltpu.roll(value, y_cells - 1, 1))
            south = jnp.where(lane == 0, moved, pltpu.roll(value, 1, 1))
            image = value - te * east - tw * west - unit_ref[2] * north - unit_ref[3] * south
            image = image - coupled[k * x_cells : (k + 1) * x_cells] * unit_ref[4]
            heavy = value * unit_ref[5]
            at = pl.ds(m, 1)
            acc_refs[0][at, :] += jnp.sum(fold_lanes(value * heavy), axis=0, keepdims=True)
            if power > 1:
                acc_refs[1][at, :] += jnp.sum(fold_lanes(before_ref[m] * heavy), axis=0, keepdims=True)
            if power < 3:
                image_ref[m] = image
                shifted = border_column(image[:, :LANES], image[:, y_cells - LANES :], high_side, m)
                column = jnp.where(lane_c == m, shifted, column)
            else:
                acc_refs[2][at, :] += jnp.sum(fold_lanes(image * heavy), axis=0, keepdims=True)
        if power < 3:
            column_ref[...] = column
            block = image_ref[pl.ds(start, GROUP)]
            found = pick(block.reshape(GROUP * x_cells, y_cells), oy)
            margin_ref[pl.ds(start, GROUP), :] = margin_values(found, inner_x)

    dots = [total_rows(ref[...]) for ref in acc_refs]
    dots.append(jnp.zeros((8 - len(dots), members), F32))
    dots_ref[...] = jnp.concatenate(dots, axis=0)


def finish_kernel(
    power,
    vf_ref,
    near_a_ref,
    near_b_ref,
    far_c_ref,
    far_d_ref,
    core_in_ref,
    diff_in_ref,
    wown_in_ref,
    sr_ref,
    scale_f_ref,
    unit_ref,
    table_ref,
    ghost_table_ref,
    *refs,
):
    if power == 1:
        (
            weight_ref,
            ofrac_ref,
            oy_ref,
            ox_ref,
            inner_margin_ref,
            inner_column_ref,
            image_in_ref,
            own_f_ref,
            *refs,
        ) = refs
    elif power == 2:
        (
            own_f_in_ref,
            weight_ref,
            ofrac_ref,
            oy_ref,
            ox_ref,
            inner_margin_ref,
            inner_column_ref,
            image_in_ref,
            *refs,
        ) = refs
    if power < 3:
        out_f_ref, diff_ref, wown_ref, to_a_ref, to_b_ref, sent_ref, core_ref, image_ref, work_ref = refs
    else:
        own_f_in_ref, v_ref, dots1_ref, dots2_ref, dots3_ref, moments_ref, acc_ref = refs
    half, frac_cells = vf_ref.shape
    x_cells, y_cells = unit_ref.shape[1:]
    members = v_ref.shape[0] if power == 3 else image_ref.shape[0]
    blocks = y_cells // LANES
    frac_blocks = frac_cells // LANES
    here = Place()
    j, high_side = here.j, here.high_side
    base = blocks * members
    plus1, minus1, plus2, minus2 = neighbours(here, near_a_ref, near_b_ref, far_c_ref, far_d_ref)
    rows = sr_ref.shape[1]

    table, ghost_table = table_ref[...], ghost_table_ref[...]
    vf = vf_ref[...]
    ghosts = by_group(minus1(base, half), plus1(base, half), minus2(0, half), plus2(0, half))
    sums = by_group(
        plus1(base + half, half), minus1(base + half, half), plus2(half, half), minus2(half, half)
    )
    size = frac_blocks * half
    their_sums = from_blocks(core_in_ref[size : 2 * size, :], half)
    if power == 1:
        at = 2 * half
        back = by_group(
            plus1(base + at, half), minus1(base + at, half), plus2(at, half), minus2(at, half)
        )
        weight = weight_ref[...]
        wsum = pick(jnp.broadcast_to(weight, (8, weight.shape[1])), ofrac_ref[...], True)
        tail = core_in_ref.shape[0] - 8 * frac_blocks
        wsum = wsum + from_blocks(core_in_ref[tail:, :], 8)
        own_f = FRACTURE_STORAGE + wsum[:1] + pick(back, table[:, rows:], True)
        own_f_ref[...] = own_f
    else:
        own_f = own_f_in_ref[...]
    sr = sr_ref[...]
    flux = sr * (diff_in_ref[...] - pick(ghosts, ghost_table))
    image_f = own_f * vf + pick(jnp.concatenate([flux, -sums], axis=1), table, True)
    image_f = image_f - wown_in_ref[...] - their_sums

    if power == 3:
        acc_ref[...] = jnp.zeros_like(acc_ref)
        acc_ref[pl.ds(pl.multiple_of(j * half, half), half), :] = fold_lanes(vf * image_f)
        for side, at, reader in ((0, x_cells - 1, plus1), (1, 0, minus1)):
            factor = unit_ref[side, at : at + 1, :] * unit_ref[5, at : at + 1, :]
            edge = v_ref[:, at, :] * factor
            for q in range(blocks):
                beyond = reader(q * members, members)
                acc_ref[...] -= edge[:, q * LANES : (q + 1) * LANES] * beyond
        last = total_rows(acc_ref[...]) + dots3_ref[2:3, :]
        gap = jnp.zeros((1, LANES - 3 * members), F32)
        lines = [
            jnp.concatenate([dots1_ref[0:1, :], dots2_ref[1:2, :], dots2_ref[0:1, :], gap], axis=1),
            jnp.concatenate([dots3_ref[1:2, :], dots3_ref[0:1, :], last, gap], axis=1),
        ]
        lines = jnp.concatenate(lines, axis=0)
        moments_ref[...] = jnp.broadcast_to(lines[None], moments_ref.shape)
        return

    next_f = image_f * scale_f_ref[0]
    out_f_ref[...] = next_f
    at = blocks * members
    send_network(next_f, sr, table, ghost_table, diff_ref, [(to_a_ref, at), (to_b_ref, at), (sent_ref, 0)])

    edges = []
    for side, at, reader in ((0, x_cells - 1, plus1), (1, 0, minus1)):
        beyond = from_blocks(reader(0, base), members)
        edge = image_in_ref[:, at, :] - unit_ref[side, at : at + 1, :] * beyond
        image_ref[:, at, :] = edge
        edges.append(edge)
    to_a_ref[0:base, :] = to_blocks(jnp.where(here.even, edges[0], edges[1]))
    to_b_ref[0:base, :] = to_blocks(jnp.where(here.even, edges[1], edges[0]))
    margin, column = finish_edges(
        edges[0], edges[1], inner_margin_ref, inner_column_ref[...], high_side, oy_ref[...], ox_ref[...]
    )
    send_core(core_ref, next_f, margin, weight_ref[...], ofrac_ref[...], column, j, work_ref, wown_ref)


def close_kernel(totals_ref, v0_ref, v1_ref, v2_ref, f0_ref, f1_ref, f2_ref, x_hbm, xf_hbm, c_ref, x_ref, xf_ref, sems):
    members, x_cells, y_cells = v0_ref.shape
    half, frac_cells = f0_ref.shape

    total = jnp.sum(totals_ref[...], axis=0)
    m0, m1, m2, m3, m4, m5 = (
        total[k // 3 : k // 3 + 1, k % 3 * members : k % 3 * members + members] for k in range(6)
    )
    alpha0 = m0 / m1
    rz1 = m0 - 2.0 * alpha0 * m1 + alpha0 * alpha0 * m2
    beta1 = rz1 / m0
    a, b = 1.0 + beta1, -alpha0
    pap1 = a * a * m1 + 2.0 * a * b * m2 + b * b * m3
    alpha1 = rz1 / pap1
    e = -alpha0 - alpha1 * a
    g = -alpha1 * b
    rz2 = m0 + 2.0 * e * m1 + (e * e + 2.0 * g) * m2 + 2.0 * e * g * m3 + g * g * m4
    beta2 = rz2 / rz1
    c = 1.0 + beta2 * a
    d = e + beta2 * b
    pap2 = c * c * m1 + 2.0 * c * d * m2 + (d * d + 2.0 * c * g) * m3 + 2.0 * d * g * m4 + g * g * m5
    alpha2 = rz2 / pap2
    c0 = alpha0 + alpha1 * a + alpha2 * c
    c1 = alpha1 * b + alpha2 * d
    c2 = alpha2 * g
    for k, row in enumerate((c0, c1, c2)):
        row = jnp.concatenate([row, jnp.zeros((1, LANES - members), F32)], axis=1)
        c_ref[k] = jnp.transpose(jnp.broadcast_to(row, (LANES, LANES)))
    j = lax.axis_index("gy")
    own = pl.ds(pl.multiple_of(j * half, half), half)

    def wide(k, rows, width):
        return jnp.concatenate([c_ref[k, rows, :]] * (width // LANES), axis=1)

    xf_ref[...] = (
        wide(0, own, frac_cells) * f0_ref[...]
        + wide(1, own, frac_cells) * f1_ref[...]
        + wide(2, own, frac_cells) * f2_ref[...]
    )

    copies = fetch((xf_ref,), (xf_hbm,), sems)
    pieces = sems.shape[0] - 1
    piece = members // pieces
    for index in range(pieces):

        @pl.loop(index * piece, (index + 1) * piece)
        def _(m):
            rows = pl.ds(m, 1)
            x_ref[m] = (
                wide(0, rows, y_cells) * v0_ref[m]
                + wide(1, rows, y_cells) * v1_ref[m]
                + wide(2, rows, y_cells) * v2_ref[m]
            )

        part = pl.ds(index * piece, piece)
        copies.append(pltpu.make_async_copy(x_ref.at[part], x_hbm.at[part], sems.at[1 + index]))
        copies[-1].start()
    for copy in copies:
        copy.wait()


def pairs_of(count, stride, phase):
    out = []
    for index in range(count):
        if (index // stride) % 2 == phase:
            mate = (index + stride) % count
            out += [(index, mate), (mate, index)]
    return out


VMEM = pl.BlockSpec(memory_space=pltpu.VMEM)


HBM = pl.BlockSpec(memory_space=pltpu.HBM)


def call(kernel, name, args, outs, scratch=(), far_in=0, far_out=False, cost=None, aliases=None):
    args = [pltpu.with_memory_space_constraint(arg, pltpu.HBM) for arg in args[:far_in]] + list(args[far_in:])
    return pl.pallas_call(
        kernel,
        name=name,
        out_shape=[jax.ShapeDtypeStruct(shape, dtype) for shape, dtype in outs],
        in_specs=[HBM] * far_in + [VMEM] * (len(args) - far_in),
        out_specs=[HBM if far_out else VMEM] * len(outs),
        scratch_shapes=list(scratch),
        compiler_params=pltpu.CompilerParams(vmem_limit_bytes=40 * 1024 * 1024),
        cost_estimate=cost,
        input_output_aliases=aliases or {},
    )(*args)


def per_device(
    source_matrix,
    source_fracture,
    aperture,
    storage,
    perm_class,
    class_perm,
    send_slots,
    isect_local,
    isect_other,
    isect_count,
    ov_cell,
    ov_frac,
    ov_weight,
    ov_count,
):
    members, x_cells, y_cells = source_matrix.shape
    half, frac_cells = source_fracture.shape
    slots = send_slots.shape[1]
    rows = isect_local.size
    margin = ov_cell.size
    count = lax.axis_size("gx")

    def near(to_a, to_b):
        return (
            lax.ppermute(to_a, "gx", pairs_of(count, 1, 0)),
            lax.ppermute(to_b, "gx", pairs_of(count, 1, 1)),
        )

    def far(value):
        return (
            lax.ppermute(value, "gx", pairs_of(count, 2, 0)),
            lax.ppermute(value, "gx", pairs_of(count, 2, 1)),
        )

    def core(value):
        return lax.ppermute(value, "gy", [(0, 1), (1, 0)])

    blocks = y_cells // LANES
    frac_blocks = frac_cells // LANES
    field = (members, x_cells, y_cells)
    own = (half, frac_cells)
    hidden = pl.CostEstimate(flops=4_000_000_000, bytes_accessed=12_000_000, transcendentals=0)
    perm, cond, oslot, to_a, to_b, sent, border = call(
        opening_kernel,
        "opening",
        (class_perm, perm_class, aperture, send_slots),
        [
            ((x_cells, y_cells), F32),
            (own, F32),
            ((frac_cells, slots), BF16),
            ((half + 8 * (-(-blocks // 8)), LANES), F32),
            ((half + 8 * (-(-blocks // 8)), LANES), F32),
            ((half, slots), F32),
            ((x_cells, LANES), F32),
        ],
        scratch=[
            pltpu.SMEM(class_perm.shape, F32),
            pltpu.VMEM(perm_class.shape, jnp.int32),
            pltpu.VMEM(aperture.shape, F32),
            pltpu.VMEM(send_slots.shape, jnp.int32),
            pltpu.SemaphoreType.DMA((4,)),
        ],
        far_in=4,
    )

    def exchange(to_a, to_b, sent, to_core):
        near_a, near_b = near(to_a, to_b)
        core_in = core(to_core)
        sent, core_in = lax.optimization_barrier((sent, core_in))
        far_c, far_d = far(sent)
        return near_a, near_b, far_c, far_d, core_in

    near_a, near_b, far_c, far_d, border = exchange(to_a, to_b, sent, border)
    source_f, live, edges, coef, oy, ox, weight, first, second, table, ghost_table, ofrac, v0, margin_in, column = call(
        inside_kernel,
        "inside",
        (
            ov_count.reshape(-1),
            isect_count,
            storage,
            source_matrix,
            source_fracture,
            ov_cell.reshape(-1, LANES),
            ov_weight.reshape(-1, LANES),
            isect_local,
            isect_other,
            ov_frac.reshape(-1, LANES),
            perm,
            border,
            oslot,
        ),
        [
            (own, F32),
            ((1, rows), F32),
            ((2, members, y_cells), F32),
            ((5, x_cells, y_cells), F32),
            ((y_cells, margin), BF16),
            ((x_cells, margin), F32),
            ((1, margin), F32),
            ((frac_cells, rows), BF16),
            ((frac_cells, rows), BF16),
            ((frac_cells, rows + slots), BF16),
            ((slots, rows), BF16),
            ((frac_cells, margin), BF16),
            (field, F32),
            ((members, margin), F32),
            ((x_cells, LANES), F32),
        ],
        scratch=[
            pltpu.SMEM((ov_count.size,), jnp.int32),
            pltpu.SMEM(isect_count.shape, jnp.int32),
            pltpu.VMEM(storage.shape, F32),
            pltpu.VMEM(field, F32),
            pltpu.VMEM((margin // LANES, LANES), jnp.int32),
            pltpu.VMEM((margin // LANES, LANES), F32),
            pltpu.VMEM(isect_local.shape, jnp.int32),
            pltpu.VMEM(isect_other.shape, jnp.int32),
            pltpu.VMEM((margin // LANES, LANES), jnp.int32),
            pltpu.SemaphoreType.DMA((10,)),
        ],
        far_in=10,
        cost=hidden,
    )
    core_rows = 2 * frac_blocks * half + x_cells
    edge_rows = blocks * members
    unit, f0, sr, scale_f, diff, wown, to_a, to_b, sent, core_msg, v0 = call(
        first_kernel,
        "first_vector",
        (
            live,
            coef,
            perm,
            cond,
            edges,
            source_f,
            weight,
            near_a,
            near_b,
            far_c,
            far_d,
            first,
            second,
            table,
            ghost_table,
            ofrac,
            oy,
            ox,
            margin_in,
            column,
            v0,
        ),
        [
            ((6, x_cells, y_cells), F32),
            (own, F32),
            ((half, rows), F32),
            ((2, half, frac_cells), F32),
            ((half, rows), F32),
            (own, F32),
            ((edge_rows + 3 * half, LANES), F32),
            ((edge_rows + 3 * half, LANES), F32),
            ((3 * half, LANES), F32),
            ((core_rows + 8 * frac_blocks, LANES), F32),
            (field, F32),
        ],
        scratch=[pltpu.VMEM((members, frac_cells), F32)],
        aliases={20: 10},
    )
    near_rows = edge_rows + 2 * half

    def interior(power, v, before, vf, before_f, core_in):
        outs = []
        if power < 3:
            outs = [(field, F32), ((members, margin), F32), ((x_cells, LANES), F32)]
        return call(
            functools.partial(interior_kernel, power),
            f"interior_{power}",
            (v, before, vf, before_f, core_in, scale_f, unit, weight, ofrac, oy, ox),
            outs + [((8, members), F32)],
            scratch=[pltpu.VMEM((members, margin), F32), pltpu.VMEM((members, frac_cells), F32)]
            + [pltpu.VMEM((members, LANES), F32)] * power,
            cost=hidden,
        )

    finish_outs = [
        (own, F32),
        ((half, rows), F32),
        (own, F32),
        ((near_rows, LANES), F32),
        ((near_rows, LANES), F32),
        ((2 * half, LANES), F32),
        ((core_rows, LANES), F32),
        (field, F32),
    ]
    finish_scratch = [pltpu.VMEM((members, frac_cells), F32)]

    near_a, near_b, far_c, far_d, core_in = exchange(to_a, to_b, sent, core_msg)
    image, margin_in, column, dots1 = interior(1, v0, v0, f0, f0, core_in)
    own_f, f1, diff, wown, to_a, to_b, sent, core_msg, v1 = call(
        functools.partial(finish_kernel, 1),
        "finish_1",
        (f0, near_a, near_b, far_c, far_d, core_in, diff, wown, sr, scale_f, unit, table, ghost_table)
        + (weight, ofrac, oy, ox, margin_in, column, image),
        [(own, F32)] + finish_outs,
        scratch=finish_scratch,
        aliases={19: 8},
    )
    near_a, near_b, far_c, far_d, core_in = exchange(to_a, to_b, sent, core_msg)
    image, margin_in, column, dots2 = interior(2, v1, v0, f1, f0, core_in)
    f2, diff, wown, to_a, to_b, sent, core_msg, v2 = call(
        functools.partial(finish_kernel, 2),
        "finish_2",
        (f1, near_a, near_b, far_c, far_d, core_in, diff, wown, sr, scale_f, unit, table, ghost_table)
        + (own_f, weight, ofrac, oy, ox, margin_in, column, image),
        finish_outs,
        scratch=finish_scratch,
        aliases={20: 7},
    )
    near_a, near_b, far_c, far_d, core_in = exchange(to_a, to_b, sent, core_msg)
    (dots3,) = interior(3, v2, v1, f2, f1, core_in)
    peers = count * lax.axis_size("gy")
    (moments,) = call(
        functools.partial(finish_kernel, 3),
        "finish_3",
        (f2, near_a, near_b, far_c, far_d, core_in, diff, wown, sr, scale_f, unit, table, ghost_table)
        + (own_f, v2, dots1, dots2, dots3),
        [((peers, 2, LANES), F32)],
        scratch=[pltpu.VMEM((members, LANES), F32)],
    )
    totals = lax.all_to_all(moments, ("gx", "gy"), 0, 0)
    return call(
        close_kernel,
        "iterate",
        (totals, v0, v1, v2, f0, f1, f2),
        [(field, F32), (own, F32)],
        scratch=[
            pltpu.VMEM((3, LANES, LANES), F32),
            pltpu.VMEM(field, F32),
            pltpu.VMEM(own, F32),
            pltpu.SemaphoreType.DMA((5,)),
        ],
        far_out=True,
    )


def solution(mesh):
    placed = (
        P("grp", "gx", "gy"),
        P(("grp", "gy"), "gx"),
        P(("grp", "gy"), "gx"),
        P("gx", "gy"),
        P("gx", "gy"),
        P(),
        P("gx", None),
        P("gx", None),
        P("gx", None),
        P("gx"),
        P("gx", "gy", None, None),
        P("gx", "gy", None, None),
        P("gx", "gy", None, None),
        P("gx", "gy", None),
    )
    return jax.shard_map(
        per_device,
        mesh=mesh,
        in_specs=placed,
        out_specs=(P("grp", "gx", "gy"), P(("grp", "gy"), "gx")),
        check_vma=False,
    )
```

```python
import functools

import jax
import jax.numpy as jnp
from jax import lax
from jax.experimental import pallas as pl
from jax.experimental.pallas import tpu as pltpu
from jax.sharding import PartitionSpec as P

FRACTURE_STORAGE = 0.1
F32 = jnp.float32
BF16 = jnp.bfloat16
LANES = 128
GROUP = 16


def split3(x):
    high = x.astype(BF16)
    rest = x - high.astype(F32)
    mid = rest.astype(BF16)
    low = (rest - mid.astype(F32)).astype(BF16)
    return jnp.concatenate([high, mid, low], axis=0)


def pick(x, table, transposed=False):
    rows = x.shape[0]
    dims = (((1,), (1 if transposed else 0,)), ((), ()))
    out = lax.dot_general(split3(x), table, dims, preferred_element_type=F32)
    return out[:rows] + out[rows : 2 * rows] + out[2 * rows :]


def fetch(sources, targets, sems):
    copies = [pltpu.make_async_copy(a, b, sems.at[k]) for k, (a, b) in enumerate(zip(sources, targets))]
    for copy in copies:
        copy.start()
    return copies


class Place:
    def __init__(self):
        count = lax.axis_size("gx")
        i = lax.axis_index("gx")
        self.j = lax.axis_index("gy")
        self.high_side = self.j == 0
        self.even = lax.rem(i, 2) == 0
        self.low_pair = lax.rem(lax.div(i, 2), 2) == 0
        self.first = i == 0
        self.last = i == count - 1


def harmonic(first_perm, second_perm):
    return 2.0 * first_perm * second_perm / (first_perm + second_perm)


def one_hot(index_row, size):
    shape = (size, index_row.shape[1])
    ids = lax.broadcasted_iota(jnp.int32, shape, 0)
    return jnp.where(ids == index_row, 1.0, 0.0).astype(BF16)


def to_blocks(x):
    return jnp.concatenate(
        [x[:, q : q + LANES] for q in range(0, x.shape[1], LANES)], axis=0
    )


def from_blocks(x, rows):
    return jnp.concatenate(
        [x[q : q + rows] for q in range(0, x.shape[0], rows)], axis=1
    )


def by_group(first, second, third, fourth):
    group = first.shape[1] // 4
    lane = lax.broadcasted_iota(jnp.int32, first.shape, 1)
    return jnp.where(
        lane < group,
        first,
        jnp.where(lane < 2 * group, second, jnp.where(lane < 3 * group, third, fourth)),
    )


def total_rows(x):
    return jnp.sum(jnp.transpose(x), axis=0, keepdims=True)


def fold_lanes(x):
    rows, width = x.shape
    out = x[:, :LANES]
    for q in range(LANES, width, LANES):
        out = out + x[:, q : q + LANES]
    return out


def opening_kernel(
    perm_table_hbm,
    class_hbm,
    aperture_hbm,
    slots_hbm,
    perm_ref,
    cond_ref,
    oslot_ref,
    near_a_ref,
    near_b_ref,
    far_ref,
    border_ref,
    perm_table_ref,
    class_ref,
    aperture_ref,
    slots_ref,
    sems,
):
    copies = fetch(
        (class_hbm, perm_table_hbm, aperture_hbm, slots_hbm),
        (class_ref, perm_table_ref, aperture_ref, slots_ref),
        sems,
    )
    for copy in copies:
        copy.wait()
    x_cells, y_cells = class_ref.shape
    half = aperture_ref.shape[0]
    here = Place()
    classes = class_ref[...]
    perm = jnp.zeros(classes.shape, F32)
    for index in range(perm_table_ref.shape[0]):
        perm = jnp.where(classes == index, perm_table_ref[index], perm)
    perm_ref[...] = perm
    border_ref[...] = jnp.where(here.high_side, perm[:, y_cells - LANES :], perm[:, :LANES])

    aperture = aperture_ref[...]
    cond = aperture * aperture * aperture
    cond_ref[...] = cond
    oslot = one_hot(slots_ref[...], cond.shape[1])
    oslot_ref[...] = oslot
    supplied = pick(cond, oslot)
    far_ref[...] = supplied
    up, down = to_blocks(perm[x_cells - 1 :]), to_blocks(perm[:1])
    blocks = up.shape[0]
    pad = jnp.zeros((near_a_ref.shape[0] - half - blocks, LANES), F32)
    for ref, edge in ((near_a_ref, jnp.where(here.even, up, down)), (near_b_ref, jnp.where(here.even, down, up))):
        ref[...] = jnp.concatenate([supplied, edge, pad], axis=0)


def neighbours(here, near_a_ref, near_b_ref, far_c_ref, far_d_ref):
    def reader(flag, at_zero, at_one):
        return lambda at, size: jnp.where(
            flag, at_zero[at : at + size, :], at_one[at : at + size, :]
        )

    return (
        reader(here.even, near_a_ref, near_b_ref),
        reader(here.even, near_b_ref, near_a_ref),
        reader(here.low_pair, far_c_ref, far_d_ref),
        reader(here.low_pair, far_d_ref, far_c_ref),
    )


def margin_values(found, ox):
    found = found.reshape(-1, *ox.shape) * ox[None]
    return jnp.sum(found, axis=1)


def border_column(tile_low, tile_high, high_side, m):
    tile = jnp.where(high_side, tile_high, tile_low)
    return pltpu.roll(tile, jnp.where(high_side, lax.rem(m + 1, LANES), m), 1)


def border_row(row_values, high_side):
    members, y_cells = row_values.shape
    tile = jnp.where(high_side, row_values[:, y_cells - LANES :], row_values[:, :LANES])
    turned = jnp.transpose(tile)
    line = jnp.where(high_side, turned[LANES - 1 :], turned[:1])
    return jnp.concatenate([line, jnp.zeros((1, LANES - members), F32)], axis=1)


def finish_edges(high_rows, low_rows, partial_ref, column, high_side, oy, ox):
    members = high_rows.shape[0]
    x_cells = ox.shape[0]
    found = pick(jnp.concatenate([high_rows, low_rows], axis=0), oy)
    margin = partial_ref[...] + found[:members] * ox[x_cells - 1 :] + found[members:] * ox[:1]
    row = lax.broadcasted_iota(jnp.int32, column.shape, 0)
    column = jnp.where(row == x_cells - 1, border_row(high_rows, high_side), column)
    return margin, jnp.where(row == 0, border_row(low_rows, high_side), column)


def send_network(vf, sr, table, ghost_table, diff_ref, refs):
    half = vf.shape[0]
    rows = diff_ref.shape[1]
    found = pick(vf, table)
    diff_ref[...] = found[:, :rows]
    if sr is None:
        for ref, at in refs:
            ref[at : at + half, :] = found[:, rows:]
        return
    sums = pick(sr * found[:, :rows], ghost_table, True)
    for ref, at in refs:
        ref[at : at + half, :] = found[:, rows:]
        ref[at + half : at + 2 * half, :] = sums


def send_core(core_ref, vf, margin, weight, ofrac, column, j, work_ref, wown_ref):
    half, frac_cells = vf.shape
    work_ref[...] = pick(margin * weight, ofrac, True)
    wown_ref[...] = work_ref[pl.ds(pl.multiple_of(j * half, half), half), :]
    other = work_ref[pl.ds(pl.multiple_of((1 - j) * half, half), half), :]
    size = frac_cells // LANES * half
    core_ref[0:size, :] = to_blocks(vf)
    core_ref[size : 2 * size, :] = to_blocks(other)
    core_ref[2 * size : 2 * size + column.shape[0], :] = column


def inside_kernel(
    ov_count_hbm,
    isect_count_hbm,
    storage_hbm,
    source_hbm,
    source_f_hbm,
    cell_hbm,
    ov_weight_hbm,
    local_hbm,
    other_hbm,
    frac_hbm,
    perm_ref,
    border_ref,
    oslot_ref,
    source_f_ref,
    storage_ref,
    live_ref,
    edge_ref,
    coef_ref,
    oy_ref,
    ox_ref,
    weight_ref,
    first_ref,
    second_ref,
    table_ref,
    ghost_table_ref,
    ofrac_ref,
    v_ref,
    margin_ref,
    column_ref,
    ov_count_ref,
    isect_count_ref,
    source_ref,
    cell_ref,
    ov_weight_ref,
    local_ref,
    other_in_ref,
    frac_ref,
    sems,
):
    members, x_cells, y_cells = source_ref.shape
    frac_cells = table_ref.shape[0]
    here = Place()
    high_side = here.high_side
    copies = fetch(
        (
            cell_hbm,
            local_hbm,
            other_hbm,
            frac_hbm,
            ov_weight_hbm,
            ov_count_hbm,
            isect_count_hbm,
            storage_hbm,
            source_f_hbm,
            source_hbm,
        ),
        (
            cell_ref,
            local_ref,
            other_in_ref,
            frac_ref,
            ov_weight_ref,
            ov_count_ref,
            isect_count_ref,
            storage_ref,
            source_f_ref,
            source_ref,
        ),
        sems,
    )

    def line(ref):
        return jnp.concatenate([ref[k : k + 1, :] for k in range(ref.shape[0])], axis=1)

    rows = local_ref.size
    perm, border = perm_ref[...], border_ref[...]
    col = jnp.where(high_side, border[:, :1], border[:, LANES - 1 :])
    lane = lax.broadcasted_iota(jnp.int32, perm.shape, 1)
    row = lax.broadcasted_iota(jnp.int32, perm.shape, 0)
    north = jnp.concatenate([perm[:, 1:], col], axis=1)
    south = jnp.concatenate([col, perm[:, :-1]], axis=1)
    tn = jnp.where((lane == y_cells - 1) & jnp.logical_not(high_side), 0.0, harmonic(perm, north))
    ts = jnp.where((lane == 0) & high_side, 0.0, harmonic(perm, south))
    east = jnp.concatenate([perm[1:], perm[:1]], axis=0)
    west = jnp.concatenate([perm[-1:], perm[:-1]], axis=0)
    te = jnp.where(row == x_cells - 1, 0.0, harmonic(perm, east))
    tw = jnp.where(row == 0, 0.0, harmonic(perm, west))
    for copy in copies[:-1]:
        copy.wait()
    cell = line(cell_ref)
    oy = one_hot(cell % y_cells, y_cells)
    oy_ref[...] = oy
    row_x = lax.broadcasted_iota(jnp.int32, ox_ref.shape, 0)
    at_x = row_x == cell // y_cells
    ox = jnp.where(at_x, 1.0, 0.0)
    ox_ref[...] = ox
    lane_w = lax.broadcasted_iota(jnp.int32, (1, LANES), 1)
    weight = jnp.concatenate(
        [jnp.where(lane_w < ov_count_ref[k], ov_weight_ref[k : k + 1, :], 0.0) for k in range(ov_weight_ref.shape[0])],
        axis=1,
    )
    weight_ref[...] = weight
    for block in range(local_ref.shape[0]):
        at = slice(block * LANES, (block + 1) * LANES)
        live_ref[:, at] = jnp.where(lane_w < isect_count_ref[block], 1.0, 0.0)
    part = storage_ref[...] + te + tw + tn + ts + pick(jnp.where(at_x, weight, 0.0), oy, True)
    coef_ref[0] = te
    coef_ref[1] = tw
    coef_ref[2] = tn
    coef_ref[3] = ts
    coef_ref[4] = part

    other = line(other_in_ref)
    first, second = one_hot(line(local_ref), frac_cells), one_hot(other, frac_cells)
    first_ref[...] = first
    second_ref[...] = second
    table_ref[:, :rows] = first - second
    table_ref[:, rows:] = oslot_ref[...]
    ghost_table_ref[...] = one_hot(other - frac_cells, ghost_table_ref.shape[0])
    ofrac_ref[...] = one_hot(line(frac_ref), frac_cells)

    inverse = 1.0 / part
    inner_x = jnp.where((row_x == 0) | (row_x == x_cells - 1), 0.0, ox)
    lane_c = lax.broadcasted_iota(jnp.int32, (x_cells, LANES), 1)
    column_ref[...] = jnp.zeros_like(column_ref)
    copies[-1].wait()
    edge_ref[0] = source_ref[:, x_cells - 1, :]
    edge_ref[1] = source_ref[:, 0, :]

    @pl.loop(0, members // GROUP)
    def _(index):
        start = index * GROUP
        block = source_ref[pl.ds(start, GROUP)] * inverse[None]
        v_ref[pl.ds(start, GROUP)] = block
        found = pick(block.reshape(GROUP * x_cells, y_cells), oy_ref[...])
        margin_ref[pl.ds(start, GROUP), :] = margin_values(found, inner_x)
        column = column_ref[...]
        for k in range(GROUP):
            m = start + k
            moved = border_column(block[k, :, :LANES], block[k, :, y_cells - LANES :], high_side, m)
            column = jnp.where(lane_c == m, moved, column)
        column_ref[...] = column


def first_kernel(
    live_ref,
    coef_ref,
    perm_ref,
    cond_ref,
    edge_ref,
    source_f_ref,
    weight_ref,
    near_a_ref,
    near_b_ref,
    far_c_ref,
    far_d_ref,
    first_ref,
    second_ref,
    table_ref,
    ghost_table_ref,
    ofrac_ref,
    oy_ref,
    ox_ref,
    inner_margin_ref,
    inner_column_ref,
    v_in_ref,
    unit_ref,
    vf_ref,
    sr_ref,
    scale_f_ref,
    diff_ref,
    wown_ref,
    to_a_ref,
    to_b_ref,
    sent_ref,
    core_ref,
    v_ref,
    work_ref,
):
    members, x_cells, y_cells = v_ref.shape
    half, frac_cells = source_f_ref.shape
    blocks = y_cells // LANES
    here = Place()
    j, high_side = here.j, here.high_side
    base = blocks * members
    plus1, minus1, plus2, minus2 = neighbours(here, near_a_ref, near_b_ref, far_c_ref, far_d_ref)

    ghosts = by_group(minus1(0, half), plus1(0, half), minus2(0, half), plus2(0, half))
    table, ghost_table = table_ref[...], ghost_table_ref[...]
    cond = cond_ref[...]
    cond_first = pick(cond, first_ref[...])
    cond_second = pick(cond, second_ref[...]) + pick(ghosts, ghost_table)
    sr = jnp.where(live_ref[...] > 0.0, harmonic(cond_first, cond_second), 0.0)
    sr_ref[...] = sr
    diag_f = FRACTURE_STORAGE + pick(sr, first_ref[...], True)
    inverse_f = 1.0 / diag_f
    scale_f_ref[0] = inverse_f
    scale_f_ref[1] = diag_f
    vf = source_f_ref[...] * inverse_f
    vf_ref[...] = vf
    refs = [(to_a_ref, base), (to_b_ref, base), (sent_ref, 0)]
    send_network(vf, sr, table, ghost_table, diff_ref, refs)
    slot_sums = pick(sr, ghost_table, True)
    for ref, at in refs:
        ref[at + 2 * half : at + 3 * half, :] = slot_sums

    perm, part = perm_ref[...], coef_ref[4]
    row = lax.broadcasted_iota(jnp.int32, perm.shape, 0)
    perm_plus = from_blocks(plus1(half, blocks), 1)
    perm_minus = from_blocks(minus1(half, blocks), 1)
    te_edge = jnp.where(here.last, 0.0, harmonic(perm[x_cells - 1 :], perm_plus))
    tw_edge = jnp.where(here.first, 0.0, harmonic(perm[:1], perm_minus))
    te = jnp.where(row == x_cells - 1, te_edge, coef_ref[0])
    tw = jnp.where(row == 0, tw_edge, coef_ref[1])
    diag = part + jnp.where(row == x_cells - 1, te_edge, 0.0) + jnp.where(row == 0, tw_edge, 0.0)
    inverse = 1.0 / diag
    unit_ref[0] = te * inverse
    unit_ref[1] = tw * inverse
    unit_ref[2] = coef_ref[2] * inverse
    unit_ref[3] = coef_ref[3] * inverse
    unit_ref[4] = inverse
    unit_ref[5] = diag
    high_rows = edge_ref[0] * inverse[x_cells - 1 :]
    low_rows = edge_ref[1] * inverse[:1]
    v_ref[:, x_cells - 1, :] = high_rows
    v_ref[:, 0, :] = low_rows
    to_a_ref[0:base, :] = to_blocks(jnp.where(here.even, high_rows, low_rows))
    to_b_ref[0:base, :] = to_blocks(jnp.where(here.even, low_rows, high_rows))
    margin, column = finish_edges(
        high_rows, low_rows, inner_margin_ref, inner_column_ref[...], high_side, oy_ref[...], ox_ref[...]
    )
    weight = weight_ref[...]
    send_core(core_ref, vf, margin, weight, ofrac_ref[...], column, j, work_ref, wown_ref)
    wsum = pick(jnp.broadcast_to(weight, (8, weight.shape[1])), ofrac_ref[...], True)
    tail = core_ref.shape[0] - 8 * (frac_cells // LANES)
    core_ref[tail:, :] = to_blocks(wsum)


def interior_kernel(
    power,
    v_ref,
    before_ref,
    vf_ref,
    before_f_ref,
    core_ref,
    scale_f_ref,
    unit_ref,
    weight_ref,
    ofrac_ref,
    oy_ref,
    ox_ref,
    *refs,
):
    image_ref, margin_ref, column_ref, dots_ref, flow_ref, work_ref, *acc_refs = refs
    members, x_cells, y_cells = v_ref.shape
    half, frac_cells = vf_ref.shape
    blocks = y_cells // LANES
    here = Place()
    j, high_side = here.j, here.high_side
    size = frac_cells // LANES * half
    theirs = from_blocks(core_ref[0:size, :], half)
    column_in = core_ref[2 * size : 2 * size + x_cells, :]
    vf = vf_ref[...]
    own_rows = pl.ds(pl.multiple_of(j * half, half), half)
    work_ref[own_rows, :] = vf
    work_ref[pl.ds(pl.multiple_of((1 - j) * half, half), half), :] = theirs
    flow_ref[...] = pick(work_ref[...], ofrac_ref[...]) * weight_ref[...]

    heavy_f = vf * scale_f_ref[1]
    for ref in acc_refs:
        ref[...] = jnp.zeros_like(ref)
    acc_refs[0][own_rows, :] = fold_lanes(vf * heavy_f)
    if power > 1:
        acc_refs[1][own_rows, :] = fold_lanes(before_f_ref[...] * heavy_f)

    lane_c = lax.broadcasted_iota(jnp.int32, (x_cells, LANES), 1)
    lane = lax.broadcasted_iota(jnp.int32, (x_cells, y_cells), 1)
    row = lax.broadcasted_iota(jnp.int32, (x_cells, y_cells), 0)
    row_x = lax.broadcasted_iota(jnp.int32, ox_ref.shape, 0)
    oy, ox = oy_ref[...], ox_ref[...]
    inner_x = jnp.where((row_x == 0) | (row_x == x_cells - 1), 0.0, ox)
    te = jnp.where(row == x_cells - 1, 0.0, unit_ref[0])
    tw = jnp.where(row == 0, 0.0, unit_ref[1])
    column_ref[...] = jnp.zeros_like(column_ref)

    @pl.loop(0, members // GROUP)
    def _(index):
        start = index * GROUP
        parts = []
        for k in range(GROUP):
            parts.append(ox * flow_ref[pl.ds(start + k, 1), :])
        coupled = pick(jnp.concatenate(parts, axis=0), oy, True)
        column = column_ref[...]
        for k in range(GROUP):
            m = start + k
            value = v_ref[m]
            east = pltpu.roll(value, x_cells - 1, 0)
            west = pltpu.roll(value, 1, 0)
            moved = pltpu.roll(column_in, jnp.where(high_side, LANES - 1 - m, lax.rem(LANES - m, LANES)), 1)
            moved = jnp.concatenate([moved] * blocks, axis=1)
            north = jnp.where(lane == y_cells - 1, moved, pltpu.roll(value, y_cells - 1, 1))
            south = jnp.where(lane == 0, moved, pltpu.roll(value, 1, 1))
            image = value - te * east - tw * west - unit_ref[2] * north - unit_ref[3] * south
            image = image - coupled[k * x_cells : (k + 1) * x_cells] * unit_ref[4]
            heavy = value * unit_ref[5]
            at = pl.ds(m, 1)
            acc_refs[0][at, :] += jnp.sum(fold_lanes(value * heavy), axis=0, keepdims=True)
            if power > 1:
                acc_refs[1][at, :] += jnp.sum(fold_lanes(before_ref[m] * heavy), axis=0, keepdims=True)
            image_ref[m] = image
            shifted = border_column(image[:, :LANES], image[:, y_cells - LANES :], high_side, m)
            column = jnp.where(lane_c == m, shifted, column)
        column_ref[...] = column
        block = image_ref[pl.ds(start, GROUP)]
        found = pick(block.reshape(GROUP * x_cells, y_cells), oy)
        margin_ref[pl.ds(start, GROUP), :] = margin_values(found, inner_x)

    dots = [total_rows(ref[...]) for ref in acc_refs]
    dots.append(jnp.zeros((8 - len(dots), members), F32))
    dots_ref[...] = jnp.concatenate(dots, axis=0)


def finish_kernel(
    power,
    vf_ref,
    near_a_ref,
    near_b_ref,
    far_c_ref,
    far_d_ref,
    core_in_ref,
    diff_in_ref,
    wown_in_ref,
    sr_ref,
    scale_f_ref,
    unit_ref,
    table_ref,
    ghost_table_ref,
    *refs,
):
    if power == 2:
        own_f_in_ref, *refs = refs
    weight_ref, ofrac_ref, oy_ref, ox_ref, inner_margin_ref, inner_column_ref, image_in_ref, *refs = refs
    if power == 1:
        own_f_ref, out_f_ref, diff_ref, wown_ref, to_a_ref, to_b_ref, sent_ref, core_ref, image_ref, work_ref = refs
    else:
        out_f_ref, diff_ref, margin_ref, to_a_ref, to_b_ref, sent_ref, core_ref, image_ref = refs
    half, frac_cells = vf_ref.shape
    x_cells, y_cells = unit_ref.shape[1:]
    members = image_ref.shape[0]
    blocks = y_cells // LANES
    frac_blocks = frac_cells // LANES
    here = Place()
    j, high_side = here.j, here.high_side
    base = blocks * members
    plus1, minus1, plus2, minus2 = neighbours(here, near_a_ref, near_b_ref, far_c_ref, far_d_ref)
    rows = sr_ref.shape[1]

    table, ghost_table = table_ref[...], ghost_table_ref[...]
    vf = vf_ref[...]
    ghosts = by_group(minus1(base, half), plus1(base, half), minus2(0, half), plus2(0, half))
    sums = by_group(
        plus1(base + half, half), minus1(base + half, half), plus2(half, half), minus2(half, half)
    )
    size = frac_blocks * half
    their_sums = from_blocks(core_in_ref[size : 2 * size, :], half)
    if power == 1:
        at = 2 * half
        back = by_group(
            plus1(base + at, half), minus1(base + at, half), plus2(at, half), minus2(at, half)
        )
        weight = weight_ref[...]
        wsum = pick(jnp.broadcast_to(weight, (8, weight.shape[1])), ofrac_ref[...], True)
        tail = core_in_ref.shape[0] - 8 * frac_blocks
        wsum = wsum + from_blocks(core_in_ref[tail:, :], 8)
        own_f = FRACTURE_STORAGE + wsum[:1] + pick(back, table[:, rows:], True)
        own_f_ref[...] = own_f
    else:
        own_f = own_f_in_ref[...]
    sr = sr_ref[...]
    flux = sr * (diff_in_ref[...] - pick(ghosts, ghost_table))
    image_f = own_f * vf + pick(jnp.concatenate([flux, -sums], axis=1), table, True)
    image_f = image_f - wown_in_ref[...] - their_sums

    next_f = image_f * scale_f_ref[0]
    out_f_ref[...] = next_f
    edge_size = base if power == 1 else base // 2
    refs = [(to_a_ref, edge_size), (to_b_ref, edge_size), (sent_ref, 0)]
    send_network(next_f, sr if power == 1 else None, table, ghost_table, diff_ref, refs)

    edges = []
    for side, at, reader in ((0, x_cells - 1, plus1), (1, 0, minus1)):
        beyond = from_blocks(reader(0, base), members)
        edge = image_in_ref[:, at, :] - unit_ref[side, at : at + 1, :] * beyond
        image_ref[:, at, :] = edge
        edges.append(edge)
    up, down = edges
    if power == 2:
        up, down = up[:, : y_cells // 2], down[:, y_cells // 2 :]
    to_a_ref[0:edge_size, :] = to_blocks(jnp.where(here.even, up, down))
    to_b_ref[0:edge_size, :] = to_blocks(jnp.where(here.even, down, up))
    margin, column = finish_edges(
        edges[0], edges[1], inner_margin_ref, inner_column_ref[...], high_side, oy_ref[...], ox_ref[...]
    )
    if power == 1:
        send_core(core_ref, next_f, margin, weight_ref[...], ofrac_ref[...], column, j, work_ref, wown_ref)
    else:
        margin_ref[...] = margin
        core_ref[0:size, :] = to_blocks(next_f)
        core_ref[size : size + x_cells, :] = column


def energy_kernel(
    v_ref,
    before_ref,
    vf_ref,
    before_f_ref,
    core_ref,
    scale_f_ref,
    unit_ref,
    coef_ref,
    storage_ref,
    weight_ref,
    ofrac_ref,
    margin_ref,
    dots_ref,
    work_ref,
    acc0_ref,
    acc1_ref,
    acc2_ref,
):
    members, x_cells, y_cells = v_ref.shape
    half, frac_cells = vf_ref.shape
    blocks = y_cells // LANES
    here = Place()
    size = frac_cells // LANES * half
    theirs = from_blocks(core_ref[0:size, :], half)
    column_in = core_ref[size : size + x_cells, :]
    vf = vf_ref[...]
    own_rows = pl.ds(pl.multiple_of(here.j * half, half), half)
    work_ref[own_rows, :] = vf
    work_ref[pl.ds(pl.multiple_of((1 - here.j) * half, half), half), :] = theirs
    gap = margin_ref[...] - pick(work_ref[...], ofrac_ref[...])
    acc2_ref[...] = fold_lanes(weight_ref[...] * gap * gap)
    heavy_f = vf * scale_f_ref[1]
    acc0_ref[...] = jnp.zeros_like(acc0_ref)
    acc1_ref[...] = jnp.zeros_like(acc1_ref)
    acc0_ref[own_rows, :] = fold_lanes(vf * heavy_f)
    acc1_ref[own_rows, :] = fold_lanes(before_f_ref[...] * heavy_f)
    lane = lax.broadcasted_iota(jnp.int32, (x_cells, y_cells), 1)
    diag, te, tn, storage = unit_ref[5], coef_ref[0], coef_ref[2], storage_ref[...]

    @pl.loop(0, members // GROUP)
    def _(index):
        start = index * GROUP
        for k in range(GROUP):
            m = start + k
            value = v_ref[m]
            east = value - pltpu.roll(value, x_cells - 1, 0)
            moved = pltpu.roll(column_in, LANES - 1 - m, 1)
            moved = jnp.concatenate([moved] * blocks, axis=1)
            north = value - jnp.where(lane == y_cells - 1, moved, pltpu.roll(value, y_cells - 1, 1))
            energy = storage * value * value + te * east * east + tn * north * north
            heavy = value * diag
            at = pl.ds(m, 1)
            acc0_ref[at, :] += jnp.sum(fold_lanes(value * heavy), axis=0, keepdims=True)
            acc1_ref[at, :] += jnp.sum(fold_lanes(before_ref[m] * heavy), axis=0, keepdims=True)
            acc2_ref[at, :] += jnp.sum(fold_lanes(energy), axis=0, keepdims=True)

    dots = [total_rows(ref[...]) for ref in (acc0_ref, acc1_ref, acc2_ref)]
    dots.append(jnp.zeros((8 - len(dots), members), F32))
    dots_ref[...] = jnp.concatenate(dots, axis=0)


def moments_kernel(
    vf_ref,
    near_a_ref,
    near_b_ref,
    far_c_ref,
    far_d_ref,
    diff_in_ref,
    sr_ref,
    unit_ref,
    ghost_table_ref,
    v_ref,
    dots1_ref,
    dots2_ref,
    dots3_ref,
    moments_ref,
    acc_ref,
):
    half = vf_ref.shape[0]
    members, x_cells, y_cells = v_ref.shape
    middle = y_cells // 2
    base = middle // LANES * members
    here = Place()
    plus1, minus1, plus2, minus2 = neighbours(here, near_a_ref, near_b_ref, far_c_ref, far_d_ref)
    vf = vf_ref[...]
    ghosts = by_group(minus1(base, half), plus1(base, half), minus2(0, half), plus2(0, half))
    gap = diff_in_ref[...] - pick(ghosts, ghost_table_ref[...])
    acc_ref[...] = jnp.zeros_like(acc_ref)
    own_rows = pl.ds(pl.multiple_of(here.j * half, half), half)
    acc_ref[own_rows, :] = fold_lanes(sr_ref[...] * gap * gap) + fold_lanes(FRACTURE_STORAGE * vf * vf)
    for side, at, reader, cut in (
        (0, x_cells - 1, plus1, slice(middle, y_cells)),
        (1, 0, minus1, slice(0, middle)),
    ):
        trans = unit_ref[side, at : at + 1, cut] * unit_ref[5, at : at + 1, cut]
        edge = v_ref[:, at, cut] - from_blocks(reader(0, base), members)
        acc_ref[...] += fold_lanes(trans * edge * edge)
    last = total_rows(acc_ref[...]) + dots3_ref[2:3, :]
    blank = jnp.zeros((1, LANES - 3 * members), F32)
    lines = [
        jnp.concatenate([dots1_ref[0:1, :], dots2_ref[1:2, :], dots2_ref[0:1, :], blank], axis=1),
        jnp.concatenate([dots3_ref[1:2, :], dots3_ref[0:1, :], last, blank], axis=1),
    ]
    lines = jnp.concatenate(lines, axis=0)
    moments_ref[...] = jnp.broadcast_to(lines[None], moments_ref.shape)


def close_kernel(totals_ref, v0_ref, v1_ref, v2_ref, f0_ref, f1_ref, f2_ref, x_hbm, xf_hbm, c_ref, x_ref, xf_ref, sems):
    members, x_cells, y_cells = v0_ref.shape
    half, frac_cells = f0_ref.shape

    total = jnp.sum(totals_ref[...], axis=0)
    m0, m1, m2, m3, m4, m5 = (
        total[k // 3 : k // 3 + 1, k % 3 * members : k % 3 * members + members] for k in range(6)
    )
    alpha0 = m0 / m1
    rz1 = m0 - 2.0 * alpha0 * m1 + alpha0 * alpha0 * m2
    beta1 = rz1 / m0
    a, b = 1.0 + beta1, -alpha0
    pap1 = a * a * m1 + 2.0 * a * b * m2 + b * b * m3
    alpha1 = rz1 / pap1
    e = -alpha0 - alpha1 * a
    g = -alpha1 * b
    rz2 = m0 + 2.0 * e * m1 + (e * e + 2.0 * g) * m2 + 2.0 * e * g * m3 + g * g * m4
    beta2 = rz2 / rz1
    c = 1.0 + beta2 * a
    d = e + beta2 * b
    pap2 = c * c * m1 + 2.0 * c * d * m2 + (d * d + 2.0 * c * g) * m3 + 2.0 * d * g * m4 + g * g * m5
    alpha2 = rz2 / pap2
    c0 = alpha0 + alpha1 * a + alpha2 * c
    c1 = alpha1 * b + alpha2 * d
    c2 = alpha2 * g
    for k, row in enumerate((c0, c1, c2)):
        row = jnp.concatenate([row, jnp.zeros((1, LANES - members), F32)], axis=1)
        c_ref[k] = jnp.transpose(jnp.broadcast_to(row, (LANES, LANES)))
    j = lax.axis_index("gy")
    own = pl.ds(pl.multiple_of(j * half, half), half)

    def wide(k, rows, width):
        return jnp.concatenate([c_ref[k, rows, :]] * (width // LANES), axis=1)

    xf_ref[...] = (
        wide(0, own, frac_cells) * f0_ref[...]
        + wide(1, own, frac_cells) * f1_ref[...]
        + wide(2, own, frac_cells) * f2_ref[...]
    )

    copies = fetch((xf_ref,), (xf_hbm,), sems)
    pieces = sems.shape[0] - 1
    piece = members // pieces
    for index in range(pieces):

        @pl.loop(index * piece, (index + 1) * piece)
        def _(m):
            rows = pl.ds(m, 1)
            x_ref[m] = (
                wide(0, rows, y_cells) * v0_ref[m]
                + wide(1, rows, y_cells) * v1_ref[m]
                + wide(2, rows, y_cells) * v2_ref[m]
            )

        part = pl.ds(index * piece, piece)
        copies.append(pltpu.make_async_copy(x_ref.at[part], x_hbm.at[part], sems.at[1 + index]))
        copies[-1].start()
    for copy in copies:
        copy.wait()


def pairs_of(count, stride, phase):
    out = []
    for index in range(count):
        if (index // stride) % 2 == phase:
            mate = (index + stride) % count
            out += [(index, mate), (mate, index)]
    return out


VMEM = pl.BlockSpec(memory_space=pltpu.VMEM)


HBM = pl.BlockSpec(memory_space=pltpu.HBM)


def call(kernel, name, args, outs, scratch=(), far_in=0, far_out=False, cost=None, aliases=None):
    args = [pltpu.with_memory_space_constraint(arg, pltpu.HBM) for arg in args[:far_in]] + list(args[far_in:])
    return pl.pallas_call(
        kernel,
        name=name,
        out_shape=[jax.ShapeDtypeStruct(shape, dtype) for shape, dtype in outs],
        in_specs=[HBM] * far_in + [VMEM] * (len(args) - far_in),
        out_specs=[HBM if far_out else VMEM] * len(outs),
        scratch_shapes=list(scratch),
        compiler_params=pltpu.CompilerParams(vmem_limit_bytes=40 * 1024 * 1024),
        cost_estimate=cost,
        input_output_aliases=aliases or {},
    )(*args)


def per_device(
    source_matrix,
    source_fracture,
    aperture,
    storage,
    perm_class,
    class_perm,
    send_slots,
    isect_local,
    isect_other,
    isect_count,
    ov_cell,
    ov_frac,
    ov_weight,
    ov_count,
):
    members, x_cells, y_cells = source_matrix.shape
    half, frac_cells = source_fracture.shape
    slots = send_slots.shape[1]
    rows = isect_local.size
    margin = ov_cell.size
    count = lax.axis_size("gx")

    def near(to_a, to_b):
        return (
            lax.ppermute(to_a, "gx", pairs_of(count, 1, 0)),
            lax.ppermute(to_b, "gx", pairs_of(count, 1, 1)),
        )

    def far(value):
        return (
            lax.ppermute(value, "gx", pairs_of(count, 2, 0)),
            lax.ppermute(value, "gx", pairs_of(count, 2, 1)),
        )

    def core(value):
        return lax.ppermute(value, "gy", [(0, 1), (1, 0)])

    blocks = y_cells // LANES
    frac_blocks = frac_cells // LANES
    field = (members, x_cells, y_cells)
    own = (half, frac_cells)
    hidden = pl.CostEstimate(flops=4_000_000_000, bytes_accessed=12_000_000, transcendentals=0)
    perm, cond, oslot, to_a, to_b, sent, border = call(
        opening_kernel,
        "opening",
        (class_perm, perm_class, aperture, send_slots),
        [
            ((x_cells, y_cells), F32),
            (own, F32),
            ((frac_cells, slots), BF16),
            ((half + 8 * (-(-blocks // 8)), LANES), F32),
            ((half + 8 * (-(-blocks // 8)), LANES), F32),
            ((half, slots), F32),
            ((x_cells, LANES), F32),
        ],
        scratch=[
            pltpu.SMEM(class_perm.shape, F32),
            pltpu.VMEM(perm_class.shape, jnp.int32),
            pltpu.VMEM(aperture.shape, F32),
            pltpu.VMEM(send_slots.shape, jnp.int32),
            pltpu.SemaphoreType.DMA((4,)),
        ],
        far_in=4,
    )

    def exchange(to_a, to_b, sent, to_core):
        near_a, near_b = near(to_a, to_b)
        core_in = core(to_core)
        sent, core_in = lax.optimization_barrier((sent, core_in))
        far_c, far_d = far(sent)
        return near_a, near_b, far_c, far_d, core_in

    near_a, near_b, far_c, far_d, border = exchange(to_a, to_b, sent, border)
    source_f, storage_in, live, edges, coef, oy, ox, weight, first, second, table, ghost_table, ofrac, v0, margin_in, column = call(
        inside_kernel,
        "inside",
        (
            ov_count.reshape(-1),
            isect_count,
            storage,
            source_matrix,
            source_fracture,
            ov_cell.reshape(-1, LANES),
            ov_weight.reshape(-1, LANES),
            isect_local,
            isect_other,
            ov_frac.reshape(-1, LANES),
            perm,
            border,
            oslot,
        ),
        [
            (own, F32),
            ((x_cells, y_cells), F32),
            ((1, rows), F32),
            ((2, members, y_cells), F32),
            ((5, x_cells, y_cells), F32),
            ((y_cells, margin), BF16),
            ((x_cells, margin), F32),
            ((1, margin), F32),
            ((frac_cells, rows), BF16),
            ((frac_cells, rows), BF16),
            ((frac_cells, rows + slots), BF16),
            ((slots, rows), BF16),
            ((frac_cells, margin), BF16),
            (field, F32),
            ((members, margin), F32),
            ((x_cells, LANES), F32),
        ],
        scratch=[
            pltpu.SMEM((ov_count.size,), jnp.int32),
            pltpu.SMEM(isect_count.shape, jnp.int32),
            pltpu.VMEM(field, F32),
            pltpu.VMEM((margin // LANES, LANES), jnp.int32),
            pltpu.VMEM((margin // LANES, LANES), F32),
            pltpu.VMEM(isect_local.shape, jnp.int32),
            pltpu.VMEM(isect_other.shape, jnp.int32),
            pltpu.VMEM((margin // LANES, LANES), jnp.int32),
            pltpu.SemaphoreType.DMA((10,)),
        ],
        far_in=10,
        cost=hidden,
    )
    core_rows = 2 * frac_blocks * half + x_cells
    edge_rows = blocks * members
    unit, f0, sr, scale_f, diff, wown, to_a, to_b, sent, core_msg, v0 = call(
        first_kernel,
        "first_vector",
        (
            live,
            coef,
            perm,
            cond,
            edges,
            source_f,
            weight,
            near_a,
            near_b,
            far_c,
            far_d,
            first,
            second,
            table,
            ghost_table,
            ofrac,
            oy,
            ox,
            margin_in,
            column,
            v0,
        ),
        [
            ((6, x_cells, y_cells), F32),
            (own, F32),
            ((half, rows), F32),
            ((2, half, frac_cells), F32),
            ((half, rows), F32),
            (own, F32),
            ((edge_rows + 3 * half, LANES), F32),
            ((edge_rows + 3 * half, LANES), F32),
            ((3 * half, LANES), F32),
            ((core_rows + 8 * frac_blocks, LANES), F32),
            (field, F32),
        ],
        scratch=[pltpu.VMEM((members, frac_cells), F32)],
        aliases={20: 10},
    )
    near_rows = edge_rows + 2 * half

    def interior(power, v, before, vf, before_f, core_in):
        outs = [(field, F32), ((members, margin), F32), ((x_cells, LANES), F32)]
        return call(
            functools.partial(interior_kernel, power),
            f"interior_{power}",
            (v, before, vf, before_f, core_in, scale_f, unit, weight, ofrac, oy, ox),
            outs + [((8, members), F32)],
            scratch=[pltpu.VMEM((members, margin), F32), pltpu.VMEM((members, frac_cells), F32)]
            + [pltpu.VMEM((members, LANES), F32)] * power,
            cost=hidden,
        )

    finish_outs = [
        (own, F32),
        ((half, rows), F32),
        (own, F32),
        ((near_rows, LANES), F32),
        ((near_rows, LANES), F32),
        ((2 * half, LANES), F32),
        ((core_rows, LANES), F32),
        (field, F32),
    ]
    finish_scratch = [pltpu.VMEM((members, frac_cells), F32)]

    near_a, near_b, far_c, far_d, core_in = exchange(to_a, to_b, sent, core_msg)
    image, margin_in, column, dots1 = interior(1, v0, v0, f0, f0, core_in)
    own_f, f1, diff, wown, to_a, to_b, sent, core_msg, v1 = call(
        functools.partial(finish_kernel, 1),
        "finish_1",
        (f0, near_a, near_b, far_c, far_d, core_in, diff, wown, sr, scale_f, unit, table, ghost_table)
        + (weight, ofrac, oy, ox, margin_in, column, image),
        [(own, F32)] + finish_outs,
        scratch=finish_scratch,
        aliases={19: 8},
    )
    near_a, near_b, far_c, far_d, core_in = exchange(to_a, to_b, sent, core_msg)
    image, margin_in, column, dots2 = interior(2, v1, v0, f1, f0, core_in)
    f2, diff, margin_in, to_a, to_b, sent, core_msg, v2 = call(
        functools.partial(finish_kernel, 2),
        "finish_2",
        (f1, near_a, near_b, far_c, far_d, core_in, diff, wown, sr, scale_f, unit, table, ghost_table)
        + (own_f, weight, ofrac, oy, ox, margin_in, column, image),
        [
            (own, F32),
            ((half, rows), F32),
            ((members, margin), F32),
            ((edge_rows // 2 + half, LANES), F32),
            ((edge_rows // 2 + half, LANES), F32),
            ((half, LANES), F32),
            ((frac_blocks * half + x_cells, LANES), F32),
            (field, F32),
        ],
        aliases={20: 7},
    )
    near_a, near_b, far_c, far_d, core_in = exchange(to_a, to_b, sent, core_msg)
    (dots3,) = call(
        energy_kernel,
        "energy",
        (v2, v1, f2, f1, core_in, scale_f, unit, coef, storage_in, weight, ofrac, margin_in),
        [((8, members), F32)],
        scratch=[pltpu.VMEM((members, frac_cells), F32)] + [pltpu.VMEM((members, LANES), F32)] * 3,
        cost=hidden,
    )
    peers = count * lax.axis_size("gy")
    (moments,) = call(
        moments_kernel,
        "moments",
        (f2, near_a, near_b, far_c, far_d, diff, sr, unit, ghost_table, v2, dots1, dots2, dots3),
        [((peers, 2, LANES), F32)],
        scratch=[pltpu.VMEM((members, LANES), F32)],
    )
    totals = lax.all_to_all(moments, ("gx", "gy"), 0, 0)
    return call(
        close_kernel,
        "iterate",
        (totals, v0, v1, v2, f0, f1, f2),
        [(field, F32), (own, F32)],
        scratch=[
            pltpu.VMEM((3, LANES, LANES), F32),
            pltpu.VMEM(field, F32),
            pltpu.VMEM(own, F32),
            pltpu.SemaphoreType.DMA((5,)),
        ],
        far_out=True,
    )


def solution(mesh):
    placed = (
        P("grp", "gx", "gy"),
        P(("grp", "gy"), "gx"),
        P(("grp", "gy"), "gx"),
        P("gx", "gy"),
        P("gx", "gy"),
        P(),
        P("gx", None),
        P("gx", None),
        P("gx", None),
        P("gx"),
        P("gx", "gy", None, None),
        P("gx", "gy", None, None),
        P("gx", "gy", None, None),
        P("gx", "gy", None),
    )
    return jax.shard_map(
        per_device,
        mesh=mesh,
        in_specs=placed,
        out_specs=(P("grp", "gx", "gy"), P(("grp", "gy"), "gx")),
        check_vma=False,
    )
```

```python
import functools

import jax
import jax.numpy as jnp
from jax import lax
from jax.experimental import pallas as pl
from jax.experimental.pallas import tpu as pltpu
from jax.sharding import PartitionSpec as P

FRACTURE_STORAGE = 0.1
F32 = jnp.float32
BF16 = jnp.bfloat16
LANES = 128
GROUP = 16


def split3(x):
    high = x.astype(BF16)
    rest = x - high.astype(F32)
    mid = rest.astype(BF16)
    low = (rest - mid.astype(F32)).astype(BF16)
    return jnp.concatenate([high, mid, low], axis=0)


def pick(x, table, transposed=False):
    rows = x.shape[0]
    dims = (((1,), (1 if transposed else 0,)), ((), ()))
    out = lax.dot_general(split3(x), table, dims, preferred_element_type=F32)
    return out[:rows] + out[rows : 2 * rows] + out[2 * rows :]


def fetch(sources, targets, sems):
    copies = [pltpu.make_async_copy(a, b, sems.at[k]) for k, (a, b) in enumerate(zip(sources, targets))]
    for copy in copies:
        copy.start()
    return copies


class Place:
    def __init__(self):
        count = lax.axis_size("gx")
        i = lax.axis_index("gx")
        self.j = lax.axis_index("gy")
        self.high_side = self.j == 0
        self.even = lax.rem(i, 2) == 0
        self.low_pair = lax.rem(lax.div(i, 2), 2) == 0
        self.first = i == 0
        self.last = i == count - 1


def harmonic(first_perm, second_perm):
    return 2.0 * first_perm * second_perm / (first_perm + second_perm)


def one_hot(index_row, size):
    shape = (size, index_row.shape[1])
    ids = lax.broadcasted_iota(jnp.int32, shape, 0)
    return jnp.where(ids == index_row, 1.0, 0.0).astype(BF16)


def to_blocks(x):
    return jnp.concatenate(
        [x[:, q : q + LANES] for q in range(0, x.shape[1], LANES)], axis=0
    )


def from_blocks(x, rows):
    return jnp.concatenate(
        [x[q : q + rows] for q in range(0, x.shape[0], rows)], axis=1
    )


def by_group(first, second, third, fourth):
    group = first.shape[1] // 4
    lane = lax.broadcasted_iota(jnp.int32, first.shape, 1)
    return jnp.where(
        lane < group,
        first,
        jnp.where(lane < 2 * group, second, jnp.where(lane < 3 * group, third, fourth)),
    )


def total_rows(x):
    return jnp.sum(jnp.transpose(x), axis=0, keepdims=True)


def fold_lanes(x):
    rows, width = x.shape
    out = x[:, :LANES]
    for q in range(LANES, width, LANES):
        out = out + x[:, q : q + LANES]
    return out


def opening_kernel(
    perm_table_hbm,
    class_hbm,
    aperture_hbm,
    slots_hbm,
    perm_ref,
    cond_ref,
    oslot_ref,
    near_a_ref,
    near_b_ref,
    far_ref,
    border_ref,
    perm_table_ref,
    class_ref,
    aperture_ref,
    slots_ref,
    sems,
):
    copies = fetch(
        (class_hbm, perm_table_hbm, aperture_hbm, slots_hbm),
        (class_ref, perm_table_ref, aperture_ref, slots_ref),
        sems,
    )
    for copy in copies:
        copy.wait()
    x_cells, y_cells = class_ref.shape
    half = aperture_ref.shape[0]
    here = Place()
    classes = class_ref[...]
    perm = jnp.zeros(classes.shape, F32)
    for index in range(perm_table_ref.shape[0]):
        perm = jnp.where(classes == index, perm_table_ref[index], perm)
    perm_ref[...] = perm
    border_ref[...] = jnp.where(here.high_side, perm[:, y_cells - LANES :], perm[:, :LANES])

    aperture = aperture_ref[...]
    cond = aperture * aperture * aperture
    cond_ref[...] = cond
    oslot = one_hot(slots_ref[...], cond.shape[1])
    oslot_ref[...] = oslot
    supplied = pick(cond, oslot)
    far_ref[...] = supplied
    up, down = to_blocks(perm[x_cells - 1 :]), to_blocks(perm[:1])
    blocks = up.shape[0]
    pad = jnp.zeros((near_a_ref.shape[0] - half - blocks, LANES), F32)
    for ref, edge in ((near_a_ref, jnp.where(here.even, up, down)), (near_b_ref, jnp.where(here.even, down, up))):
        ref[...] = jnp.concatenate([supplied, edge, pad], axis=0)


def neighbours(here, near_a_ref, near_b_ref, far_c_ref, far_d_ref):
    def reader(flag, at_zero, at_one):
        return lambda at, size: jnp.where(
            flag, at_zero[at : at + size, :], at_one[at : at + size, :]
        )

    return (
        reader(here.even, near_a_ref, near_b_ref),
        reader(here.even, near_b_ref, near_a_ref),
        reader(here.low_pair, far_c_ref, far_d_ref),
        reader(here.low_pair, far_d_ref, far_c_ref),
    )


def margin_values(found, ox):
    found = found.reshape(-1, *ox.shape) * ox[None]
    return jnp.sum(found, axis=1)


def border_column(tile_low, tile_high, high_side, m):
    tile = jnp.where(high_side, tile_high, tile_low)
    return pltpu.roll(tile, jnp.where(high_side, lax.rem(m + 1, LANES), m), 1)


def border_row(row_values, high_side):
    members, y_cells = row_values.shape
    tile = jnp.where(high_side, row_values[:, y_cells - LANES :], row_values[:, :LANES])
    turned = jnp.transpose(tile)
    line = jnp.where(high_side, turned[LANES - 1 :], turned[:1])
    return jnp.concatenate([line, jnp.zeros((1, LANES - members), F32)], axis=1)


def finish_edges(high_rows, low_rows, partial_ref, column, high_side, oy, ox):
    members = high_rows.shape[0]
    x_cells = ox.shape[0]
    found = pick(jnp.concatenate([high_rows, low_rows], axis=0), oy)
    margin = partial_ref[...] + found[:members] * ox[x_cells - 1 :] + found[members:] * ox[:1]
    row = lax.broadcasted_iota(jnp.int32, column.shape, 0)
    column = jnp.where(row == x_cells - 1, border_row(high_rows, high_side), column)
    return margin, jnp.where(row == 0, border_row(low_rows, high_side), column)


def send_network(vf, sr, table, ghost_table, diff_ref, refs):
    half = vf.shape[0]
    rows = diff_ref.shape[1]
    found = pick(vf, table)
    diff_ref[...] = found[:, :rows]
    if sr is None:
        for ref, at in refs:
            ref[at : at + half, :] = found[:, rows:]
        return
    sums = pick(sr * found[:, :rows], ghost_table, True)
    for ref, at in refs:
        ref[at : at + half, :] = found[:, rows:]
        ref[at + half : at + 2 * half, :] = sums


def send_core(core_ref, vf, margin, weight, ofrac, column, j, work_ref, wown_ref):
    half, frac_cells = vf.shape
    work_ref[...] = pick(margin * weight, ofrac, True)
    wown_ref[...] = work_ref[pl.ds(pl.multiple_of(j * half, half), half), :]
    other = work_ref[pl.ds(pl.multiple_of((1 - j) * half, half), half), :]
    size = frac_cells // LANES * half
    core_ref[0:size, :] = to_blocks(vf)
    core_ref[size : 2 * size, :] = to_blocks(other)
    core_ref[2 * size : 2 * size + column.shape[0], :] = column


def inside_kernel(
    ov_count_hbm,
    isect_count_hbm,
    storage_hbm,
    source_hbm,
    source_f_hbm,
    cell_hbm,
    ov_weight_hbm,
    local_hbm,
    other_hbm,
    frac_hbm,
    perm_ref,
    border_ref,
    oslot_ref,
    cond_ref,
    source_f_ref,
    storage_ref,
    live_ref,
    edge_ref,
    coef_ref,
    oy_ref,
    ox_ref,
    weight_ref,
    first_ref,
    cond_first_ref,
    cond_second_ref,
    wsum_ref,
    table_ref,
    ghost_table_ref,
    ofrac_ref,
    v_ref,
    margin_ref,
    column_ref,
    ov_count_ref,
    isect_count_ref,
    source_ref,
    cell_ref,
    ov_weight_ref,
    local_ref,
    other_in_ref,
    frac_ref,
    sems,
):
    members, x_cells, y_cells = source_ref.shape
    frac_cells = table_ref.shape[0]
    here = Place()
    high_side = here.high_side
    copies = fetch(
        (
            cell_hbm,
            local_hbm,
            other_hbm,
            frac_hbm,
            ov_weight_hbm,
            ov_count_hbm,
            isect_count_hbm,
            storage_hbm,
            source_f_hbm,
            source_hbm,
        ),
        (
            cell_ref,
            local_ref,
            other_in_ref,
            frac_ref,
            ov_weight_ref,
            ov_count_ref,
            isect_count_ref,
            storage_ref,
            source_f_ref,
            source_ref,
        ),
        sems,
    )

    def line(ref):
        return jnp.concatenate([ref[k : k + 1, :] for k in range(ref.shape[0])], axis=1)

    rows = local_ref.size
    perm, border = perm_ref[...], border_ref[...]
    col = jnp.where(high_side, border[:, :1], border[:, LANES - 1 :])
    lane = lax.broadcasted_iota(jnp.int32, perm.shape, 1)
    row = lax.broadcasted_iota(jnp.int32, perm.shape, 0)
    north = jnp.concatenate([perm[:, 1:], col], axis=1)
    south = jnp.concatenate([col, perm[:, :-1]], axis=1)
    tn = jnp.where((lane == y_cells - 1) & jnp.logical_not(high_side), 0.0, harmonic(perm, north))
    ts = jnp.where((lane == 0) & high_side, 0.0, harmonic(perm, south))
    east = jnp.concatenate([perm[1:], perm[:1]], axis=0)
    west = jnp.concatenate([perm[-1:], perm[:-1]], axis=0)
    te = jnp.where(row == x_cells - 1, 0.0, harmonic(perm, east))
    tw = jnp.where(row == 0, 0.0, harmonic(perm, west))
    for copy in copies[:-1]:
        copy.wait()
    cell = line(cell_ref)
    oy = one_hot(cell % y_cells, y_cells)
    oy_ref[...] = oy
    row_x = lax.broadcasted_iota(jnp.int32, ox_ref.shape, 0)
    at_x = row_x == cell // y_cells
    ox = jnp.where(at_x, 1.0, 0.0)
    ox_ref[...] = ox
    lane_w = lax.broadcasted_iota(jnp.int32, (1, LANES), 1)
    weight = jnp.concatenate(
        [jnp.where(lane_w < ov_count_ref[k], ov_weight_ref[k : k + 1, :], 0.0) for k in range(ov_weight_ref.shape[0])],
        axis=1,
    )
    weight_ref[...] = weight
    for block in range(local_ref.shape[0]):
        at = slice(block * LANES, (block + 1) * LANES)
        live_ref[:, at] = jnp.where(lane_w < isect_count_ref[block], 1.0, 0.0)
    part = storage_ref[...] + te + tw + tn + ts + pick(jnp.where(at_x, weight, 0.0), oy, True)
    coef_ref[0] = te
    coef_ref[1] = tw
    coef_ref[2] = tn
    coef_ref[3] = ts
    coef_ref[4] = part

    other = line(other_in_ref)
    first, second = one_hot(line(local_ref), frac_cells), one_hot(other, frac_cells)
    first_ref[...] = first
    cond = cond_ref[...]
    cond_first_ref[...] = pick(cond, first)
    cond_second_ref[...] = pick(cond, second)
    table_ref[:, :rows] = first - second
    table_ref[:, rows:] = oslot_ref[...]
    ghost_table_ref[...] = one_hot(other - frac_cells, ghost_table_ref.shape[0])
    ofrac = one_hot(line(frac_ref), frac_cells)
    ofrac_ref[...] = ofrac
    wsum_ref[...] = pick(jnp.broadcast_to(weight, (8, weight.shape[1])), ofrac, True)

    inverse = 1.0 / part
    inner_x = jnp.where((row_x == 0) | (row_x == x_cells - 1), 0.0, ox)
    lane_c = lax.broadcasted_iota(jnp.int32, (x_cells, LANES), 1)
    column_ref[...] = jnp.zeros_like(column_ref)
    copies[-1].wait()
    edge_ref[0] = source_ref[:, x_cells - 1, :]
    edge_ref[1] = source_ref[:, 0, :]

    @pl.loop(0, members // GROUP)
    def _(index):
        start = index * GROUP
        block = source_ref[pl.ds(start, GROUP)] * inverse[None]
        v_ref[pl.ds(start, GROUP)] = block
        found = pick(block.reshape(GROUP * x_cells, y_cells), oy_ref[...])
        margin_ref[pl.ds(start, GROUP), :] = margin_values(found, inner_x)
        column = column_ref[...]
        for k in range(GROUP):
            m = start + k
            moved = border_column(block[k, :, :LANES], block[k, :, y_cells - LANES :], high_side, m)
            column = jnp.where(lane_c == m, moved, column)
        column_ref[...] = column


def first_kernel(
    live_ref,
    coef_ref,
    perm_ref,
    edge_ref,
    source_f_ref,
    weight_ref,
    near_a_ref,
    near_b_ref,
    far_c_ref,
    far_d_ref,
    first_ref,
    cond_first_ref,
    cond_second_ref,
    wsum_ref,
    table_ref,
    ghost_table_ref,
    ofrac_ref,
    oy_ref,
    ox_ref,
    inner_margin_ref,
    inner_column_ref,
    v_in_ref,
    unit_ref,
    vf_ref,
    sr_ref,
    scale_f_ref,
    diff_ref,
    wown_ref,
    to_a_ref,
    to_b_ref,
    sent_ref,
    core_ref,
    v_ref,
    work_ref,
):
    members, x_cells, y_cells = v_ref.shape
    half, frac_cells = source_f_ref.shape
    blocks = y_cells // LANES
    here = Place()
    j, high_side = here.j, here.high_side
    base = blocks * members
    plus1, minus1, plus2, minus2 = neighbours(here, near_a_ref, near_b_ref, far_c_ref, far_d_ref)

    ghosts = by_group(minus1(0, half), plus1(0, half), minus2(0, half), plus2(0, half))
    table, ghost_table = table_ref[...], ghost_table_ref[...]
    cond_first = cond_first_ref[...]
    cond_second = cond_second_ref[...] + pick(ghosts, ghost_table)
    sr = jnp.where(live_ref[...] > 0.0, harmonic(cond_first, cond_second), 0.0)
    sr_ref[...] = sr
    diag_f = FRACTURE_STORAGE + pick(sr, first_ref[...], True)
    inverse_f = 1.0 / diag_f
    scale_f_ref[0] = inverse_f
    scale_f_ref[1] = diag_f
    vf = source_f_ref[...] * inverse_f
    vf_ref[...] = vf
    refs = [(to_a_ref, base), (to_b_ref, base), (sent_ref, 0)]
    send_network(vf, sr, table, ghost_table, diff_ref, refs)
    slot_sums = pick(sr, ghost_table, True)
    for ref, at in refs:
        ref[at + 2 * half : at + 3 * half, :] = slot_sums

    perm, part = perm_ref[...], coef_ref[4]
    row = lax.broadcasted_iota(jnp.int32, perm.shape, 0)
    perm_plus = from_blocks(plus1(half, blocks), 1)
    perm_minus = from_blocks(minus1(half, blocks), 1)
    te_edge = jnp.where(here.last, 0.0, harmonic(perm[x_cells - 1 :], perm_plus))
    tw_edge = jnp.where(here.first, 0.0, harmonic(perm[:1], perm_minus))
    te = jnp.where(row == x_cells - 1, te_edge, coef_ref[0])
    tw = jnp.where(row == 0, tw_edge, coef_ref[1])
    diag = part + jnp.where(row == x_cells - 1, te_edge, 0.0) + jnp.where(row == 0, tw_edge, 0.0)
    inverse = 1.0 / diag
    unit_ref[0] = te * inverse
    unit_ref[1] = tw * inverse
    unit_ref[2] = coef_ref[2] * inverse
    unit_ref[3] = coef_ref[3] * inverse
    unit_ref[4] = inverse
    unit_ref[5] = diag
    high_rows = edge_ref[0] * inverse[x_cells - 1 :]
    low_rows = edge_ref[1] * inverse[:1]
    v_ref[:, x_cells - 1, :] = high_rows
    v_ref[:, 0, :] = low_rows
    to_a_ref[0:base, :] = to_blocks(jnp.where(here.even, high_rows, low_rows))
    to_b_ref[0:base, :] = to_blocks(jnp.where(here.even, low_rows, high_rows))
    margin, column = finish_edges(
        high_rows, low_rows, inner_margin_ref, inner_column_ref[...], high_side, oy_ref[...], ox_ref[...]
    )
    weight = weight_ref[...]
    send_core(core_ref, vf, margin, weight, ofrac_ref[...], column, j, work_ref, wown_ref)
    tail = core_ref.shape[0] - 8 * (frac_cells // LANES)
    core_ref[tail:, :] = to_blocks(wsum_ref[...])


def interior_kernel(
    power,
    v_ref,
    before_ref,
    vf_ref,
    before_f_ref,
    core_ref,
    scale_f_ref,
    unit_ref,
    weight_ref,
    ofrac_ref,
    oy_ref,
    ox_ref,
    *refs,
):
    image_ref, margin_ref, column_ref, dots_ref, flow_ref, work_ref, *acc_refs = refs
    members, x_cells, y_cells = v_ref.shape
    half, frac_cells = vf_ref.shape
    blocks = y_cells // LANES
    here = Place()
    j, high_side = here.j, here.high_side
    size = frac_cells // LANES * half
    theirs = from_blocks(core_ref[0:size, :], half)
    column_in = core_ref[2 * size : 2 * size + x_cells, :]
    vf = vf_ref[...]
    own_rows = pl.ds(pl.multiple_of(j * half, half), half)
    work_ref[own_rows, :] = vf
    work_ref[pl.ds(pl.multiple_of((1 - j) * half, half), half), :] = theirs
    flow_ref[...] = pick(work_ref[...], ofrac_ref[...]) * weight_ref[...]

    heavy_f = vf * scale_f_ref[1]
    for ref in acc_refs:
        ref[...] = jnp.zeros_like(ref)
    acc_refs[0][own_rows, :] = fold_lanes(vf * heavy_f)
    if power > 1:
        acc_refs[1][own_rows, :] = fold_lanes(before_f_ref[...] * heavy_f)

    lane_c = lax.broadcasted_iota(jnp.int32, (x_cells, LANES), 1)
    lane = lax.broadcasted_iota(jnp.int32, (x_cells, y_cells), 1)
    row = lax.broadcasted_iota(jnp.int32, (x_cells, y_cells), 0)
    row_x = lax.broadcasted_iota(jnp.int32, ox_ref.shape, 0)
    oy, ox = oy_ref[...], ox_ref[...]
    inner_x = jnp.where((row_x == 0) | (row_x == x_cells - 1), 0.0, ox)
    te = jnp.where(row == x_cells - 1, 0.0, unit_ref[0])
    tw = jnp.where(row == 0, 0.0, unit_ref[1])
    column_ref[...] = jnp.zeros_like(column_ref)

    @pl.loop(0, members // GROUP)
    def _(index):
        start = index * GROUP
        parts = []
        for k in range(GROUP):
            parts.append(ox * flow_ref[pl.ds(start + k, 1), :])
        coupled = pick(jnp.concatenate(parts, axis=0), oy, True)
        column = column_ref[...]
        for k in range(GROUP):
            m = start + k
            value = v_ref[m]
            east = pltpu.roll(value, x_cells - 1, 0)
            west = pltpu.roll(value, 1, 0)
            moved = pltpu.roll(column_in, jnp.where(high_side, LANES - 1 - m, lax.rem(LANES - m, LANES)), 1)
            moved = jnp.concatenate([moved] * blocks, axis=1)
            north = jnp.where(lane == y_cells - 1, moved, pltpu.roll(value, y_cells - 1, 1))
            south = jnp.where(lane == 0, moved, pltpu.roll(value, 1, 1))
            image = value - te * east - tw * west - unit_ref[2] * north - unit_ref[3] * south
            image = image - coupled[k * x_cells : (k + 1) * x_cells] * unit_ref[4]
            heavy = value * unit_ref[5]
            at = pl.ds(m, 1)
            acc_refs[0][at, :] += jnp.sum(fold_lanes(value * heavy), axis=0, keepdims=True)
            if power > 1:
                acc_refs[1][at, :] += jnp.sum(fold_lanes(before_ref[m] * heavy), axis=0, keepdims=True)
            image_ref[m] = image
            shifted = border_column(image[:, :LANES], image[:, y_cells - LANES :], high_side, m)
            column = jnp.where(lane_c == m, shifted, column)
        column_ref[...] = column
        block = image_ref[pl.ds(start, GROUP)]
        found = pick(block.reshape(GROUP * x_cells, y_cells), oy)
        margin_ref[pl.ds(start, GROUP), :] = margin_values(found, inner_x)

    dots = [total_rows(ref[...]) for ref in acc_refs]
    dots.append(jnp.zeros((8 - len(dots), members), F32))
    dots_ref[...] = jnp.concatenate(dots, axis=0)


def finish_kernel(
    power,
    vf_ref,
    near_a_ref,
    near_b_ref,
    far_c_ref,
    far_d_ref,
    core_in_ref,
    diff_in_ref,
    wown_in_ref,
    sr_ref,
    scale_f_ref,
    unit_ref,
    table_ref,
    ghost_table_ref,
    *refs,
):
    own_f_in_ref, *refs = refs
    weight_ref, ofrac_ref, oy_ref, ox_ref, inner_margin_ref, inner_column_ref, image_in_ref, *refs = refs
    if power == 1:
        own_f_ref, out_f_ref, diff_ref, wown_ref, to_a_ref, to_b_ref, sent_ref, core_ref, image_ref, work_ref = refs
    else:
        out_f_ref, diff_ref, margin_ref, to_a_ref, to_b_ref, sent_ref, core_ref, image_ref = refs
    half, frac_cells = vf_ref.shape
    x_cells, y_cells = unit_ref.shape[1:]
    members = image_ref.shape[0]
    blocks = y_cells // LANES
    frac_blocks = frac_cells // LANES
    here = Place()
    j, high_side = here.j, here.high_side
    base = blocks * members
    plus1, minus1, plus2, minus2 = neighbours(here, near_a_ref, near_b_ref, far_c_ref, far_d_ref)
    rows = sr_ref.shape[1]

    table, ghost_table = table_ref[...], ghost_table_ref[...]
    vf = vf_ref[...]
    ghosts = by_group(minus1(base, half), plus1(base, half), minus2(0, half), plus2(0, half))
    sums = by_group(
        plus1(base + half, half), minus1(base + half, half), plus2(half, half), minus2(half, half)
    )
    size = frac_blocks * half
    their_sums = from_blocks(core_in_ref[size : 2 * size, :], half)
    if power == 1:
        at = 2 * half
        back = by_group(
            plus1(base + at, half), minus1(base + at, half), plus2(at, half), minus2(at, half)
        )
        tail = core_in_ref.shape[0] - 8 * frac_blocks
        wsum = own_f_in_ref[...] + from_blocks(core_in_ref[tail:, :], 8)
        own_f = FRACTURE_STORAGE + wsum[:1] + pick(back, table[:, rows:], True)
        own_f_ref[...] = own_f
    else:
        own_f = own_f_in_ref[...]
    sr = sr_ref[...]
    flux = sr * (diff_in_ref[...] - pick(ghosts, ghost_table))
    image_f = own_f * vf + pick(jnp.concatenate([flux, -sums], axis=1), table, True)
    image_f = image_f - wown_in_ref[...] - their_sums

    next_f = image_f * scale_f_ref[0]
    out_f_ref[...] = next_f
    edge_size = base if power == 1 else base // 2
    refs = [(to_a_ref, edge_size), (to_b_ref, edge_size), (sent_ref, 0)]
    send_network(next_f, sr if power == 1 else None, table, ghost_table, diff_ref, refs)

    edges = []
    for side, at, reader in ((0, x_cells - 1, plus1), (1, 0, minus1)):
        beyond = from_blocks(reader(0, base), members)
        edge = image_in_ref[:, at, :] - unit_ref[side, at : at + 1, :] * beyond
        image_ref[:, at, :] = edge
        edges.append(edge)
    up, down = edges
    if power == 2:
        up, down = up[:, : y_cells // 2], down[:, y_cells // 2 :]
    to_a_ref[0:edge_size, :] = to_blocks(jnp.where(here.even, up, down))
    to_b_ref[0:edge_size, :] = to_blocks(jnp.where(here.even, down, up))
    margin, column = finish_edges(
        edges[0], edges[1], inner_margin_ref, inner_column_ref[...], high_side, oy_ref[...], ox_ref[...]
    )
    if power == 1:
        send_core(core_ref, next_f, margin, weight_ref[...], ofrac_ref[...], column, j, work_ref, wown_ref)
    else:
        margin_ref[...] = margin
        core_ref[0:size, :] = to_blocks(next_f)
        core_ref[size : size + x_cells, :] = column


def energy_kernel(
    v_ref,
    before_ref,
    vf_ref,
    before_f_ref,
    core_ref,
    scale_f_ref,
    unit_ref,
    coef_ref,
    storage_ref,
    weight_ref,
    ofrac_ref,
    margin_ref,
    dots_ref,
    work_ref,
    acc0_ref,
    acc1_ref,
    acc2_ref,
):
    members, x_cells, y_cells = v_ref.shape
    half, frac_cells = vf_ref.shape
    blocks = y_cells // LANES
    here = Place()
    size = frac_cells // LANES * half
    theirs = from_blocks(core_ref[0:size, :], half)
    column_in = core_ref[size : size + x_cells, :]
    vf = vf_ref[...]
    own_rows = pl.ds(pl.multiple_of(here.j * half, half), half)
    work_ref[own_rows, :] = vf
    work_ref[pl.ds(pl.multiple_of((1 - here.j) * half, half), half), :] = theirs
    gap = margin_ref[...] - pick(work_ref[...], ofrac_ref[...])
    acc2_ref[...] = fold_lanes(weight_ref[...] * gap * gap)
    heavy_f = vf * scale_f_ref[1]
    acc0_ref[...] = jnp.zeros_like(acc0_ref)
    acc1_ref[...] = jnp.zeros_like(acc1_ref)
    acc0_ref[own_rows, :] = fold_lanes(vf * heavy_f)
    acc1_ref[own_rows, :] = fold_lanes(before_f_ref[...] * heavy_f)
    lane = lax.broadcasted_iota(jnp.int32, (x_cells, y_cells), 1)
    diag, te, tn, storage = unit_ref[5], coef_ref[0], coef_ref[2], storage_ref[...]

    @pl.loop(0, members // GROUP)
    def _(index):
        start = index * GROUP
        for k in range(GROUP):
            m = start + k
            value = v_ref[m]
            east = value - pltpu.roll(value, x_cells - 1, 0)
            moved = pltpu.roll(column_in, LANES - 1 - m, 1)
            moved = jnp.concatenate([moved] * blocks, axis=1)
            north = value - jnp.where(lane == y_cells - 1, moved, pltpu.roll(value, y_cells - 1, 1))
            energy = storage * value * value + te * east * east + tn * north * north
            heavy = value * diag
            at = pl.ds(m, 1)
            acc0_ref[at, :] += jnp.sum(fold_lanes(value * heavy), axis=0, keepdims=True)
            acc1_ref[at, :] += jnp.sum(fold_lanes(before_ref[m] * heavy), axis=0, keepdims=True)
            acc2_ref[at, :] += jnp.sum(fold_lanes(energy), axis=0, keepdims=True)

    dots = [total_rows(ref[...]) for ref in (acc0_ref, acc1_ref, acc2_ref)]
    dots.append(jnp.zeros((8 - len(dots), members), F32))
    dots_ref[...] = jnp.concatenate(dots, axis=0)


def moments_kernel(
    vf_ref,
    near_a_ref,
    near_b_ref,
    far_c_ref,
    far_d_ref,
    diff_in_ref,
    sr_ref,
    unit_ref,
    ghost_table_ref,
    v_ref,
    dots1_ref,
    dots2_ref,
    dots3_ref,
    moments_ref,
    acc_ref,
):
    half = vf_ref.shape[0]
    members, x_cells, y_cells = v_ref.shape
    middle = y_cells // 2
    base = middle // LANES * members
    here = Place()
    plus1, minus1, plus2, minus2 = neighbours(here, near_a_ref, near_b_ref, far_c_ref, far_d_ref)
    vf = vf_ref[...]
    ghosts = by_group(minus1(base, half), plus1(base, half), minus2(0, half), plus2(0, half))
    gap = diff_in_ref[...] - pick(ghosts, ghost_table_ref[...])
    acc_ref[...] = jnp.zeros_like(acc_ref)
    own_rows = pl.ds(pl.multiple_of(here.j * half, half), half)
    acc_ref[own_rows, :] = fold_lanes(sr_ref[...] * gap * gap) + fold_lanes(FRACTURE_STORAGE * vf * vf)
    for side, at, reader, cut in (
        (0, x_cells - 1, plus1, slice(middle, y_cells)),
        (1, 0, minus1, slice(0, middle)),
    ):
        trans = unit_ref[side, at : at + 1, cut] * unit_ref[5, at : at + 1, cut]
        edge = v_ref[:, at, cut] - from_blocks(reader(0, base), members)
        acc_ref[...] += fold_lanes(trans * edge * edge)
    last = total_rows(acc_ref[...]) + dots3_ref[2:3, :]
    blank = jnp.zeros((1, LANES - 3 * members), F32)
    lines = [
        jnp.concatenate([dots1_ref[0:1, :], dots2_ref[1:2, :], dots2_ref[0:1, :], blank], axis=1),
        jnp.concatenate([dots3_ref[1:2, :], dots3_ref[0:1, :], last, blank], axis=1),
    ]
    lines = jnp.concatenate(lines, axis=0)
    moments_ref[...] = jnp.broadcast_to(lines[None], moments_ref.shape)


def close_kernel(totals_ref, v0_ref, v1_ref, v2_ref, f0_ref, f1_ref, f2_ref, x_hbm, xf_hbm, c_ref, x_ref, xf_ref, sems):
    members, x_cells, y_cells = v0_ref.shape
    half, frac_cells = f0_ref.shape

    total = jnp.sum(totals_ref[...], axis=0)
    m0, m1, m2, m3, m4, m5 = (
        total[k // 3 : k // 3 + 1, k % 3 * members : k % 3 * members + members] for k in range(6)
    )
    alpha0 = m0 / m1
    rz1 = m0 - 2.0 * alpha0 * m1 + alpha0 * alpha0 * m2
    beta1 = rz1 / m0
    a, b = 1.0 + beta1, -alpha0
    pap1 = a * a * m1 + 2.0 * a * b * m2 + b * b * m3
    alpha1 = rz1 / pap1
    e = -alpha0 - alpha1 * a
    g = -alpha1 * b
    rz2 = m0 + 2.0 * e * m1 + (e * e + 2.0 * g) * m2 + 2.0 * e * g * m3 + g * g * m4
    beta2 = rz2 / rz1
    c = 1.0 + beta2 * a
    d = e + beta2 * b
    pap2 = c * c * m1 + 2.0 * c * d * m2 + (d * d + 2.0 * c * g) * m3 + 2.0 * d * g * m4 + g * g * m5
    alpha2 = rz2 / pap2
    c0 = alpha0 + alpha1 * a + alpha2 * c
    c1 = alpha1 * b + alpha2 * d
    c2 = alpha2 * g
    for k, row in enumerate((c0, c1, c2)):
        row = jnp.concatenate([row, jnp.zeros((1, LANES - members), F32)], axis=1)
        c_ref[k] = jnp.transpose(jnp.broadcast_to(row, (LANES, LANES)))
    j = lax.axis_index("gy")
    own = pl.ds(pl.multiple_of(j * half, half), half)

    def wide(k, rows, width):
        return jnp.concatenate([c_ref[k, rows, :]] * (width // LANES), axis=1)

    xf_ref[...] = (
        wide(0, own, frac_cells) * f0_ref[...]
        + wide(1, own, frac_cells) * f1_ref[...]
        + wide(2, own, frac_cells) * f2_ref[...]
    )

    copies = fetch((xf_ref,), (xf_hbm,), sems)
    pieces = sems.shape[0] - 1
    piece = members // pieces
    for index in range(pieces):

        @pl.loop(index * piece, (index + 1) * piece)
        def _(m):
            rows = pl.ds(m, 1)
            x_ref[m] = (
                wide(0, rows, y_cells) * v0_ref[m]
                + wide(1, rows, y_cells) * v1_ref[m]
                + wide(2, rows, y_cells) * v2_ref[m]
            )

        part = pl.ds(index * piece, piece)
        copies.append(pltpu.make_async_copy(x_ref.at[part], x_hbm.at[part], sems.at[1 + index]))
        copies[-1].start()
    for copy in copies:
        copy.wait()


def pairs_of(count, stride, phase):
    out = []
    for index in range(count):
        if (index // stride) % 2 == phase:
            mate = (index + stride) % count
            out += [(index, mate), (mate, index)]
    return out


VMEM = pl.BlockSpec(memory_space=pltpu.VMEM)


HBM = pl.BlockSpec(memory_space=pltpu.HBM)


def call(kernel, name, args, outs, scratch=(), far_in=0, far_out=False, cost=None, aliases=None):
    args = [pltpu.with_memory_space_constraint(arg, pltpu.HBM) for arg in args[:far_in]] + list(args[far_in:])
    return pl.pallas_call(
        kernel,
        name=name,
        out_shape=[jax.ShapeDtypeStruct(shape, dtype) for shape, dtype in outs],
        in_specs=[HBM] * far_in + [VMEM] * (len(args) - far_in),
        out_specs=[HBM if far_out else VMEM] * len(outs),
        scratch_shapes=list(scratch),
        compiler_params=pltpu.CompilerParams(vmem_limit_bytes=40 * 1024 * 1024),
        cost_estimate=cost,
        input_output_aliases=aliases or {},
    )(*args)


def per_device(
    source_matrix,
    source_fracture,
    aperture,
    storage,
    perm_class,
    class_perm,
    send_slots,
    isect_local,
    isect_other,
    isect_count,
    ov_cell,
    ov_frac,
    ov_weight,
    ov_count,
):
    members, x_cells, y_cells = source_matrix.shape
    half, frac_cells = source_fracture.shape
    slots = send_slots.shape[1]
    rows = isect_local.size
    margin = ov_cell.size
    count = lax.axis_size("gx")

    def near(to_a, to_b):
        return (
            lax.ppermute(to_a, "gx", pairs_of(count, 1, 0)),
            lax.ppermute(to_b, "gx", pairs_of(count, 1, 1)),
        )

    def far(value):
        return (
            lax.ppermute(value, "gx", pairs_of(count, 2, 0)),
            lax.ppermute(value, "gx", pairs_of(count, 2, 1)),
        )

    def core(value):
        return lax.ppermute(value, "gy", [(0, 1), (1, 0)])

    blocks = y_cells // LANES
    frac_blocks = frac_cells // LANES
    field = (members, x_cells, y_cells)
    own = (half, frac_cells)
    hidden = pl.CostEstimate(flops=4_000_000_000, bytes_accessed=12_000_000, transcendentals=0)
    perm, cond, oslot, to_a, to_b, sent, border = call(
        opening_kernel,
        "opening",
        (class_perm, perm_class, aperture, send_slots),
        [
            ((x_cells, y_cells), F32),
            (own, F32),
            ((frac_cells, slots), BF16),
            ((half + 8 * (-(-blocks // 8)), LANES), F32),
            ((half + 8 * (-(-blocks // 8)), LANES), F32),
            ((half, slots), F32),
            ((x_cells, LANES), F32),
        ],
        scratch=[
            pltpu.SMEM(class_perm.shape, F32),
            pltpu.VMEM(perm_class.shape, jnp.int32),
            pltpu.VMEM(aperture.shape, F32),
            pltpu.VMEM(send_slots.shape, jnp.int32),
            pltpu.SemaphoreType.DMA((4,)),
        ],
        far_in=4,
    )

    def exchange(to_a, to_b, sent, to_core):
        near_a, near_b = near(to_a, to_b)
        core_in = core(to_core)
        sent, core_in = lax.optimization_barrier((sent, core_in))
        far_c, far_d = far(sent)
        return near_a, near_b, far_c, far_d, core_in

    near_a, near_b, far_c, far_d, border = exchange(to_a, to_b, sent, border)
    source_f, storage_in, live, edges, coef, oy, ox, weight, *network, v0, margin_in, column = call(
        inside_kernel,
        "inside",
        (
            ov_count.reshape(-1),
            isect_count,
            storage,
            source_matrix,
            source_fracture,
            ov_cell.reshape(-1, LANES),
            ov_weight.reshape(-1, LANES),
            isect_local,
            isect_other,
            ov_frac.reshape(-1, LANES),
            perm,
            border,
            oslot,
            cond,
        ),
        [
            (own, F32),
            ((x_cells, y_cells), F32),
            ((1, rows), F32),
            ((2, members, y_cells), F32),
            ((5, x_cells, y_cells), F32),
            ((y_cells, margin), BF16),
            ((x_cells, margin), F32),
            ((1, margin), F32),
            ((frac_cells, rows), BF16),
            ((half, rows), F32),
            ((half, rows), F32),
            ((8, frac_cells), F32),
            ((frac_cells, rows + slots), BF16),
            ((slots, rows), BF16),
            ((frac_cells, margin), BF16),
            (field, F32),
            ((members, margin), F32),
            ((x_cells, LANES), F32),
        ],
        scratch=[
            pltpu.SMEM((ov_count.size,), jnp.int32),
            pltpu.SMEM(isect_count.shape, jnp.int32),
            pltpu.VMEM(field, F32),
            pltpu.VMEM((margin // LANES, LANES), jnp.int32),
            pltpu.VMEM((margin // LANES, LANES), F32),
            pltpu.VMEM(isect_local.shape, jnp.int32),
            pltpu.VMEM(isect_other.shape, jnp.int32),
            pltpu.VMEM((margin // LANES, LANES), jnp.int32),
            pltpu.SemaphoreType.DMA((10,)),
        ],
        far_in=10,
        cost=hidden,
    )
    first, cond_first, cond_second, wsum, table, ghost_table, ofrac = network
    core_rows = 2 * frac_blocks * half + x_cells
    edge_rows = blocks * members
    unit, f0, sr, scale_f, diff, wown, to_a, to_b, sent, core_msg, v0 = call(
        first_kernel,
        "first_vector",
        (
            live,
            coef,
            perm,
            edges,
            source_f,
            weight,
            near_a,
            near_b,
            far_c,
            far_d,
            *network,
            oy,
            ox,
            margin_in,
            column,
            v0,
        ),
        [
            ((6, x_cells, y_cells), F32),
            (own, F32),
            ((half, rows), F32),
            ((2, half, frac_cells), F32),
            ((half, rows), F32),
            (own, F32),
            ((edge_rows + 3 * half, LANES), F32),
            ((edge_rows + 3 * half, LANES), F32),
            ((3 * half, LANES), F32),
            ((core_rows + 8 * frac_blocks, LANES), F32),
            (field, F32),
        ],
        scratch=[pltpu.VMEM((members, frac_cells), F32)],
        aliases={21: 10},
    )
    near_rows = edge_rows + 2 * half

    def interior(power, v, before, vf, before_f, core_in):
        outs = [(field, F32), ((members, margin), F32), ((x_cells, LANES), F32)]
        return call(
            functools.partial(interior_kernel, power),
            f"interior_{power}",
            (v, before, vf, before_f, core_in, scale_f, unit, weight, ofrac, oy, ox),
            outs + [((8, members), F32)],
            scratch=[pltpu.VMEM((members, margin), F32), pltpu.VMEM((members, frac_cells), F32)]
            + [pltpu.VMEM((members, LANES), F32)] * power,
            cost=hidden,
        )

    finish_outs = [
        (own, F32),
        ((half, rows), F32),
        (own, F32),
        ((near_rows, LANES), F32),
        ((near_rows, LANES), F32),
        ((2 * half, LANES), F32),
        ((core_rows, LANES), F32),
        (field, F32),
    ]
    finish_scratch = [pltpu.VMEM((members, frac_cells), F32)]

    near_a, near_b, far_c, far_d, core_in = exchange(to_a, to_b, sent, core_msg)
    image, margin_in, column, dots1 = interior(1, v0, v0, f0, f0, core_in)
    own_f, f1, diff, wown, to_a, to_b, sent, core_msg, v1 = call(
        functools.partial(finish_kernel, 1),
        "finish_1",
        (f0, near_a, near_b, far_c, far_d, core_in, diff, wown, sr, scale_f, unit, table, ghost_table)
        + (wsum, weight, ofrac, oy, ox, margin_in, column, image),
        [(own, F32)] + finish_outs,
        scratch=finish_scratch,
        aliases={20: 8},
    )
    near_a, near_b, far_c, far_d, core_in = exchange(to_a, to_b, sent, core_msg)
    image, margin_in, column, dots2 = interior(2, v1, v0, f1, f0, core_in)
    f2, diff, margin_in, to_a, to_b, sent, core_msg, v2 = call(
        functools.partial(finish_kernel, 2),
        "finish_2",
        (f1, near_a, near_b, far_c, far_d, core_in, diff, wown, sr, scale_f, unit, table, ghost_table)
        + (own_f, weight, ofrac, oy, ox, margin_in, column, image),
        [
            (own, F32),
            ((half, rows), F32),
            ((members, margin), F32),
            ((edge_rows // 2 + half, LANES), F32),
            ((edge_rows // 2 + half, LANES), F32),
            ((half, LANES), F32),
            ((frac_blocks * half + x_cells, LANES), F32),
            (field, F32),
        ],
        aliases={20: 7},
    )
    near_a, near_b, far_c, far_d, core_in = exchange(to_a, to_b, sent, core_msg)
    (dots3,) = call(
        energy_kernel,
        "energy",
        (v2, v1, f2, f1, core_in, scale_f, unit, coef, storage_in, weight, ofrac, margin_in),
        [((8, members), F32)],
        scratch=[pltpu.VMEM((members, frac_cells), F32)] + [pltpu.VMEM((members, LANES), F32)] * 3,
        cost=hidden,
    )
    peers = count * lax.axis_size("gy")
    (moments,) = call(
        moments_kernel,
        "moments",
        (f2, near_a, near_b, far_c, far_d, diff, sr, unit, ghost_table, v2, dots1, dots2, dots3),
        [((peers, 2, LANES), F32)],
        scratch=[pltpu.VMEM((members, LANES), F32)],
    )
    totals = lax.all_to_all(moments, ("gx", "gy"), 0, 0)
    return call(
        close_kernel,
        "iterate",
        (totals, v0, v1, v2, f0, f1, f2),
        [(field, F32), (own, F32)],
        scratch=[
            pltpu.VMEM((3, LANES, LANES), F32),
            pltpu.VMEM(field, F32),
            pltpu.VMEM(own, F32),
            pltpu.SemaphoreType.DMA((5,)),
        ],
        far_out=True,
    )


def solution(mesh):
    placed = (
        P("grp", "gx", "gy"),
        P(("grp", "gy"), "gx"),
        P(("grp", "gy"), "gx"),
        P("gx", "gy"),
        P("gx", "gy"),
        P(),
        P("gx", None),
        P("gx", None),
        P("gx", None),
        P("gx"),
        P("gx", "gy", None, None),
        P("gx", "gy", None, None),
        P("gx", "gy", None, None),
        P("gx", "gy", None),
    )
    return jax.shard_map(
        per_device,
        mesh=mesh,
        in_specs=placed,
        out_specs=(P("grp", "gx", "gy"), P(("grp", "gy"), "gx")),
        check_vma=False,
    )
```

```python
import functools

import jax
import jax.numpy as jnp
from jax import lax
from jax.experimental import pallas as pl
from jax.experimental.pallas import tpu as pltpu
from jax.sharding import PartitionSpec as P

FRACTURE_STORAGE = 0.1
F32 = jnp.float32
BF16 = jnp.bfloat16
LANES = 128
GROUP = 32


def split3(x):
    high = x.astype(BF16)
    rest = x - high.astype(F32)
    mid = rest.astype(BF16)
    low = (rest - mid.astype(F32)).astype(BF16)
    return jnp.concatenate([high, mid, low], axis=0)


def pick(x, table, transposed=False):
    rows = x.shape[0]
    dims = (((1,), (1 if transposed else 0,)), ((), ()))
    out = lax.dot_general(split3(x), table, dims, preferred_element_type=F32)
    return out[:rows] + out[rows : 2 * rows] + out[2 * rows :]


def fetch(sources, targets, sems):
    copies = [pltpu.make_async_copy(a, b, sems.at[k]) for k, (a, b) in enumerate(zip(sources, targets))]
    for copy in copies:
        copy.start()
    return copies


class Place:
    def __init__(self):
        count = lax.axis_size("gx")
        i = lax.axis_index("gx")
        self.j = lax.axis_index("gy")
        self.high_side = self.j == 0
        self.even = lax.rem(i, 2) == 0
        self.low_pair = lax.rem(lax.div(i, 2), 2) == 0
        self.first = i == 0
        self.last = i == count - 1


def harmonic(first_perm, second_perm):
    return 2.0 * first_perm * second_perm / (first_perm + second_perm)


def one_hot(index_row, size):
    shape = (size, index_row.shape[1])
    ids = lax.broadcasted_iota(jnp.int32, shape, 0)
    return jnp.where(ids == index_row, 1.0, 0.0).astype(BF16)


def to_blocks(x):
    return jnp.concatenate(
        [x[:, q : q + LANES] for q in range(0, x.shape[1], LANES)], axis=0
    )


def from_blocks(x, rows):
    return jnp.concatenate(
        [x[q : q + rows] for q in range(0, x.shape[0], rows)], axis=1
    )


def by_group(first, second, third, fourth):
    group = first.shape[1] // 4
    lane = lax.broadcasted_iota(jnp.int32, first.shape, 1)
    return jnp.where(
        lane < group,
        first,
        jnp.where(lane < 2 * group, second, jnp.where(lane < 3 * group, third, fourth)),
    )


def total_rows(x):
    return jnp.sum(jnp.transpose(x), axis=0, keepdims=True)


def fold_lanes(x):
    rows, width = x.shape
    out = x[:, :LANES]
    for q in range(LANES, width, LANES):
        out = out + x[:, q : q + LANES]
    return out


def opening_kernel(
    perm_table_hbm,
    class_hbm,
    aperture_hbm,
    slots_hbm,
    perm_ref,
    cond_ref,
    oslot_ref,
    near_a_ref,
    near_b_ref,
    far_ref,
    border_ref,
    perm_table_ref,
    class_ref,
    aperture_ref,
    slots_ref,
    sems,
):
    copies = fetch(
        (class_hbm, perm_table_hbm, aperture_hbm, slots_hbm),
        (class_ref, perm_table_ref, aperture_ref, slots_ref),
        sems,
    )
    for copy in copies:
        copy.wait()
    x_cells, y_cells = class_ref.shape
    half = aperture_ref.shape[0]
    here = Place()
    classes = class_ref[...]
    perm = jnp.zeros(classes.shape, F32)
    for index in range(perm_table_ref.shape[0]):
        perm = jnp.where(classes == index, perm_table_ref[index], perm)
    perm_ref[...] = perm
    border_ref[...] = jnp.where(here.high_side, perm[:, y_cells - LANES :], perm[:, :LANES])

    aperture = aperture_ref[...]
    cond = aperture * aperture * aperture
    cond_ref[...] = cond
    oslot = one_hot(slots_ref[...], cond.shape[1])
    oslot_ref[...] = oslot
    supplied = pick(cond, oslot)
    far_ref[...] = supplied
    up, down = to_blocks(perm[x_cells - 1 :]), to_blocks(perm[:1])
    blocks = up.shape[0]
    pad = jnp.zeros((near_a_ref.shape[0] - half - blocks, LANES), F32)
    for ref, edge in ((near_a_ref, jnp.where(here.even, up, down)), (near_b_ref, jnp.where(here.even, down, up))):
        ref[...] = jnp.concatenate([supplied, edge, pad], axis=0)


def neighbours(here, near_a_ref, near_b_ref, far_c_ref, far_d_ref):
    def reader(flag, at_zero, at_one):
        return lambda at, size: jnp.where(
            flag, at_zero[at : at + size, :], at_one[at : at + size, :]
        )

    return (
        reader(here.even, near_a_ref, near_b_ref),
        reader(here.even, near_b_ref, near_a_ref),
        reader(here.low_pair, far_c_ref, far_d_ref),
        reader(here.low_pair, far_d_ref, far_c_ref),
    )


def margin_values(found, ox):
    found = found.reshape(-1, *ox.shape) * ox[None]
    return jnp.sum(found, axis=1)


def border_column(tile_low, tile_high, high_side, m):
    tile = jnp.where(high_side, tile_high, tile_low)
    return pltpu.roll(tile, jnp.where(high_side, lax.rem(m + 1, LANES), m), 1)


def border_row(row_values, high_side):
    members, y_cells = row_values.shape
    tile = jnp.where(high_side, row_values[:, y_cells - LANES :], row_values[:, :LANES])
    turned = jnp.transpose(tile)
    line = jnp.where(high_side, turned[LANES - 1 :], turned[:1])
    return jnp.concatenate([line, jnp.zeros((1, LANES - members), F32)], axis=1)


def finish_edges(high_rows, low_rows, partial_ref, column, high_side, oy, ox):
    members = high_rows.shape[0]
    x_cells = ox.shape[0]
    found = pick(jnp.concatenate([high_rows, low_rows], axis=0), oy)
    margin = partial_ref[...] + found[:members] * ox[x_cells - 1 :] + found[members:] * ox[:1]
    row = lax.broadcasted_iota(jnp.int32, column.shape, 0)
    column = jnp.where(row == x_cells - 1, border_row(high_rows, high_side), column)
    return margin, jnp.where(row == 0, border_row(low_rows, high_side), column)


def send_network(vf, sr, table, ghost_table, diff_ref, refs):
    half = vf.shape[0]
    rows = diff_ref.shape[1]
    found = pick(vf, table)
    diff_ref[...] = found[:, :rows]
    if sr is None:
        for ref, at in refs:
            ref[at : at + half, :] = found[:, rows:]
        return
    sums = pick(sr * found[:, :rows], ghost_table, True)
    for ref, at in refs:
        ref[at : at + half, :] = found[:, rows:]
        ref[at + half : at + 2 * half, :] = sums


def send_core(core_ref, vf, margin, weight, ofrac, column, j, work_ref, wown_ref):
    half, frac_cells = vf.shape
    work_ref[...] = pick(margin * weight, ofrac, True)
    wown_ref[...] = work_ref[pl.ds(pl.multiple_of(j * half, half), half), :]
    other = work_ref[pl.ds(pl.multiple_of((1 - j) * half, half), half), :]
    size = frac_cells // LANES * half
    core_ref[0:size, :] = to_blocks(vf)
    core_ref[size : 2 * size, :] = to_blocks(other)
    core_ref[2 * size : 2 * size + column.shape[0], :] = column


def inside_kernel(
    ov_count_hbm,
    isect_count_hbm,
    storage_hbm,
    source_hbm,
    source_f_hbm,
    cell_hbm,
    ov_weight_hbm,
    local_hbm,
    other_hbm,
    frac_hbm,
    perm_ref,
    border_ref,
    oslot_ref,
    cond_ref,
    source_f_ref,
    storage_ref,
    live_ref,
    edge_ref,
    coef_ref,
    oy_ref,
    ox_ref,
    weight_ref,
    first_ref,
    cond_first_ref,
    cond_second_ref,
    wsum_ref,
    table_ref,
    ghost_table_ref,
    ofrac_ref,
    v_ref,
    margin_ref,
    column_ref,
    ov_count_ref,
    isect_count_ref,
    source_ref,
    cell_ref,
    ov_weight_ref,
    local_ref,
    other_in_ref,
    frac_ref,
    sems,
):
    members, x_cells, y_cells = source_ref.shape
    frac_cells = table_ref.shape[0]
    here = Place()
    high_side = here.high_side
    copies = fetch(
        (
            cell_hbm,
            local_hbm,
            other_hbm,
            frac_hbm,
            ov_weight_hbm,
            ov_count_hbm,
            isect_count_hbm,
            storage_hbm,
            source_f_hbm,
            source_hbm,
        ),
        (
            cell_ref,
            local_ref,
            other_in_ref,
            frac_ref,
            ov_weight_ref,
            ov_count_ref,
            isect_count_ref,
            storage_ref,
            source_f_ref,
            source_ref,
        ),
        sems,
    )

    def line(ref):
        return jnp.concatenate([ref[k : k + 1, :] for k in range(ref.shape[0])], axis=1)

    rows = local_ref.size
    perm, border = perm_ref[...], border_ref[...]
    col = jnp.where(high_side, border[:, :1], border[:, LANES - 1 :])
    lane = lax.broadcasted_iota(jnp.int32, perm.shape, 1)
    row = lax.broadcasted_iota(jnp.int32, perm.shape, 0)
    north = jnp.concatenate([perm[:, 1:], col], axis=1)
    south = jnp.concatenate([col, perm[:, :-1]], axis=1)
    tn = jnp.where((lane == y_cells - 1) & jnp.logical_not(high_side), 0.0, harmonic(perm, north))
    ts = jnp.where((lane == 0) & high_side, 0.0, harmonic(perm, south))
    east = jnp.concatenate([perm[1:], perm[:1]], axis=0)
    west = jnp.concatenate([perm[-1:], perm[:-1]], axis=0)
    te = jnp.where(row == x_cells - 1, 0.0, harmonic(perm, east))
    tw = jnp.where(row == 0, 0.0, harmonic(perm, west))
    for copy in copies[:-1]:
        copy.wait()
    cell = line(cell_ref)
    oy = one_hot(cell % y_cells, y_cells)
    oy_ref[...] = oy
    row_x = lax.broadcasted_iota(jnp.int32, ox_ref.shape, 0)
    at_x = row_x == cell // y_cells
    ox = jnp.where(at_x, 1.0, 0.0)
    ox_ref[...] = ox
    lane_w = lax.broadcasted_iota(jnp.int32, (1, LANES), 1)
    weight = jnp.concatenate(
        [jnp.where(lane_w < ov_count_ref[k], ov_weight_ref[k : k + 1, :], 0.0) for k in range(ov_weight_ref.shape[0])],
        axis=1,
    )
    weight_ref[...] = weight
    for block in range(local_ref.shape[0]):
        at = slice(block * LANES, (block + 1) * LANES)
        live_ref[:, at] = jnp.where(lane_w < isect_count_ref[block], 1.0, 0.0)
    part = storage_ref[...] + te + tw + tn + ts + pick(jnp.where(at_x, weight, 0.0), oy, True)
    coef_ref[0] = te
    coef_ref[1] = tw
    coef_ref[2] = tn
    coef_ref[3] = ts
    coef_ref[4] = part

    other = line(other_in_ref)
    first, second = one_hot(line(local_ref), frac_cells), one_hot(other, frac_cells)
    first_ref[...] = first
    cond = cond_ref[...]
    cond_first_ref[...] = pick(cond, first)
    cond_second_ref[...] = pick(cond, second)
    table_ref[:, :rows] = first - second
    table_ref[:, rows:] = oslot_ref[...]
    ghost_table_ref[...] = one_hot(other - frac_cells, ghost_table_ref.shape[0])
    ofrac = one_hot(line(frac_ref), frac_cells)
    ofrac_ref[...] = ofrac
    wsum_ref[...] = pick(jnp.broadcast_to(weight, (8, weight.shape[1])), ofrac, True)

    inverse = 1.0 / part
    inner_x = jnp.where((row_x == 0) | (row_x == x_cells - 1), 0.0, ox)
    lane_c = lax.broadcasted_iota(jnp.int32, (x_cells, LANES), 1)
    column_ref[...] = jnp.zeros_like(column_ref)
    copies[-1].wait()
    edge_ref[0] = source_ref[:, x_cells - 1, :]
    edge_ref[1] = source_ref[:, 0, :]

    @pl.loop(0, members // GROUP)
    def _(index):
        start = index * GROUP
        block = source_ref[pl.ds(start, GROUP)] * inverse[None]
        v_ref[pl.ds(start, GROUP)] = block
        found = pick(block.reshape(GROUP * x_cells, y_cells), oy_ref[...])
        margin_ref[pl.ds(start, GROUP), :] = margin_values(found, inner_x)
        column = column_ref[...]
        for k in range(GROUP):
            m = start + k
            moved = border_column(block[k, :, :LANES], block[k, :, y_cells - LANES :], high_side, m)
            column = jnp.where(lane_c == m, moved, column)
        column_ref[...] = column


def first_kernel(
    live_ref,
    coef_ref,
    perm_ref,
    edge_ref,
    source_f_ref,
    weight_ref,
    near_a_ref,
    near_b_ref,
    far_c_ref,
    far_d_ref,
    first_ref,
    cond_first_ref,
    cond_second_ref,
    wsum_ref,
    table_ref,
    ghost_table_ref,
    ofrac_ref,
    oy_ref,
    ox_ref,
    inner_margin_ref,
    inner_column_ref,
    v_in_ref,
    unit_ref,
    vf_ref,
    sr_ref,
    scale_f_ref,
    diff_ref,
    wown_ref,
    to_a_ref,
    to_b_ref,
    sent_ref,
    core_ref,
    v_ref,
    work_ref,
):
    members, x_cells, y_cells = v_ref.shape
    half, frac_cells = source_f_ref.shape
    blocks = y_cells // LANES
    here = Place()
    j, high_side = here.j, here.high_side
    base = blocks * members
    plus1, minus1, plus2, minus2 = neighbours(here, near_a_ref, near_b_ref, far_c_ref, far_d_ref)

    ghosts = by_group(minus1(0, half), plus1(0, half), minus2(0, half), plus2(0, half))
    table, ghost_table = table_ref[...], ghost_table_ref[...]
    cond_first = cond_first_ref[...]
    cond_second = cond_second_ref[...] + pick(ghosts, ghost_table)
    sr = jnp.where(live_ref[...] > 0.0, harmonic(cond_first, cond_second), 0.0)
    sr_ref[...] = sr
    diag_f = FRACTURE_STORAGE + pick(sr, first_ref[...], True)
    inverse_f = 1.0 / diag_f
    scale_f_ref[0] = inverse_f
    scale_f_ref[1] = diag_f
    vf = source_f_ref[...] * inverse_f
    vf_ref[...] = vf
    refs = [(to_a_ref, base), (to_b_ref, base), (sent_ref, 0)]
    send_network(vf, sr, table, ghost_table, diff_ref, refs)
    slot_sums = pick(sr, ghost_table, True)
    for ref, at in refs:
        ref[at + 2 * half : at + 3 * half, :] = slot_sums

    perm, part = perm_ref[...], coef_ref[4]
    row = lax.broadcasted_iota(jnp.int32, perm.shape, 0)
    perm_plus = from_blocks(plus1(half, blocks), 1)
    perm_minus = from_blocks(minus1(half, blocks), 1)
    te_edge = jnp.where(here.last, 0.0, harmonic(perm[x_cells - 1 :], perm_plus))
    tw_edge = jnp.where(here.first, 0.0, harmonic(perm[:1], perm_minus))
    te = jnp.where(row == x_cells - 1, te_edge, coef_ref[0])
    tw = jnp.where(row == 0, tw_edge, coef_ref[1])
    diag = part + jnp.where(row == x_cells - 1, te_edge, 0.0) + jnp.where(row == 0, tw_edge, 0.0)
    inverse = 1.0 / diag
    unit_ref[0] = te * inverse
    unit_ref[1] = tw * inverse
    unit_ref[2] = coef_ref[2] * inverse
    unit_ref[3] = coef_ref[3] * inverse
    unit_ref[4] = inverse
    unit_ref[5] = diag
    high_rows = edge_ref[0] * inverse[x_cells - 1 :]
    low_rows = edge_ref[1] * inverse[:1]
    v_ref[:, x_cells - 1, :] = high_rows
    v_ref[:, 0, :] = low_rows
    to_a_ref[0:base, :] = to_blocks(jnp.where(here.even, high_rows, low_rows))
    to_b_ref[0:base, :] = to_blocks(jnp.where(here.even, low_rows, high_rows))
    margin, column = finish_edges(
        high_rows, low_rows, inner_margin_ref, inner_column_ref[...], high_side, oy_ref[...], ox_ref[...]
    )
    weight = weight_ref[...]
    send_core(core_ref, vf, margin, weight, ofrac_ref[...], column, j, work_ref, wown_ref)
    tail = core_ref.shape[0] - 8 * (frac_cells // LANES)
    core_ref[tail:, :] = to_blocks(wsum_ref[...])


def interior_kernel(
    power,
    v_ref,
    before_ref,
    vf_ref,
    before_f_ref,
    core_ref,
    scale_f_ref,
    unit_ref,
    weight_ref,
    ofrac_ref,
    oy_ref,
    ox_ref,
    *refs,
):
    image_ref, margin_ref, column_ref, dots_ref, flow_ref, work_ref, *acc_refs = refs
    members, x_cells, y_cells = v_ref.shape
    half, frac_cells = vf_ref.shape
    blocks = y_cells // LANES
    here = Place()
    j, high_side = here.j, here.high_side
    size = frac_cells // LANES * half
    theirs = from_blocks(core_ref[0:size, :], half)
    column_in = core_ref[2 * size : 2 * size + x_cells, :]
    vf = vf_ref[...]
    own_rows = pl.ds(pl.multiple_of(j * half, half), half)
    work_ref[own_rows, :] = vf
    work_ref[pl.ds(pl.multiple_of((1 - j) * half, half), half), :] = theirs
    flow_ref[...] = pick(work_ref[...], ofrac_ref[...]) * weight_ref[...]

    heavy_f = vf * scale_f_ref[1]
    for ref in acc_refs:
        ref[...] = jnp.zeros_like(ref)
    acc_refs[0][own_rows, :] = fold_lanes(vf * heavy_f)
    if power > 1:
        acc_refs[1][own_rows, :] = fold_lanes(before_f_ref[...] * heavy_f)

    lane_c = lax.broadcasted_iota(jnp.int32, (x_cells, LANES), 1)
    lane = lax.broadcasted_iota(jnp.int32, (x_cells, y_cells), 1)
    row = lax.broadcasted_iota(jnp.int32, (x_cells, y_cells), 0)
    row_x = lax.broadcasted_iota(jnp.int32, ox_ref.shape, 0)
    oy, ox = oy_ref[...], ox_ref[...]
    inner_x = jnp.where((row_x == 0) | (row_x == x_cells - 1), 0.0, ox)
    te = jnp.where(row == x_cells - 1, 0.0, unit_ref[0])
    tw = jnp.where(row == 0, 0.0, unit_ref[1])
    column_ref[...] = jnp.zeros_like(column_ref)

    @pl.loop(0, members // GROUP)
    def _(index):
        start = index * GROUP
        parts = []
        for k in range(GROUP):
            parts.append(ox * flow_ref[pl.ds(start + k, 1), :])
        coupled = pick(jnp.concatenate(parts, axis=0), oy, True)
        column = column_ref[...]
        for k in range(GROUP):
            m = start + k
            value = v_ref[m]
            east = pltpu.roll(value, x_cells - 1, 0)
            west = pltpu.roll(value, 1, 0)
            moved = pltpu.roll(column_in, jnp.where(high_side, LANES - 1 - m, lax.rem(LANES - m, LANES)), 1)
            moved = jnp.concatenate([moved] * blocks, axis=1)
            north = jnp.where(lane == y_cells - 1, moved, pltpu.roll(value, y_cells - 1, 1))
            south = jnp.where(lane == 0, moved, pltpu.roll(value, 1, 1))
            image = value - te * east - tw * west - unit_ref[2] * north - unit_ref[3] * south
            image = image - coupled[k * x_cells : (k + 1) * x_cells] * unit_ref[4]
            heavy = value * unit_ref[5]
            at = pl.ds(m, 1)
            acc_refs[0][at, :] += jnp.sum(fold_lanes(value * heavy), axis=0, keepdims=True)
            if power > 1:
                acc_refs[1][at, :] += jnp.sum(fold_lanes(before_ref[m] * heavy), axis=0, keepdims=True)
            image_ref[m] = image
            shifted = border_column(image[:, :LANES], image[:, y_cells - LANES :], high_side, m)
            column = jnp.where(lane_c == m, shifted, column)
        column_ref[...] = column
        block = image_ref[pl.ds(start, GROUP)]
        found = pick(block.reshape(GROUP * x_cells, y_cells), oy)
        margin_ref[pl.ds(start, GROUP), :] = margin_values(found, inner_x)

    dots = [total_rows(ref[...]) for ref in acc_refs]
    dots.append(jnp.zeros((8 - len(dots), members), F32))
    dots_ref[...] = jnp.concatenate(dots, axis=0)


def finish_kernel(
    power,
    vf_ref,
    near_a_ref,
    near_b_ref,
    far_c_ref,
    far_d_ref,
    core_in_ref,
    diff_in_ref,
    wown_in_ref,
    sr_ref,
    scale_f_ref,
    unit_ref,
    table_ref,
    ghost_table_ref,
    *refs,
):
    own_f_in_ref, *refs = refs
    weight_ref, ofrac_ref, oy_ref, ox_ref, inner_margin_ref, inner_column_ref, image_in_ref, *refs = refs
    if power == 1:
        own_f_ref, out_f_ref, diff_ref, wown_ref, to_a_ref, to_b_ref, sent_ref, core_ref, image_ref, work_ref = refs
    else:
        out_f_ref, diff_ref, margin_ref, to_a_ref, to_b_ref, sent_ref, core_ref, image_ref = refs
    half, frac_cells = vf_ref.shape
    x_cells, y_cells = unit_ref.shape[1:]
    members = image_ref.shape[0]
    blocks = y_cells // LANES
    frac_blocks = frac_cells // LANES
    here = Place()
    j, high_side = here.j, here.high_side
    base = blocks * members
    plus1, minus1, plus2, minus2 = neighbours(here, near_a_ref, near_b_ref, far_c_ref, far_d_ref)
    rows = sr_ref.shape[1]

    table, ghost_table = table_ref[...], ghost_table_ref[...]
    vf = vf_ref[...]
    ghosts = by_group(minus1(base, half), plus1(base, half), minus2(0, half), plus2(0, half))
    sums = by_group(
        plus1(base + half, half), minus1(base + half, half), plus2(half, half), minus2(half, half)
    )
    size = frac_blocks * half
    their_sums = from_blocks(core_in_ref[size : 2 * size, :], half)
    if power == 1:
        at = 2 * half
        back = by_group(
            plus1(base + at, half), minus1(base + at, half), plus2(at, half), minus2(at, half)
        )
        tail = core_in_ref.shape[0] - 8 * frac_blocks
        wsum = own_f_in_ref[...] + from_blocks(core_in_ref[tail:, :], 8)
        own_f = FRACTURE_STORAGE + wsum[:1] + pick(back, table[:, rows:], True)
        own_f_ref[...] = own_f
    else:
        own_f = own_f_in_ref[...]
    sr = sr_ref[...]
    flux = sr * (diff_in_ref[...] - pick(ghosts, ghost_table))
    image_f = own_f * vf + pick(jnp.concatenate([flux, -sums], axis=1), table, True)
    image_f = image_f - wown_in_ref[...] - their_sums

    next_f = image_f * scale_f_ref[0]
    out_f_ref[...] = next_f
    edge_size = base if power == 1 else base // 2
    refs = [(to_a_ref, edge_size), (to_b_ref, edge_size), (sent_ref, 0)]
    send_network(next_f, sr if power == 1 else None, table, ghost_table, diff_ref, refs)

    edges = []
    for side, at, reader in ((0, x_cells - 1, plus1), (1, 0, minus1)):
        beyond = from_blocks(reader(0, base), members)
        edge = image_in_ref[:, at, :] - unit_ref[side, at : at + 1, :] * beyond
        image_ref[:, at, :] = edge
        edges.append(edge)
    up, down = edges
    if power == 2:
        up, down = up[:, : y_cells // 2], down[:, y_cells // 2 :]
    to_a_ref[0:edge_size, :] = to_blocks(jnp.where(here.even, up, down))
    to_b_ref[0:edge_size, :] = to_blocks(jnp.where(here.even, down, up))
    margin, column = finish_edges(
        edges[0], edges[1], inner_margin_ref, inner_column_ref[...], high_side, oy_ref[...], ox_ref[...]
    )
    if power == 1:
        send_core(core_ref, next_f, margin, weight_ref[...], ofrac_ref[...], column, j, work_ref, wown_ref)
    else:
        margin_ref[...] = margin
        core_ref[0:size, :] = to_blocks(next_f)
        core_ref[size : size + x_cells, :] = column


def energy_kernel(
    v_ref,
    before_ref,
    vf_ref,
    before_f_ref,
    core_ref,
    scale_f_ref,
    unit_ref,
    coef_ref,
    storage_ref,
    weight_ref,
    ofrac_ref,
    margin_ref,
    dots_ref,
    work_ref,
    acc0_ref,
    acc1_ref,
    acc2_ref,
):
    members, x_cells, y_cells = v_ref.shape
    half, frac_cells = vf_ref.shape
    blocks = y_cells // LANES
    here = Place()
    size = frac_cells // LANES * half
    theirs = from_blocks(core_ref[0:size, :], half)
    column_in = core_ref[size : size + x_cells, :]
    vf = vf_ref[...]
    own_rows = pl.ds(pl.multiple_of(here.j * half, half), half)
    work_ref[own_rows, :] = vf
    work_ref[pl.ds(pl.multiple_of((1 - here.j) * half, half), half), :] = theirs
    gap = margin_ref[...] - pick(work_ref[...], ofrac_ref[...])
    acc2_ref[...] = fold_lanes(weight_ref[...] * gap * gap)
    heavy_f = vf * scale_f_ref[1]
    acc0_ref[...] = jnp.zeros_like(acc0_ref)
    acc1_ref[...] = jnp.zeros_like(acc1_ref)
    acc0_ref[own_rows, :] = fold_lanes(vf * heavy_f)
    acc1_ref[own_rows, :] = fold_lanes(before_f_ref[...] * heavy_f)
    lane = lax.broadcasted_iota(jnp.int32, (x_cells, y_cells), 1)
    diag, te, tn, storage = unit_ref[5], coef_ref[0], coef_ref[2], storage_ref[...]

    @pl.loop(0, members // GROUP)
    def _(index):
        start = index * GROUP
        for k in range(GROUP):
            m = start + k
            value = v_ref[m]
            east = value - pltpu.roll(value, x_cells - 1, 0)
            moved = pltpu.roll(column_in, LANES - 1 - m, 1)
            moved = jnp.concatenate([moved] * blocks, axis=1)
            north = value - jnp.where(lane == y_cells - 1, moved, pltpu.roll(value, y_cells - 1, 1))
            energy = storage * value * value + te * east * east + tn * north * north
            heavy = value * diag
            at = pl.ds(m, 1)
            acc0_ref[at, :] += jnp.sum(fold_lanes(value * heavy), axis=0, keepdims=True)
            acc1_ref[at, :] += jnp.sum(fold_lanes(before_ref[m] * heavy), axis=0, keepdims=True)
            acc2_ref[at, :] += jnp.sum(fold_lanes(energy), axis=0, keepdims=True)

    dots = [total_rows(ref[...]) for ref in (acc0_ref, acc1_ref, acc2_ref)]
    dots.append(jnp.zeros((8 - len(dots), members), F32))
    dots_ref[...] = jnp.concatenate(dots, axis=0)


def moments_kernel(
    vf_ref,
    near_a_ref,
    near_b_ref,
    far_c_ref,
    far_d_ref,
    diff_in_ref,
    sr_ref,
    unit_ref,
    ghost_table_ref,
    v_ref,
    dots1_ref,
    dots2_ref,
    dots3_ref,
    moments_ref,
    acc_ref,
):
    half = vf_ref.shape[0]
    members, x_cells, y_cells = v_ref.shape
    middle = y_cells // 2
    base = middle // LANES * members
    here = Place()
    plus1, minus1, plus2, minus2 = neighbours(here, near_a_ref, near_b_ref, far_c_ref, far_d_ref)
    vf = vf_ref[...]
    ghosts = by_group(minus1(base, half), plus1(base, half), minus2(0, half), plus2(0, half))
    gap = diff_in_ref[...] - pick(ghosts, ghost_table_ref[...])
    acc_ref[...] = jnp.zeros_like(acc_ref)
    own_rows = pl.ds(pl.multiple_of(here.j * half, half), half)
    acc_ref[own_rows, :] = fold_lanes(sr_ref[...] * gap * gap) + fold_lanes(FRACTURE_STORAGE * vf * vf)
    for side, at, reader, cut in (
        (0, x_cells - 1, plus1, slice(middle, y_cells)),
        (1, 0, minus1, slice(0, middle)),
    ):
        trans = unit_ref[side, at : at + 1, cut] * unit_ref[5, at : at + 1, cut]
        edge = v_ref[:, at, cut] - from_blocks(reader(0, base), members)
        acc_ref[...] += fold_lanes(trans * edge * edge)
    last = total_rows(acc_ref[...]) + dots3_ref[2:3, :]
    blank = jnp.zeros((1, LANES - 3 * members), F32)
    lines = [
        jnp.concatenate([dots1_ref[0:1, :], dots2_ref[1:2, :], dots2_ref[0:1, :], blank], axis=1),
        jnp.concatenate([dots3_ref[1:2, :], dots3_ref[0:1, :], last, blank], axis=1),
    ]
    lines = jnp.concatenate(lines, axis=0)
    moments_ref[...] = jnp.broadcast_to(lines[None], moments_ref.shape)


def close_kernel(totals_ref, v0_ref, v1_ref, v2_ref, f0_ref, f1_ref, f2_ref, x_hbm, xf_hbm, c_ref, x_ref, xf_ref, sems):
    members, x_cells, y_cells = v0_ref.shape
    half, frac_cells = f0_ref.shape

    total = jnp.sum(totals_ref[...], axis=0)
    m0, m1, m2, m3, m4, m5 = (
        total[k // 3 : k // 3 + 1, k % 3 * members : k % 3 * members + members] for k in range(6)
    )
    alpha0 = m0 / m1
    rz1 = m0 - 2.0 * alpha0 * m1 + alpha0 * alpha0 * m2
    beta1 = rz1 / m0
    a, b = 1.0 + beta1, -alpha0
    pap1 = a * a * m1 + 2.0 * a * b * m2 + b * b * m3
    alpha1 = rz1 / pap1
    e = -alpha0 - alpha1 * a
    g = -alpha1 * b
    rz2 = m0 + 2.0 * e * m1 + (e * e + 2.0 * g) * m2 + 2.0 * e * g * m3 + g * g * m4
    beta2 = rz2 / rz1
    c = 1.0 + beta2 * a
    d = e + beta2 * b
    pap2 = c * c * m1 + 2.0 * c * d * m2 + (d * d + 2.0 * c * g) * m3 + 2.0 * d * g * m4 + g * g * m5
    alpha2 = rz2 / pap2
    c0 = alpha0 + alpha1 * a + alpha2 * c
    c1 = alpha1 * b + alpha2 * d
    c2 = alpha2 * g
    for k, row in enumerate((c0, c1, c2)):
        row = jnp.concatenate([row, jnp.zeros((1, LANES - members), F32)], axis=1)
        c_ref[k] = jnp.transpose(jnp.broadcast_to(row, (LANES, LANES)))
    j = lax.axis_index("gy")
    own = pl.ds(pl.multiple_of(j * half, half), half)

    def wide(k, rows, width):
        return jnp.concatenate([c_ref[k, rows, :]] * (width // LANES), axis=1)

    xf_ref[...] = (
        wide(0, own, frac_cells) * f0_ref[...]
        + wide(1, own, frac_cells) * f1_ref[...]
        + wide(2, own, frac_cells) * f2_ref[...]
    )

    copies = fetch((xf_ref,), (xf_hbm,), sems)
    pieces = sems.shape[0] - 1
    piece = members // pieces
    for index in range(pieces):

        @pl.loop(index * piece, (index + 1) * piece)
        def _(m):
            rows = pl.ds(m, 1)
            x_ref[m] = (
                wide(0, rows, y_cells) * v0_ref[m]
                + wide(1, rows, y_cells) * v1_ref[m]
                + wide(2, rows, y_cells) * v2_ref[m]
            )

        part = pl.ds(index * piece, piece)
        copies.append(pltpu.make_async_copy(x_ref.at[part], x_hbm.at[part], sems.at[1 + index]))
        copies[-1].start()
    for copy in copies:
        copy.wait()


def pairs_of(count, stride, phase):
    out = []
    for index in range(count):
        if (index // stride) % 2 == phase:
            mate = (index + stride) % count
            out += [(index, mate), (mate, index)]
    return out


VMEM = pl.BlockSpec(memory_space=pltpu.VMEM)


HBM = pl.BlockSpec(memory_space=pltpu.HBM)


def call(kernel, name, args, outs, scratch=(), far_in=0, far_out=False, cost=None, aliases=None):
    args = [pltpu.with_memory_space_constraint(arg, pltpu.HBM) for arg in args[:far_in]] + list(args[far_in:])
    return pl.pallas_call(
        kernel,
        name=name,
        out_shape=[jax.ShapeDtypeStruct(shape, dtype) for shape, dtype in outs],
        in_specs=[HBM] * far_in + [VMEM] * (len(args) - far_in),
        out_specs=[HBM if far_out else VMEM] * len(outs),
        scratch_shapes=list(scratch),
        compiler_params=pltpu.CompilerParams(vmem_limit_bytes=40 * 1024 * 1024),
        cost_estimate=cost,
        input_output_aliases=aliases or {},
    )(*args)


def per_device(
    source_matrix,
    source_fracture,
    aperture,
    storage,
    perm_class,
    class_perm,
    send_slots,
    isect_local,
    isect_other,
    isect_count,
    ov_cell,
    ov_frac,
    ov_weight,
    ov_count,
):
    members, x_cells, y_cells = source_matrix.shape
    half, frac_cells = source_fracture.shape
    slots = send_slots.shape[1]
    rows = isect_local.size
    margin = ov_cell.size
    count = lax.axis_size("gx")

    def near(to_a, to_b):
        return (
            lax.ppermute(to_a, "gx", pairs_of(count, 1, 0)),
            lax.ppermute(to_b, "gx", pairs_of(count, 1, 1)),
        )

    def far(value):
        return (
            lax.ppermute(value, "gx", pairs_of(count, 2, 0)),
            lax.ppermute(value, "gx", pairs_of(count, 2, 1)),
        )

    def core(value):
        return lax.ppermute(value, "gy", [(0, 1), (1, 0)])

    blocks = y_cells // LANES
    frac_blocks = frac_cells // LANES
    field = (members, x_cells, y_cells)
    own = (half, frac_cells)
    hidden = pl.CostEstimate(flops=4_000_000_000, bytes_accessed=12_000_000, transcendentals=0)
    perm, cond, oslot, to_a, to_b, sent, border = call(
        opening_kernel,
        "opening",
        (class_perm, perm_class, aperture, send_slots),
        [
            ((x_cells, y_cells), F32),
            (own, F32),
            ((frac_cells, slots), BF16),
            ((half + 8 * (-(-blocks // 8)), LANES), F32),
            ((half + 8 * (-(-blocks // 8)), LANES), F32),
            ((half, slots), F32),
            ((x_cells, LANES), F32),
        ],
        scratch=[
            pltpu.SMEM(class_perm.shape, F32),
            pltpu.VMEM(perm_class.shape, jnp.int32),
            pltpu.VMEM(aperture.shape, F32),
            pltpu.VMEM(send_slots.shape, jnp.int32),
            pltpu.SemaphoreType.DMA((4,)),
        ],
        far_in=4,
    )

    def exchange(to_a, to_b, sent, to_core):
        near_a, near_b = near(to_a, to_b)
        core_in = core(to_core)
        sent, core_in = lax.optimization_barrier((sent, core_in))
        far_c, far_d = far(sent)
        return near_a, near_b, far_c, far_d, core_in

    near_a, near_b, far_c, far_d, border = exchange(to_a, to_b, sent, border)
    source_f, storage_in, live, edges, coef, oy, ox, weight, *network, v0, margin_in, column = call(
        inside_kernel,
        "inside",
        (
            ov_count.reshape(-1),
            isect_count,
            storage,
            source_matrix,
            source_fracture,
            ov_cell.reshape(-1, LANES),
            ov_weight.reshape(-1, LANES),
            isect_local,
            isect_other,
            ov_frac.reshape(-1, LANES),
            perm,
            border,
            oslot,
            cond,
        ),
        [
            (own, F32),
            ((x_cells, y_cells), F32),
            ((1, rows), F32),
            ((2, members, y_cells), F32),
            ((5, x_cells, y_cells), F32),
            ((y_cells, margin), BF16),
            ((x_cells, margin), F32),
            ((1, margin), F32),
            ((frac_cells, rows), BF16),
            ((half, rows), F32),
            ((half, rows), F32),
            ((8, frac_cells), F32),
            ((frac_cells, rows + slots), BF16),
            ((slots, rows), BF16),
            ((frac_cells, margin), BF16),
            (field, F32),
            ((members, margin), F32),
            ((x_cells, LANES), F32),
        ],
        scratch=[
            pltpu.SMEM((ov_count.size,), jnp.int32),
            pltpu.SMEM(isect_count.shape, jnp.int32),
            pltpu.VMEM(field, F32),
            pltpu.VMEM((margin // LANES, LANES), jnp.int32),
            pltpu.VMEM((margin // LANES, LANES), F32),
            pltpu.VMEM(isect_local.shape, jnp.int32),
            pltpu.VMEM(isect_other.shape, jnp.int32),
            pltpu.VMEM((margin // LANES, LANES), jnp.int32),
            pltpu.SemaphoreType.DMA((10,)),
        ],
        far_in=10,
        cost=hidden,
    )
    first, cond_first, cond_second, wsum, table, ghost_table, ofrac = network
    core_rows = 2 * frac_blocks * half + x_cells
    edge_rows = blocks * members
    unit, f0, sr, scale_f, diff, wown, to_a, to_b, sent, core_msg, v0 = call(
        first_kernel,
        "first_vector",
        (
            live,
            coef,
            perm,
            edges,
            source_f,
            weight,
            near_a,
            near_b,
            far_c,
            far_d,
            *network,
            oy,
            ox,
            margin_in,
            column,
            v0,
        ),
        [
            ((6, x_cells, y_cells), F32),
            (own, F32),
            ((half, rows), F32),
            ((2, half, frac_cells), F32),
            ((half, rows), F32),
            (own, F32),
            ((edge_rows + 3 * half, LANES), F32),
            ((edge_rows + 3 * half, LANES), F32),
            ((3 * half, LANES), F32),
            ((core_rows + 8 * frac_blocks, LANES), F32),
            (field, F32),
        ],
        scratch=[pltpu.VMEM((members, frac_cells), F32)],
        aliases={21: 10},
    )
    near_rows = edge_rows + 2 * half

    def interior(power, v, before, vf, before_f, core_in):
        outs = [(field, F32), ((members, margin), F32), ((x_cells, LANES), F32)]
        return call(
            functools.partial(interior_kernel, power),
            f"interior_{power}",
            (v, before, vf, before_f, core_in, scale_f, unit, weight, ofrac, oy, ox),
            outs + [((8, members), F32)],
            scratch=[pltpu.VMEM((members, margin), F32), pltpu.VMEM((members, frac_cells), F32)]
            + [pltpu.VMEM((members, LANES), F32)] * power,
            cost=hidden,
        )

    finish_outs = [
        (own, F32),
        ((half, rows), F32),
        (own, F32),
        ((near_rows, LANES), F32),
        ((near_rows, LANES), F32),
        ((2 * half, LANES), F32),
        ((core_rows, LANES), F32),
        (field, F32),
    ]
    finish_scratch = [pltpu.VMEM((members, frac_cells), F32)]

    near_a, near_b, far_c, far_d, core_in = exchange(to_a, to_b, sent, core_msg)
    image, margin_in, column, dots1 = interior(1, v0, v0, f0, f0, core_in)
    own_f, f1, diff, wown, to_a, to_b, sent, core_msg, v1 = call(
        functools.partial(finish_kernel, 1),
        "finish_1",
        (f0, near_a, near_b, far_c, far_d, core_in, diff, wown, sr, scale_f, unit, table, ghost_table)
        + (wsum, weight, ofrac, oy, ox, margin_in, column, image),
        [(own, F32)] + finish_outs,
        scratch=finish_scratch,
        aliases={20: 8},
    )
    near_a, near_b, far_c, far_d, core_in = exchange(to_a, to_b, sent, core_msg)
    image, margin_in, column, dots2 = interior(2, v1, v0, f1, f0, core_in)
    f2, diff, margin_in, to_a, to_b, sent, core_msg, v2 = call(
        functools.partial(finish_kernel, 2),
        "finish_2",
        (f1, near_a, near_b, far_c, far_d, core_in, diff, wown, sr, scale_f, unit, table, ghost_table)
        + (own_f, weight, ofrac, oy, ox, margin_in, column, image),
        [
            (own, F32),
            ((half, rows), F32),
            ((members, margin), F32),
            ((edge_rows // 2 + half, LANES), F32),
            ((edge_rows // 2 + half, LANES), F32),
            ((half, LANES), F32),
            ((frac_blocks * half + x_cells, LANES), F32),
            (field, F32),
        ],
        aliases={20: 7},
    )
    near_a, near_b, far_c, far_d, core_in = exchange(to_a, to_b, sent, core_msg)
    (dots3,) = call(
        energy_kernel,
        "energy",
        (v2, v1, f2, f1, core_in, scale_f, unit, coef, storage_in, weight, ofrac, margin_in),
        [((8, members), F32)],
        scratch=[pltpu.VMEM((members, frac_cells), F32)] + [pltpu.VMEM((members, LANES), F32)] * 3,
        cost=hidden,
    )
    peers = count * lax.axis_size("gy")
    (moments,) = call(
        moments_kernel,
        "moments",
        (f2, near_a, near_b, far_c, far_d, diff, sr, unit, ghost_table, v2, dots1, dots2, dots3),
        [((peers, 2, LANES), F32)],
        scratch=[pltpu.VMEM((members, LANES), F32)],
    )
    totals = lax.all_to_all(moments, ("gx", "gy"), 0, 0)
    return call(
        close_kernel,
        "iterate",
        (totals, v0, v1, v2, f0, f1, f2),
        [(field, F32), (own, F32)],
        scratch=[
            pltpu.VMEM((3, LANES, LANES), F32),
            pltpu.VMEM(field, F32),
            pltpu.VMEM(own, F32),
            pltpu.SemaphoreType.DMA((9,)),
        ],
        far_out=True,
    )


def solution(mesh):
    placed = (
        P("grp", "gx", "gy"),
        P(("grp", "gy"), "gx"),
        P(("grp", "gy"), "gx"),
        P("gx", "gy"),
        P("gx", "gy"),
        P(),
        P("gx", None),
        P("gx", None),
        P("gx", None),
        P("gx"),
        P("gx", "gy", None, None),
        P("gx", "gy", None, None),
        P("gx", "gy", None, None),
        P("gx", "gy", None),
    )
    return jax.shard_map(
        per_device,
        mesh=mesh,
        in_specs=placed,
        out_specs=(P("grp", "gx", "gy"), P(("grp", "gy"), "gx")),
        check_vma=False,
    )
```

```python
import functools

import jax
import jax.numpy as jnp
from jax import lax
from jax.experimental import pallas as pl
from jax.experimental.pallas import tpu as pltpu
from jax.sharding import PartitionSpec as P

FRACTURE_STORAGE = 0.1
F32 = jnp.float32
BF16 = jnp.bfloat16
LANES = 128
GROUP = 16


def split3(x):
    high = x.astype(BF16)
    rest = x - high.astype(F32)
    mid = rest.astype(BF16)
    low = (rest - mid.astype(F32)).astype(BF16)
    return jnp.concatenate([high, mid, low], axis=0)


def pick(x, table, transposed=False):
    rows = x.shape[0]
    dims = (((1,), (1 if transposed else 0,)), ((), ()))
    out = lax.dot_general(split3(x), table, dims, preferred_element_type=F32)
    return out[:rows] + out[rows : 2 * rows] + out[2 * rows :]


def fetch(sources, targets, sems):
    copies = [pltpu.make_async_copy(a, b, sems.at[k]) for k, (a, b) in enumerate(zip(sources, targets))]
    for copy in copies:
        copy.start()
    return copies


class Place:
    def __init__(self):
        count = lax.axis_size("gx")
        i = lax.axis_index("gx")
        self.j = lax.axis_index("gy")
        self.high_side = self.j == 0
        self.even = lax.rem(i, 2) == 0
        self.low_pair = lax.rem(lax.div(i, 2), 2) == 0
        self.first = i == 0
        self.last = i == count - 1


def harmonic(first_perm, second_perm):
    return 2.0 * first_perm * second_perm / (first_perm + second_perm)


def one_hot(index_row, size):
    shape = (size, index_row.shape[1])
    ids = lax.broadcasted_iota(jnp.int32, shape, 0)
    return jnp.where(ids == index_row, 1.0, 0.0).astype(BF16)


def to_blocks(x):
    return jnp.concatenate(
        [x[:, q : q + LANES] for q in range(0, x.shape[1], LANES)], axis=0
    )


def from_blocks(x, rows):
    return jnp.concatenate(
        [x[q : q + rows] for q in range(0, x.shape[0], rows)], axis=1
    )


def by_group(first, second, third, fourth):
    group = first.shape[1] // 4
    lane = lax.broadcasted_iota(jnp.int32, first.shape, 1)
    return jnp.where(
        lane < group,
        first,
        jnp.where(lane < 2 * group, second, jnp.where(lane < 3 * group, third, fourth)),
    )


def total_rows(x):
    return jnp.sum(jnp.transpose(x), axis=0, keepdims=True)


def fold_lanes(x):
    rows, width = x.shape
    out = x[:, :LANES]
    for q in range(LANES, width, LANES):
        out = out + x[:, q : q + LANES]
    return out


def opening_kernel(
    perm_table_hbm,
    class_hbm,
    aperture_hbm,
    slots_hbm,
    perm_ref,
    cond_ref,
    oslot_ref,
    near_a_ref,
    near_b_ref,
    far_ref,
    border_ref,
    perm_table_ref,
    class_ref,
    aperture_ref,
    slots_ref,
    sems,
):
    copies = fetch(
        (class_hbm, perm_table_hbm, aperture_hbm, slots_hbm),
        (class_ref, perm_table_ref, aperture_ref, slots_ref),
        sems,
    )
    for copy in copies:
        copy.wait()
    x_cells, y_cells = class_ref.shape
    half = aperture_ref.shape[0]
    here = Place()
    classes = class_ref[...]
    perm = jnp.zeros(classes.shape, F32)
    for index in range(perm_table_ref.shape[0]):
        perm = jnp.where(classes == index, perm_table_ref[index], perm)
    perm_ref[...] = perm
    border_ref[...] = jnp.where(here.high_side, perm[:, y_cells - LANES :], perm[:, :LANES])

    aperture = aperture_ref[...]
    cond = aperture * aperture * aperture
    cond_ref[...] = cond
    oslot = one_hot(slots_ref[...], cond.shape[1])
    oslot_ref[...] = oslot
    supplied = pick(cond, oslot)
    far_ref[...] = supplied
    up, down = to_blocks(perm[x_cells - 1 :]), to_blocks(perm[:1])
    blocks = up.shape[0]
    pad = jnp.zeros((near_a_ref.shape[0] - half - blocks, LANES), F32)
    for ref, edge in ((near_a_ref, jnp.where(here.even, up, down)), (near_b_ref, jnp.where(here.even, down, up))):
        ref[...] = jnp.concatenate([supplied, edge, pad], axis=0)


def neighbours(here, near_a_ref, near_b_ref, far_c_ref, far_d_ref):
    def reader(flag, at_zero, at_one):
        return lambda at, size: jnp.where(
            flag, at_zero[at : at + size, :], at_one[at : at + size, :]
        )

    return (
        reader(here.even, near_a_ref, near_b_ref),
        reader(here.even, near_b_ref, near_a_ref),
        reader(here.low_pair, far_c_ref, far_d_ref),
        reader(here.low_pair, far_d_ref, far_c_ref),
    )


def margin_values(found, ox):
    found = found.reshape(-1, *ox.shape) * ox[None]
    return jnp.sum(found, axis=1)


def border_column(tile_low, tile_high, high_side, m):
    tile = jnp.where(high_side, tile_high, tile_low)
    return pltpu.roll(tile, jnp.where(high_side, lax.rem(m + 1, LANES), m), 1)


def border_row(row_values, high_side):
    members, y_cells = row_values.shape
    tile = jnp.where(high_side, row_values[:, y_cells - LANES :], row_values[:, :LANES])
    turned = jnp.transpose(tile)
    line = jnp.where(high_side, turned[LANES - 1 :], turned[:1])
    return jnp.concatenate([line, jnp.zeros((1, LANES - members), F32)], axis=1)


def finish_edges(high_rows, low_rows, partial_ref, column, high_side, oy, ox):
    members = high_rows.shape[0]
    x_cells = ox.shape[0]
    found = pick(jnp.concatenate([high_rows, low_rows], axis=0), oy)
    margin = partial_ref[...] + found[:members] * ox[x_cells - 1 :] + found[members:] * ox[:1]
    row = lax.broadcasted_iota(jnp.int32, column.shape, 0)
    column = jnp.where(row == x_cells - 1, border_row(high_rows, high_side), column)
    return margin, jnp.where(row == 0, border_row(low_rows, high_side), column)


def send_network(vf, sr, table, ghost_table, diff_ref, refs):
    half = vf.shape[0]
    rows = diff_ref.shape[1]
    found = pick(vf, table)
    diff_ref[...] = found[:, :rows]
    if sr is None:
        for ref, at in refs:
            ref[at : at + half, :] = found[:, rows:]
        return
    sums = pick(sr * found[:, :rows], ghost_table, True)
    for ref, at in refs:
        ref[at : at + half, :] = found[:, rows:]
        ref[at + half : at + 2 * half, :] = sums


def send_core(core_ref, vf, margin, weight, ofrac, column, j, work_ref, wown_ref):
    half, frac_cells = vf.shape
    work_ref[...] = pick(margin * weight, ofrac, True)
    wown_ref[...] = work_ref[pl.ds(pl.multiple_of(j * half, half), half), :]
    other = work_ref[pl.ds(pl.multiple_of((1 - j) * half, half), half), :]
    size = frac_cells // LANES * half
    core_ref[0:size, :] = to_blocks(vf)
    core_ref[size : 2 * size, :] = to_blocks(other)
    core_ref[2 * size : 2 * size + column.shape[0], :] = column


def inside_kernel(
    ov_count_hbm,
    isect_count_hbm,
    storage_hbm,
    source_hbm,
    source_f_hbm,
    cell_hbm,
    ov_weight_hbm,
    local_hbm,
    other_hbm,
    frac_hbm,
    perm_ref,
    border_ref,
    oslot_ref,
    cond_ref,
    source_f_ref,
    storage_ref,
    live_ref,
    edge_ref,
    coef_ref,
    oy_ref,
    ox_ref,
    weight_ref,
    first_ref,
    cond_first_ref,
    cond_second_ref,
    wsum_ref,
    table_ref,
    ghost_table_ref,
    ofrac_ref,
    v_ref,
    margin_ref,
    column_ref,
    ov_count_ref,
    isect_count_ref,
    source_ref,
    cell_ref,
    ov_weight_ref,
    local_ref,
    other_in_ref,
    frac_ref,
    sems,
):
    members, x_cells, y_cells = source_ref.shape
    frac_cells = table_ref.shape[0]
    here = Place()
    high_side = here.high_side
    copies = fetch(
        (
            cell_hbm,
            local_hbm,
            other_hbm,
            frac_hbm,
            ov_weight_hbm,
            ov_count_hbm,
            isect_count_hbm,
            storage_hbm,
            source_f_hbm,
            source_hbm,
        ),
        (
            cell_ref,
            local_ref,
            other_in_ref,
            frac_ref,
            ov_weight_ref,
            ov_count_ref,
            isect_count_ref,
            storage_ref,
            source_f_ref,
            source_ref,
        ),
        sems,
    )

    def line(ref):
        return jnp.concatenate([ref[k : k + 1, :] for k in range(ref.shape[0])], axis=1)

    rows = local_ref.size
    perm, border = perm_ref[...], border_ref[...]
    col = jnp.where(high_side, border[:, :1], border[:, LANES - 1 :])
    lane = lax.broadcasted_iota(jnp.int32, perm.shape, 1)
    row = lax.broadcasted_iota(jnp.int32, perm.shape, 0)
    north = jnp.concatenate([perm[:, 1:], col], axis=1)
    south = jnp.concatenate([col, perm[:, :-1]], axis=1)
    tn = jnp.where((lane == y_cells - 1) & jnp.logical_not(high_side), 0.0, harmonic(perm, north))
    ts = jnp.where((lane == 0) & high_side, 0.0, harmonic(perm, south))
    east = jnp.concatenate([perm[1:], perm[:1]], axis=0)
    west = jnp.concatenate([perm[-1:], perm[:-1]], axis=0)
    te = jnp.where(row == x_cells - 1, 0.0, harmonic(perm, east))
    tw = jnp.where(row == 0, 0.0, harmonic(perm, west))
    for copy in copies[:-1]:
        copy.wait()
    cell = line(cell_ref)
    oy = one_hot(cell % y_cells, y_cells)
    oy_ref[...] = oy
    row_x = lax.broadcasted_iota(jnp.int32, ox_ref.shape, 0)
    at_x = row_x == cell // y_cells
    ox = jnp.where(at_x, 1.0, 0.0)
    ox_ref[...] = ox
    lane_w = lax.broadcasted_iota(jnp.int32, (1, LANES), 1)
    weight = jnp.concatenate(
        [jnp.where(lane_w < ov_count_ref[k], ov_weight_ref[k : k + 1, :], 0.0) for k in range(ov_weight_ref.shape[0])],
        axis=1,
    )
    weight_ref[...] = weight
    for block in range(local_ref.shape[0]):
        at = slice(block * LANES, (block + 1) * LANES)
        live_ref[:, at] = jnp.where(lane_w < isect_count_ref[block], 1.0, 0.0)
    part = storage_ref[...] + te + tw + tn + ts + pick(jnp.where(at_x, weight, 0.0), oy, True)
    coef_ref[0] = te
    coef_ref[1] = tw
    coef_ref[2] = tn
    coef_ref[3] = ts
    coef_ref[4] = part

    other = line(other_in_ref)
    first, second = one_hot(line(local_ref), frac_cells), one_hot(other, frac_cells)
    first_ref[...] = first
    cond = cond_ref[...]
    cond_first_ref[...] = pick(cond, first)
    cond_second_ref[...] = pick(cond, second)
    table_ref[:, :rows] = first - second
    table_ref[:, rows:] = oslot_ref[...]
    ghost_table_ref[...] = one_hot(other - frac_cells, ghost_table_ref.shape[0])
    ofrac = one_hot(line(frac_ref), frac_cells)
    ofrac_ref[...] = ofrac
    wsum_ref[...] = pick(jnp.broadcast_to(weight, (8, weight.shape[1])), ofrac, True)

    inverse = 1.0 / part
    inner_x = jnp.where((row_x == 0) | (row_x == x_cells - 1), 0.0, ox)
    lane_c = lax.broadcasted_iota(jnp.int32, (x_cells, LANES), 1)
    column_ref[...] = jnp.zeros_like(column_ref)
    copies[-1].wait()
    edge_ref[0] = source_ref[:, x_cells - 1, :]
    edge_ref[1] = source_ref[:, 0, :]

    @pl.loop(0, members // GROUP)
    def _(index):
        start = index * GROUP
        block = source_ref[pl.ds(start, GROUP)] * inverse[None]
        v_ref[pl.ds(start, GROUP)] = block
        found = pick(block.reshape(GROUP * x_cells, y_cells), oy_ref[...])
        margin_ref[pl.ds(start, GROUP), :] = margin_values(found, inner_x)
        column = column_ref[...]
        for k in range(GROUP):
            m = start + k
            moved = border_column(block[k, :, :LANES], block[k, :, y_cells - LANES :], high_side, m)
            column = jnp.where(lane_c == m, moved, column)
        column_ref[...] = column


def first_kernel(
    live_ref,
    coef_ref,
    perm_ref,
    edge_ref,
    source_f_ref,
    weight_ref,
    near_a_ref,
    near_b_ref,
    far_c_ref,
    far_d_ref,
    first_ref,
    cond_first_ref,
    cond_second_ref,
    wsum_ref,
    table_ref,
    ghost_table_ref,
    ofrac_ref,
    oy_ref,
    ox_ref,
    inner_margin_ref,
    inner_column_ref,
    v_in_ref,
    unit_ref,
    vf_ref,
    sr_ref,
    scale_f_ref,
    diff_ref,
    wown_ref,
    to_a_ref,
    to_b_ref,
    sent_ref,
    core_ref,
    v_ref,
    work_ref,
):
    members, x_cells, y_cells = v_ref.shape
    half, frac_cells = source_f_ref.shape
    blocks = y_cells // LANES
    here = Place()
    j, high_side = here.j, here.high_side
    base = blocks * members
    plus1, minus1, plus2, minus2 = neighbours(here, near_a_ref, near_b_ref, far_c_ref, far_d_ref)

    ghosts = by_group(minus1(0, half), plus1(0, half), minus2(0, half), plus2(0, half))
    table, ghost_table = table_ref[...], ghost_table_ref[...]
    cond_first = cond_first_ref[...]
    cond_second = cond_second_ref[...] + pick(ghosts, ghost_table)
    sr = jnp.where(live_ref[...] > 0.0, harmonic(cond_first, cond_second), 0.0)
    sr_ref[...] = sr
    diag_f = FRACTURE_STORAGE + pick(sr, first_ref[...], True)
    inverse_f = 1.0 / diag_f
    scale_f_ref[0] = inverse_f
    scale_f_ref[1] = diag_f
    vf = source_f_ref[...] * inverse_f
    vf_ref[...] = vf
    refs = [(to_a_ref, base), (to_b_ref, base), (sent_ref, 0)]
    send_network(vf, sr, table, ghost_table, diff_ref, refs)
    slot_sums = pick(sr, ghost_table, True)
    for ref, at in refs:
        ref[at + 2 * half : at + 3 * half, :] = slot_sums

    perm, part = perm_ref[...], coef_ref[4]
    row = lax.broadcasted_iota(jnp.int32, perm.shape, 0)
    perm_plus = from_blocks(plus1(half, blocks), 1)
    perm_minus = from_blocks(minus1(half, blocks), 1)
    te_edge = jnp.where(here.last, 0.0, harmonic(perm[x_cells - 1 :], perm_plus))
    tw_edge = jnp.where(here.first, 0.0, harmonic(perm[:1], perm_minus))
    te = jnp.where(row == x_cells - 1, te_edge, coef_ref[0])
    tw = jnp.where(row == 0, tw_edge, coef_ref[1])
    diag = part + jnp.where(row == x_cells - 1, te_edge, 0.0) + jnp.where(row == 0, tw_edge, 0.0)
    inverse = 1.0 / diag
    unit_ref[0] = te * inverse
    unit_ref[1] = tw * inverse
    unit_ref[2] = coef_ref[2] * inverse
    unit_ref[3] = coef_ref[3] * inverse
    unit_ref[4] = inverse
    unit_ref[5] = diag
    high_rows = edge_ref[0] * inverse[x_cells - 1 :]
    low_rows = edge_ref[1] * inverse[:1]
    v_ref[:, x_cells - 1, :] = high_rows
    v_ref[:, 0, :] = low_rows
    to_a_ref[0:base, :] = to_blocks(jnp.where(here.even, high_rows, low_rows))
    to_b_ref[0:base, :] = to_blocks(jnp.where(here.even, low_rows, high_rows))
    margin, column = finish_edges(
        high_rows, low_rows, inner_margin_ref, inner_column_ref[...], high_side, oy_ref[...], ox_ref[...]
    )
    weight = weight_ref[...]
    send_core(core_ref, vf, margin, weight, ofrac_ref[...], column, j, work_ref, wown_ref)
    tail = core_ref.shape[0] - 8 * (frac_cells // LANES)
    core_ref[tail:, :] = to_blocks(wsum_ref[...])


def interior_kernel(
    power,
    v_ref,
    before_ref,
    vf_ref,
    before_f_ref,
    core_ref,
    scale_f_ref,
    unit_ref,
    weight_ref,
    ofrac_ref,
    oy_ref,
    ox_ref,
    *refs,
):
    image_ref, margin_ref, column_ref, dots_ref, flow_ref, work_ref, *acc_refs = refs
    members, x_cells, y_cells = v_ref.shape
    half, frac_cells = vf_ref.shape
    blocks = y_cells // LANES
    here = Place()
    j, high_side = here.j, here.high_side
    size = frac_cells // LANES * half
    theirs = from_blocks(core_ref[0:size, :], half)
    column_in = core_ref[2 * size : 2 * size + x_cells, :]
    vf = vf_ref[...]
    own_rows = pl.ds(pl.multiple_of(j * half, half), half)
    work_ref[own_rows, :] = vf
    work_ref[pl.ds(pl.multiple_of((1 - j) * half, half), half), :] = theirs
    flow_ref[...] = pick(work_ref[...], ofrac_ref[...]) * weight_ref[...]

    heavy_f = vf * scale_f_ref[1]
    for ref in acc_refs:
        ref[...] = jnp.zeros_like(ref)
    acc_refs[0][own_rows, :] = fold_lanes(vf * heavy_f)
    if power > 1:
        acc_refs[1][own_rows, :] = fold_lanes(before_f_ref[...] * heavy_f)

    lane_c = lax.broadcasted_iota(jnp.int32, (x_cells, LANES), 1)
    lane = lax.broadcasted_iota(jnp.int32, (x_cells, y_cells), 1)
    row = lax.broadcasted_iota(jnp.int32, (x_cells, y_cells), 0)
    row_x = lax.broadcasted_iota(jnp.int32, ox_ref.shape, 0)
    oy, ox = oy_ref[...], ox_ref[...]
    inner_x = jnp.where((row_x == 0) | (row_x == x_cells - 1), 0.0, ox)
    te = jnp.where(row == x_cells - 1, 0.0, unit_ref[0])
    tw = jnp.where(row == 0, 0.0, unit_ref[1])
    column_ref[...] = jnp.zeros_like(column_ref)

    @pl.loop(0, members // GROUP)
    def _(index):
        start = index * GROUP
        parts = []
        for k in range(GROUP):
            parts.append(ox * flow_ref[pl.ds(start + k, 1), :])
        coupled = pick(jnp.concatenate(parts, axis=0), oy, True)
        column = column_ref[...]
        for k in range(GROUP):
            m = start + k
            value = v_ref[m]
            east = pltpu.roll(value, x_cells - 1, 0)
            west = pltpu.roll(value, 1, 0)
            moved = pltpu.roll(column_in, jnp.where(high_side, LANES - 1 - m, lax.rem(LANES - m, LANES)), 1)
            moved = jnp.concatenate([moved] * blocks, axis=1)
            north = jnp.where(lane == y_cells - 1, moved, pltpu.roll(value, y_cells - 1, 1))
            south = jnp.where(lane == 0, moved, pltpu.roll(value, 1, 1))
            image = value - te * east - tw * west - unit_ref[2] * north - unit_ref[3] * south
            image = image - coupled[k * x_cells : (k + 1) * x_cells] * unit_ref[4]
            heavy = value * unit_ref[5]
            at = pl.ds(m, 1)
            acc_refs[0][at, :] += jnp.sum(fold_lanes(value * heavy), axis=0, keepdims=True)
            if power > 1:
                acc_refs[1][at, :] += jnp.sum(fold_lanes(before_ref[m] * heavy), axis=0, keepdims=True)
            image_ref[m] = image
            shifted = border_column(image[:, :LANES], image[:, y_cells - LANES :], high_side, m)
            column = jnp.where(lane_c == m, shifted, column)
        column_ref[...] = column
        block = image_ref[pl.ds(start, GROUP)]
        found = pick(block.reshape(GROUP * x_cells, y_cells), oy)
        margin_ref[pl.ds(start, GROUP), :] = margin_values(found, inner_x)

    dots = [total_rows(ref[...]) for ref in acc_refs]
    dots.append(jnp.zeros((8 - len(dots), members), F32))
    dots_ref[...] = jnp.concatenate(dots, axis=0)


def finish_kernel(
    power,
    vf_ref,
    near_a_ref,
    near_b_ref,
    far_c_ref,
    far_d_ref,
    core_in_ref,
    diff_in_ref,
    wown_in_ref,
    sr_ref,
    scale_f_ref,
    unit_ref,
    table_ref,
    ghost_table_ref,
    *refs,
):
    own_f_in_ref, *refs = refs
    weight_ref, ofrac_ref, oy_ref, ox_ref, inner_margin_ref, inner_column_ref, image_in_ref, *refs = refs
    if power == 1:
        own_f_ref, out_f_ref, diff_ref, wown_ref, to_a_ref, to_b_ref, sent_ref, core_ref, image_ref, work_ref = refs
    else:
        out_f_ref, diff_ref, margin_ref, to_a_ref, to_b_ref, sent_ref, core_ref, image_ref = refs
    half, frac_cells = vf_ref.shape
    x_cells, y_cells = unit_ref.shape[1:]
    members = image_ref.shape[0]
    blocks = y_cells // LANES
    frac_blocks = frac_cells // LANES
    here = Place()
    j, high_side = here.j, here.high_side
    base = blocks * members
    plus1, minus1, plus2, minus2 = neighbours(here, near_a_ref, near_b_ref, far_c_ref, far_d_ref)
    rows = sr_ref.shape[1]

    table, ghost_table = table_ref[...], ghost_table_ref[...]
    vf = vf_ref[...]
    ghosts = by_group(minus1(base, half), plus1(base, half), minus2(0, half), plus2(0, half))
    sums = by_group(
        plus1(base + half, half), minus1(base + half, half), plus2(half, half), minus2(half, half)
    )
    size = frac_blocks * half
    their_sums = from_blocks(core_in_ref[size : 2 * size, :], half)
    if power == 1:
        at = 2 * half
        back = by_group(
            plus1(base + at, half), minus1(base + at, half), plus2(at, half), minus2(at, half)
        )
        tail = core_in_ref.shape[0] - 8 * frac_blocks
        wsum = own_f_in_ref[...] + from_blocks(core_in_ref[tail:, :], 8)
        own_f = FRACTURE_STORAGE + wsum[:1] + pick(back, table[:, rows:], True)
        own_f_ref[...] = own_f
    else:
        own_f = own_f_in_ref[...]
    sr = sr_ref[...]
    flux = sr * (diff_in_ref[...] - pick(ghosts, ghost_table))
    image_f = own_f * vf + pick(jnp.concatenate([flux, -sums], axis=1), table, True)
    image_f = image_f - wown_in_ref[...] - their_sums

    next_f = image_f * scale_f_ref[0]
    out_f_ref[...] = next_f
    edge_size = base if power == 1 else base // 2
    refs = [(to_a_ref, edge_size), (to_b_ref, edge_size), (sent_ref, 0)]
    send_network(next_f, sr if power == 1 else None, table, ghost_table, diff_ref, refs)

    edges = []
    for side, at, reader in ((0, x_cells - 1, plus1), (1, 0, minus1)):
        beyond = from_blocks(reader(0, base), members)
        edge = image_in_ref[:, at, :] - unit_ref[side, at : at + 1, :] * beyond
        image_ref[:, at, :] = edge
        edges.append(edge)
    up, down = edges
    if power == 2:
        up, down = up[:, : y_cells // 2], down[:, y_cells // 2 :]
    to_a_ref[0:edge_size, :] = to_blocks(jnp.where(here.even, up, down))
    to_b_ref[0:edge_size, :] = to_blocks(jnp.where(here.even, down, up))
    margin, column = finish_edges(
        edges[0], edges[1], inner_margin_ref, inner_column_ref[...], high_side, oy_ref[...], ox_ref[...]
    )
    if power == 1:
        send_core(core_ref, next_f, margin, weight_ref[...], ofrac_ref[...], column, j, work_ref, wown_ref)
    else:
        margin_ref[...] = margin
        core_ref[0:size, :] = to_blocks(next_f)
        core_ref[size : size + x_cells, :] = column


def energy_kernel(
    v_ref,
    before_ref,
    vf_ref,
    before_f_ref,
    core_ref,
    scale_f_ref,
    unit_ref,
    coef_ref,
    storage_ref,
    weight_ref,
    ofrac_ref,
    margin_ref,
    dots_ref,
    work_ref,
    acc0_ref,
    acc1_ref,
    acc2_ref,
):
    members, x_cells, y_cells = v_ref.shape
    half, frac_cells = vf_ref.shape
    blocks = y_cells // LANES
    here = Place()
    size = frac_cells // LANES * half
    theirs = from_blocks(core_ref[0:size, :], half)
    column_in = core_ref[size : size + x_cells, :]
    vf = vf_ref[...]
    own_rows = pl.ds(pl.multiple_of(here.j * half, half), half)
    work_ref[own_rows, :] = vf
    work_ref[pl.ds(pl.multiple_of((1 - here.j) * half, half), half), :] = theirs
    gap = margin_ref[...] - pick(work_ref[...], ofrac_ref[...])
    acc2_ref[...] = fold_lanes(weight_ref[...] * gap * gap)
    heavy_f = vf * scale_f_ref[1]
    acc0_ref[...] = jnp.zeros_like(acc0_ref)
    acc1_ref[...] = jnp.zeros_like(acc1_ref)
    acc0_ref[own_rows, :] = fold_lanes(vf * heavy_f)
    acc1_ref[own_rows, :] = fold_lanes(before_f_ref[...] * heavy_f)
    lane = lax.broadcasted_iota(jnp.int32, (x_cells, y_cells), 1)
    diag, te, tn, storage = unit_ref[5], coef_ref[0], coef_ref[2], storage_ref[...]

    @pl.loop(0, members // GROUP)
    def _(index):
        start = index * GROUP
        for k in range(GROUP):
            m = start + k
            value = v_ref[m]
            east = value - pltpu.roll(value, x_cells - 1, 0)
            moved = pltpu.roll(column_in, LANES - 1 - m, 1)
            moved = jnp.concatenate([moved] * blocks, axis=1)
            north = value - jnp.where(lane == y_cells - 1, moved, pltpu.roll(value, y_cells - 1, 1))
            energy = storage * value * value + te * east * east + tn * north * north
            heavy = value * diag
            at = pl.ds(m, 1)
            acc0_ref[at, :] += jnp.sum(fold_lanes(value * heavy), axis=0, keepdims=True)
            acc1_ref[at, :] += jnp.sum(fold_lanes(before_ref[m] * heavy), axis=0, keepdims=True)
            acc2_ref[at, :] += jnp.sum(fold_lanes(energy), axis=0, keepdims=True)

    dots = [total_rows(ref[...]) for ref in (acc0_ref, acc1_ref, acc2_ref)]
    dots.append(jnp.zeros((8 - len(dots), members), F32))
    dots_ref[...] = jnp.concatenate(dots, axis=0)


def moments_kernel(
    vf_ref,
    near_a_ref,
    near_b_ref,
    far_c_ref,
    far_d_ref,
    diff_in_ref,
    sr_ref,
    unit_ref,
    ghost_table_ref,
    v_ref,
    dots1_ref,
    dots2_ref,
    dots3_ref,
    moments_ref,
    acc_ref,
):
    half = vf_ref.shape[0]
    members, x_cells, y_cells = v_ref.shape
    middle = y_cells // 2
    base = middle // LANES * members
    here = Place()
    plus1, minus1, plus2, minus2 = neighbours(here, near_a_ref, near_b_ref, far_c_ref, far_d_ref)
    vf = vf_ref[...]
    ghosts = by_group(minus1(base, half), plus1(base, half), minus2(0, half), plus2(0, half))
    gap = diff_in_ref[...] - pick(ghosts, ghost_table_ref[...])
    acc_ref[...] = jnp.zeros_like(acc_ref)
    own_rows = pl.ds(pl.multiple_of(here.j * half, half), half)
    acc_ref[own_rows, :] = fold_lanes(sr_ref[...] * gap * gap) + fold_lanes(FRACTURE_STORAGE * vf * vf)
    for side, at, reader, cut in (
        (0, x_cells - 1, plus1, slice(middle, y_cells)),
        (1, 0, minus1, slice(0, middle)),
    ):
        trans = unit_ref[side, at : at + 1, cut] * unit_ref[5, at : at + 1, cut]
        edge = v_ref[:, at, cut] - from_blocks(reader(0, base), members)
        acc_ref[...] += fold_lanes(trans * edge * edge)
    last = total_rows(acc_ref[...]) + dots3_ref[2:3, :]
    blank = jnp.zeros((1, LANES - 3 * members), F32)
    lines = [
        jnp.concatenate([dots1_ref[0:1, :], dots2_ref[1:2, :], dots2_ref[0:1, :], blank], axis=1),
        jnp.concatenate([dots3_ref[1:2, :], dots3_ref[0:1, :], last, blank], axis=1),
    ]
    lines = jnp.concatenate(lines, axis=0)
    moments_ref[...] = jnp.broadcast_to(lines[None], moments_ref.shape)


def close_kernel(totals_ref, v0_ref, v1_ref, v2_ref, f0_ref, f1_ref, f2_ref, x_hbm, xf_hbm, c_ref, x_ref, xf_ref, sems):
    members, x_cells, y_cells = v0_ref.shape
    half, frac_cells = f0_ref.shape

    total = jnp.sum(totals_ref[...], axis=0)
    m0, m1, m2, m3, m4, m5 = (
        total[k // 3 : k // 3 + 1, k % 3 * members : k % 3 * members + members] for k in range(6)
    )
    alpha0 = m0 / m1
    rz1 = m0 - 2.0 * alpha0 * m1 + alpha0 * alpha0 * m2
    beta1 = rz1 / m0
    a, b = 1.0 + beta1, -alpha0
    pap1 = a * a * m1 + 2.0 * a * b * m2 + b * b * m3
    alpha1 = rz1 / pap1
    e = -alpha0 - alpha1 * a
    g = -alpha1 * b
    rz2 = m0 + 2.0 * e * m1 + (e * e + 2.0 * g) * m2 + 2.0 * e * g * m3 + g * g * m4
    beta2 = rz2 / rz1
    c = 1.0 + beta2 * a
    d = e + beta2 * b
    pap2 = c * c * m1 + 2.0 * c * d * m2 + (d * d + 2.0 * c * g) * m3 + 2.0 * d * g * m4 + g * g * m5
    alpha2 = rz2 / pap2
    c0 = alpha0 + alpha1 * a + alpha2 * c
    c1 = alpha1 * b + alpha2 * d
    c2 = alpha2 * g
    for k, row in enumerate((c0, c1, c2)):
        row = jnp.concatenate([row, jnp.zeros((1, LANES - members), F32)], axis=1)
        c_ref[k] = jnp.transpose(jnp.broadcast_to(row, (LANES, LANES)))
    j = lax.axis_index("gy")
    own = pl.ds(pl.multiple_of(j * half, half), half)

    def wide(k, rows, width):
        return jnp.concatenate([c_ref[k, rows, :]] * (width // LANES), axis=1)

    xf_ref[...] = (
        wide(0, own, frac_cells) * f0_ref[...]
        + wide(1, own, frac_cells) * f1_ref[...]
        + wide(2, own, frac_cells) * f2_ref[...]
    )

    copies = fetch((xf_ref,), (xf_hbm,), sems)
    pieces = sems.shape[0] - 1
    piece = members // pieces
    for index in range(pieces):

        @pl.loop(index * piece, (index + 1) * piece)
        def _(m):
            rows = pl.ds(m, 1)
            x_ref[m] = (
                wide(0, rows, y_cells) * v0_ref[m]
                + wide(1, rows, y_cells) * v1_ref[m]
                + wide(2, rows, y_cells) * v2_ref[m]
            )

        part = pl.ds(index * piece, piece)
        copies.append(pltpu.make_async_copy(x_ref.at[part], x_hbm.at[part], sems.at[1 + index]))
        copies[-1].start()
    for copy in copies:
        copy.wait()


def pairs_of(count, stride, phase):
    out = []
    for index in range(count):
        if (index // stride) % 2 == phase:
            mate = (index + stride) % count
            out += [(index, mate), (mate, index)]
    return out


VMEM = pl.BlockSpec(memory_space=pltpu.VMEM)


HBM = pl.BlockSpec(memory_space=pltpu.HBM)


def call(kernel, name, args, outs, scratch=(), far_in=0, far_out=False, cost=None, aliases=None):
    args = [pltpu.with_memory_space_constraint(arg, pltpu.HBM) for arg in args[:far_in]] + list(args[far_in:])
    return pl.pallas_call(
        kernel,
        name=name,
        out_shape=[jax.ShapeDtypeStruct(shape, dtype) for shape, dtype in outs],
        in_specs=[HBM] * far_in + [VMEM] * (len(args) - far_in),
        out_specs=[HBM if far_out else VMEM] * len(outs),
        scratch_shapes=list(scratch),
        compiler_params=pltpu.CompilerParams(vmem_limit_bytes=40 * 1024 * 1024),
        cost_estimate=cost,
        input_output_aliases=aliases or {},
    )(*args)


def per_device(
    source_matrix,
    source_fracture,
    aperture,
    storage,
    perm_class,
    class_perm,
    send_slots,
    isect_local,
    isect_other,
    isect_count,
    ov_cell,
    ov_frac,
    ov_weight,
    ov_count,
):
    members, x_cells, y_cells = source_matrix.shape
    half, frac_cells = source_fracture.shape
    slots = send_slots.shape[1]
    rows = isect_local.size
    margin = ov_cell.size
    count = lax.axis_size("gx")

    def near(to_a, to_b):
        return (
            lax.ppermute(to_a, "gx", pairs_of(count, 1, 0)),
            lax.ppermute(to_b, "gx", pairs_of(count, 1, 1)),
        )

    def far(value):
        return (
            lax.ppermute(value, "gx", pairs_of(count, 2, 0)),
            lax.ppermute(value, "gx", pairs_of(count, 2, 1)),
        )

    def core(value):
        return lax.ppermute(value, "gy", [(0, 1), (1, 0)])

    blocks = y_cells // LANES
    frac_blocks = frac_cells // LANES
    field = (members, x_cells, y_cells)
    own = (half, frac_cells)
    hidden = pl.CostEstimate(flops=4_000_000_000, bytes_accessed=12_000_000, transcendentals=0)
    perm, cond, oslot, to_a, to_b, sent, border = call(
        opening_kernel,
        "opening",
        (class_perm, perm_class, aperture, send_slots),
        [
            ((x_cells, y_cells), F32),
            (own, F32),
            ((frac_cells, slots), BF16),
            ((half + 8 * (-(-blocks // 8)), LANES), F32),
            ((half + 8 * (-(-blocks // 8)), LANES), F32),
            ((half, slots), F32),
            ((x_cells, LANES), F32),
        ],
        scratch=[
            pltpu.SMEM(class_perm.shape, F32),
            pltpu.VMEM(perm_class.shape, jnp.int32),
            pltpu.VMEM(aperture.shape, F32),
            pltpu.VMEM(send_slots.shape, jnp.int32),
            pltpu.SemaphoreType.DMA((4,)),
        ],
        far_in=4,
    )

    def exchange(to_a, to_b, sent, to_core):
        near_a, near_b = near(to_a, to_b)
        core_in = core(to_core)
        sent, core_in = lax.optimization_barrier((sent, core_in))
        far_c, far_d = far(sent)
        return near_a, near_b, far_c, far_d, core_in

    near_a = lax.ppermute(to_a, "gx", pairs_of(count, 1, 0))
    far_d = lax.ppermute(sent, "gx", pairs_of(count, 2, 1))
    border = core(border)
    sent, to_b, border = lax.optimization_barrier((sent, to_b, border))
    near_b = lax.ppermute(to_b, "gx", pairs_of(count, 1, 1))
    far_c = lax.ppermute(sent, "gx", pairs_of(count, 2, 0))
    source_f, storage_in, live, edges, coef, oy, ox, weight, *network, v0, margin_in, column = call(
        inside_kernel,
        "inside",
        (
            ov_count.reshape(-1),
            isect_count,
            storage,
            source_matrix,
            source_fracture,
            ov_cell.reshape(-1, LANES),
            ov_weight.reshape(-1, LANES),
            isect_local,
            isect_other,
            ov_frac.reshape(-1, LANES),
            perm,
            border,
            oslot,
            cond,
        ),
        [
            (own, F32),
            ((x_cells, y_cells), F32),
            ((1, rows), F32),
            ((2, members, y_cells), F32),
            ((5, x_cells, y_cells), F32),
            ((y_cells, margin), BF16),
            ((x_cells, margin), F32),
            ((1, margin), F32),
            ((frac_cells, rows), BF16),
            ((half, rows), F32),
            ((half, rows), F32),
            ((8, frac_cells), F32),
            ((frac_cells, rows + slots), BF16),
            ((slots, rows), BF16),
            ((frac_cells, margin), BF16),
            (field, F32),
            ((members, margin), F32),
            ((x_cells, LANES), F32),
        ],
        scratch=[
            pltpu.SMEM((ov_count.size,), jnp.int32),
            pltpu.SMEM(isect_count.shape, jnp.int32),
            pltpu.VMEM(field, F32),
            pltpu.VMEM((margin // LANES, LANES), jnp.int32),
            pltpu.VMEM((margin // LANES, LANES), F32),
            pltpu.VMEM(isect_local.shape, jnp.int32),
            pltpu.VMEM(isect_other.shape, jnp.int32),
            pltpu.VMEM((margin // LANES, LANES), jnp.int32),
            pltpu.SemaphoreType.DMA((10,)),
        ],
        far_in=10,
        cost=hidden,
    )
    first, cond_first, cond_second, wsum, table, ghost_table, ofrac = network
    core_rows = 2 * frac_blocks * half + x_cells
    edge_rows = blocks * members
    unit, f0, sr, scale_f, diff, wown, to_a, to_b, sent, core_msg, v0 = call(
        first_kernel,
        "first_vector",
        (
            live,
            coef,
            perm,
            edges,
            source_f,
            weight,
            near_a,
            near_b,
            far_c,
            far_d,
            *network,
            oy,
            ox,
            margin_in,
            column,
            v0,
        ),
        [
            ((6, x_cells, y_cells), F32),
            (own, F32),
            ((half, rows), F32),
            ((2, half, frac_cells), F32),
            ((half, rows), F32),
            (own, F32),
            ((edge_rows + 3 * half, LANES), F32),
            ((edge_rows + 3 * half, LANES), F32),
            ((3 * half, LANES), F32),
            ((core_rows + 8 * frac_blocks, LANES), F32),
            (field, F32),
        ],
        scratch=[pltpu.VMEM((members, frac_cells), F32)],
        aliases={21: 10},
    )
    near_rows = edge_rows + 2 * half

    def interior(power, v, before, vf, before_f, core_in):
        outs = [(field, F32), ((members, margin), F32), ((x_cells, LANES), F32)]
        return call(
            functools.partial(interior_kernel, power),
            f"interior_{power}",
            (v, before, vf, before_f, core_in, scale_f, unit, weight, ofrac, oy, ox),
            outs + [((8, members), F32)],
            scratch=[pltpu.VMEM((members, margin), F32), pltpu.VMEM((members, frac_cells), F32)]
            + [pltpu.VMEM((members, LANES), F32)] * power,
            cost=hidden,
        )

    finish_outs = [
        (own, F32),
        ((half, rows), F32),
        (own, F32),
        ((near_rows, LANES), F32),
        ((near_rows, LANES), F32),
        ((2 * half, LANES), F32),
        ((core_rows, LANES), F32),
        (field, F32),
    ]
    finish_scratch = [pltpu.VMEM((members, frac_cells), F32)]

    near_a, near_b, far_c, far_d, core_in = exchange(to_a, to_b, sent, core_msg)
    image, margin_in, column, dots1 = interior(1, v0, v0, f0, f0, core_in)
    own_f, f1, diff, wown, to_a, to_b, sent, core_msg, v1 = call(
        functools.partial(finish_kernel, 1),
        "finish_1",
        (f0, near_a, near_b, far_c, far_d, core_in, diff, wown, sr, scale_f, unit, table, ghost_table)
        + (wsum, weight, ofrac, oy, ox, margin_in, column, image),
        [(own, F32)] + finish_outs,
        scratch=finish_scratch,
        aliases={20: 8},
    )
    near_a, near_b, far_c, far_d, core_in = exchange(to_a, to_b, sent, core_msg)
    image, margin_in, column, dots2 = interior(2, v1, v0, f1, f0, core_in)
    f2, diff, margin_in, to_a, to_b, sent, core_msg, v2 = call(
        functools.partial(finish_kernel, 2),
        "finish_2",
        (f1, near_a, near_b, far_c, far_d, core_in, diff, wown, sr, scale_f, unit, table, ghost_table)
        + (own_f, weight, ofrac, oy, ox, margin_in, column, image),
        [
            (own, F32),
            ((half, rows), F32),
            ((members, margin), F32),
            ((edge_rows // 2 + half, LANES), F32),
            ((edge_rows // 2 + half, LANES), F32),
            ((half, LANES), F32),
            ((frac_blocks * half + x_cells, LANES), F32),
            (field, F32),
        ],
        aliases={20: 7},
    )
    near_a, near_b, far_c, far_d, core_in = exchange(to_a, to_b, sent, core_msg)
    (dots3,) = call(
        energy_kernel,
        "energy",
        (v2, v1, f2, f1, core_in, scale_f, unit, coef, storage_in, weight, ofrac, margin_in),
        [((8, members), F32)],
        scratch=[pltpu.VMEM((members, frac_cells), F32)] + [pltpu.VMEM((members, LANES), F32)] * 3,
        cost=hidden,
    )
    peers = count * lax.axis_size("gy")
    (moments,) = call(
        moments_kernel,
        "moments",
        (f2, near_a, near_b, far_c, far_d, diff, sr, unit, ghost_table, v2, dots1, dots2, dots3),
        [((peers, 2, LANES), F32)],
        scratch=[pltpu.VMEM((members, LANES), F32)],
    )
    totals = lax.all_to_all(moments, ("gx", "gy"), 0, 0)
    return call(
        close_kernel,
        "iterate",
        (totals, v0, v1, v2, f0, f1, f2),
        [(field, F32), (own, F32)],
        scratch=[
            pltpu.VMEM((3, LANES, LANES), F32),
            pltpu.VMEM(field, F32),
            pltpu.VMEM(own, F32),
            pltpu.SemaphoreType.DMA((5,)),
        ],
        far_out=True,
    )


def solution(mesh):
    placed = (
        P("grp", "gx", "gy"),
        P(("grp", "gy"), "gx"),
        P(("grp", "gy"), "gx"),
        P("gx", "gy"),
        P("gx", "gy"),
        P(),
        P("gx", None),
        P("gx", None),
        P("gx", None),
        P("gx"),
        P("gx", "gy", None, None),
        P("gx", "gy", None, None),
        P("gx", "gy", None, None),
        P("gx", "gy", None),
    )
    return jax.shard_map(
        per_device,
        mesh=mesh,
        in_specs=placed,
        out_specs=(P("grp", "gx", "gy"), P(("grp", "gy"), "gx")),
        check_vma=False,
    )
```
